32 devices in a mesh: seq: 4 (over y, x), row: 8 (over z, core).
Axes of the slice: x: 2, y: 2, z: 4, core: 2. Of those that a mesh axis runs over, the one named last changes fastest.
Arguments:
- tokens: bfloat16 [8, 1024, 2048], P('row', 'seq'), may hold values from -6 to 6
- segment_ids: int32 [8, 1024], P('row', 'seq'), may hold values from 0 to 2, as said below
- w_query: bfloat16 [2048, 2048], P(('seq', 'row')), may hold values from -0.125 to 0.125
- w_key: bfloat16 [2048, 2048], P(('seq', 'row')), may hold values from -0.125 to 0.125
- w_value: bfloat16 [2048, 2048], P(('seq', 'row')), may hold values from -0.125 to 0.125
- w_out: bfloat16 [2048, 2048], P(('seq', 'row')), may hold values from -0.125 to 0.125
- w_gate: bfloat16 [2048, 8192], P(('seq', 'row')), may hold values from -0.125 to 0.125
- w_up: bfloat16 [2048, 8192], P(('seq', 'row')), may hold values from -0.125 to 0.125
- w_down: bfloat16 [8192, 2048], P(('seq', 'row')), may hold values from -0.0625 to 0.0625
- query_gain: bfloat16 [2048], P(('seq', 'row')), may hold values from 0.099609375 to 1.8984375
- key_gain: bfloat16 [2048], P(('seq', 'row')), may hold values from 0.099609375 to 1.8984375
- attn_gain: bfloat16 [2048], P(('seq', 'row')), may hold values from 0.099609375 to 1.8984375
- ff_gain: bfloat16 [2048], P(('seq', 'row')), may hold values from 0.099609375 to 1.8984375
- cotangent: bfloat16 [8, 1024, 2048], P('row', 'seq'), may hold values from -6 to 6
Outputs:
- mixed: bfloat16 [8, 1024, 2048], P('row', 'seq')
- input_grad: float32 [8, 1024, 2048], P('row', 'seq')
- grad_query: float32 [2048, 2048], P(('seq', 'row'))
- grad_key: float32 [2048, 2048], P(('seq', 'row'))
- grad_value: float32 [2048, 2048], P(('seq', 'row'))
- grad_out: float32 [2048, 2048], P(('seq', 'row'))
- grad_gate: float32 [2048, 8192], P(('seq', 'row'))
- grad_up: float32 [2048, 8192], P(('seq', 'row'))
- grad_down: float32 [8192, 2048], P(('seq', 'row'))
- grad_query_gain: float32 [2048], P(('seq', 'row'))
- grad_key_gain: float32 [2048], P(('seq', 'row'))
- grad_attn_gain: float32 [2048], P(('seq', 'row'))
- grad_ff_gain: float32 [2048], P(('seq', 'row'))
The draws below stay inside these ranges and needn't reach their ends.
Inputs may be any that keep to these rules, and one draw needn't show every extreme that they name: Along each sequence segment_ids never fall; segment 0 holds the first 1 to 128 tokens, segment 2 the last 1 to 128 tokens, and segment 1 all between.
All inputs are finite; a program needn't handle non-finite values.
Results may differ from the reference program's by a relative error of at most 0.03.
Values may be sent and summed in bfloat16 or wider, within the bound.
No kernel may reach another device: no remote copies, remote signals or barrier semaphores. Data moves between devices by JAX's collectives and lax.ppermute only.
A program may use at most 512 MiB of HBM per device.

```python
import math
import jax
import jax.numpy as jnp
from jax import lax

D = 2048
HEADS = 16
HEAD_DIM = 128
FF = 8192
TOK_DEV = 256
SEQ_LEN = 1024
ROWS = 8


def draw_segment_ids(key, part):
    key = jax.random.fold_in(key, 7)
    first_key, last_key = jax.random.split(key)
    head_len = jax.random.randint(first_key, (ROWS, 1), 1, TOK_DEV // 2 + 1)
    tail_len = jax.random.randint(last_key, (ROWS, 1), 1, TOK_DEV // 2 + 1)
    places = jnp.arange(SEQ_LEN, dtype=jnp.int32)[None, :]
    return (places >= head_len).astype(jnp.int32) + (places >= SEQ_LEN - tail_len).astype(jnp.int32)


def strengthened(entries, stream_key, source, target, parts, factor):
    def block_of(dim):
        return (jnp.arange(entries.shape[dim]) // (entries.shape[dim] // parts)).reshape((-1,) + (1,) * (entries.ndim - 1 - dim))

    near = jax.random.permutation(stream_key, parts)[block_of(target)]
    other_side = (block_of(target) + parts // 2) % parts
    return jnp.where((block_of(source) == near) | (block_of(source) == other_side), factor * entries, entries)


def level_of(stream_key, dims, shards, least, largest):
    def one(axis_at, shards_of):
        draws = jax.random.uniform(jax.random.fold_in(jax.random.fold_in(stream_key, 6), axis_at), (shards_of,), jnp.float32, least / len(shards), largest / len(shards))
        return jnp.repeat(jnp.exp(draws), dims[axis_at] // shards_of).reshape((-1,) + (1,) * (len(dims) - axis_at - 1))

    gain = one(*shards[0])
    for cut in shards[1:]:
        gain = gain * one(*cut)
    return gain


def scatter_about(key, dims, width, bound, shards=(), held_as=jnp.bfloat16):
    entries = jax.random.normal(key, dims, jnp.float32) * width
    if len(shards) > 0:
        entries = level_of(key, dims, shards, -0.22, 0.18) * entries
    return jnp.clip(entries, min=-bound, max=bound).astype(held_as)


def noise_with(key, dims, deviation, limit, pieces, heavy, kind=jnp.bfloat16):
    drawn = deviation * jax.random.normal(key, dims, jnp.float32)
    if pieces:
        drawn = drawn * level_of(key, dims, pieces, -0.22, 0.18)
    return jnp.clip(strengthened(drawn, jax.random.fold_in(key, 3), *heavy), -limit, limit).astype(kind)


def setup_inputs(seed: int = 0) -> dict:
    streams_of = jax.random.split(jax.random.key(seed), 15)
    return {
        "tokens": noise_with(streams_of[0], (ROWS, SEQ_LEN, D), 1.0, 6.0, ((0, 8), (1, 4)), (0, 2, 8, 2.0)),
        "segment_ids": draw_segment_ids(jax.random.fold_in(streams_of[14], 71), 0),
        "w_query": scatter_about(streams_of[2], (D, D), D ** -0.5, 0.125, ((0, 32),)),
        "w_key": scatter_about(streams_of[3], (D, D), D ** -0.5, 0.125, ((0, 32),)),
        "w_value": scatter_about(streams_of[4], (D, D), D ** -0.5, 0.125, ((0, 32),)),
        "w_out": scatter_about(streams_of[5], (D, D), D ** -0.5, 0.125, ((0, 32),)),
        "w_gate": scatter_about(streams_of[6], (D, FF), D ** -0.5, 0.125, ((0, 32),)),
        "w_up": scatter_about(streams_of[7], (D, FF), D ** -0.5, 0.125, ((0, 32),)),
        "w_down": scatter_about(streams_of[8], (FF, D), FF ** -0.5, 0.0625, ((0, 32),)),
        "query_gain": jnp.clip(1.0 + 0.18 * jax.random.normal(streams_of[9], (D,), jnp.float32), 0.099609375, 1.8984375).astype(jnp.bfloat16),
        "key_gain": jnp.clip(1.0 + 0.18 * jax.random.normal(streams_of[10], (D,), jnp.float32), 0.099609375, 1.8984375).astype(jnp.bfloat16),
        "attn_gain": jnp.clip(1.0 + 0.18 * jax.random.normal(streams_of[11], (D,), jnp.float32), 0.099609375, 1.8984375).astype(jnp.bfloat16),
        "ff_gain": jnp.clip(1.0 + 0.18 * jax.random.normal(streams_of[12], (D,), jnp.float32), 0.099609375, 1.8984375).astype(jnp.bfloat16),
        "cotangent": noise_with(streams_of[13], (ROWS, SEQ_LEN, D), 1.0, 6.0, ((0, 8), (1, 4)), (0, 2, 8, 2.0)),
    }


rope_base = 500000.0
norm_eps = 1e-06
masked_score = -1e+30

@jax.custom_vjp
def low(v):
    return lax.optimization_barrier(v.astype(jnp.bfloat16)).astype(jnp.float32)

@jax.custom_vjp
def low_back(v):
    return v

def low_keep(v):
    return (low(v), None)

def low_pass(kept, grad):
    return (grad,)

def back_keep(v):
    return (v, None)

def back_low(kept, grad):
    return (low(grad),)
low.defvjp(low_keep, low_pass)
low_back.defvjp(back_keep, back_low)

def matmul_hi(left_side, right_side):
    return jnp.dot(left_side, right_side, precision=lax.Precision.HIGHEST)

def rope_tables(positions, head_dim):
    half_dim = head_dim // 2
    frequency = rope_base ** (-(jnp.arange(half_dim, dtype=jnp.float32) * 2.0 / head_dim))
    angles = positions.astype(jnp.float32)[:, None] * frequency[None, :]
    return (jnp.cos(angles)[:, None, :], jnp.sin(angles)[:, None, :])

def rms_scale(values, gain_vec):
    return values * lax.rsqrt(lax.optimization_barrier(jnp.mean(values * values, axis=-1, keepdims=True)) + norm_eps) * gain_vec

def normed_rope(raw_proj, gain_vec, cosine_table, sine_table, head_count):
    normed = rms_scale(raw_proj, gain_vec)
    split_heads = normed.reshape(raw_proj.shape[0], head_count, -1)
    half_dim = split_heads.shape[-1] // 2
    first_half = split_heads[..., :half_dim]
    second = split_heads[..., half_dim:]
    return jnp.concatenate([first_half * cosine_table - second * sine_table, second * cosine_table + first_half * sine_table], axis=-1)

def attention(query, key_all, value_all, row_ids):
    length = query.shape[0]
    block_rows = math.gcd(length, 512)
    key_pos = jnp.arange(length, dtype=jnp.int32)
    score_scale = HEAD_DIM ** (-0.5)

    def one_block(row_start):
        query_blk = lax.dynamic_slice_in_dim(query, row_start, block_rows, 0)
        query_ids = lax.dynamic_slice_in_dim(row_ids, row_start, block_rows, 0)
        query_pos = row_start + jnp.arange(block_rows, dtype=jnp.int32)
        scores = jnp.einsum('qhd,khd->hqk', query_blk, key_all, precision=lax.Precision.HIGHEST) * score_scale
        scores = low_back(scores)
        allowed = (query_ids[:, None] == row_ids[None, :]) & (query_pos[:, None] >= key_pos[None, :])
        scores = jnp.where(allowed[None], scores, masked_score)
        top_score = lax.optimization_barrier(jnp.max(scores, axis=-1, keepdims=True))
        expo = jnp.exp(scores - top_score)
        probability = expo / lax.optimization_barrier(jnp.sum(expo, axis=-1, keepdims=True))
        return jnp.einsum('hqk,khd->qhd', low(probability), value_all, precision=lax.Precision.HIGHEST)
    starts = jnp.arange(length // block_rows, dtype=jnp.int32) * block_rows
    blocks = lax.map(jax.checkpoint(one_block), starts)
    return blocks.reshape(length, -1)

def layer_row(row_input, row_ids, w_query, w_key, w_value, w_out, w_gate, w_up, w_down, query_gain, key_gain, attn_gain, ff_gain):
    length = row_input.shape[0]
    cosine_table, sine_table = rope_tables(jnp.arange(length, dtype=jnp.int32), HEAD_DIM)
    query_raw = low_back(matmul_hi(row_input, w_query))
    key_raw = low_back(matmul_hi(row_input, w_key))
    value_all = low(low_back(matmul_hi(row_input, w_value))).reshape(length, HEADS, HEAD_DIM)
    query = low(normed_rope(query_raw, query_gain, cosine_table, sine_table, HEADS))
    key_all = low(normed_rope(key_raw, key_gain, cosine_table, sine_table, HEADS))
    attn_low = low(low_back(attention(query, key_all, value_all, row_ids)))
    branch = low_back(matmul_hi(attn_low, w_out))
    hidden = row_input + rms_scale(branch, attn_gain)
    hidden_low = low(hidden)
    gate_act = low_back(matmul_hi(hidden_low, w_gate))
    up_act = low_back(matmul_hi(hidden_low, w_up))
    middle = low(jax.nn.silu(gate_act) * up_act)
    ff_raw = low_back(matmul_hi(middle, w_down))
    return hidden + rms_scale(ff_raw, ff_gain)

def reference(tokens, segment_ids, w_query, w_key, w_value, w_out, w_gate, w_up, w_down, query_gain, key_gain, attn_gain, ff_gain, cotangent):
    weights = tuple((item.astype(jnp.float32) for item in (w_query, w_key, w_value, w_out, w_gate, w_up, w_down, query_gain, key_gain, attn_gain, ff_gain)))

    def forward(all_rows, *params):
        row_fn = jax.checkpoint(lambda row_input, row_ids: layer_row(row_input, row_ids, *params))
        return lax.map(lambda pair_in: row_fn(pair_in[0], pair_in[1]), (all_rows, segment_ids))
    result, pullback = jax.vjp(forward, tokens.astype(jnp.float32), *weights)
    grads = pullback(cotangent.astype(jnp.float32))
    return (result.astype(jnp.bfloat16), grads[0], grads[1], grads[2], grads[3], grads[4], grads[5], grads[6], grads[7], grads[8], grads[9], grads[10], grads[11])
```

```python
import functools
import math

import jax
import jax.numpy as jnp
from jax import lax
from jax.experimental import pallas as pl
from jax.experimental.pallas import tpu as pltpu
from jax.sharding import Mesh
from jax.sharding import PartitionSpec as P

HEADS = 16

rope_base = 500000.0
norm_eps = 1e-06
masked_score = -1e30

bf16 = jnp.bfloat16
f32 = jnp.float32


def dims_of(axis):
    count = lax.axis_size(axis)
    return [(axis, 1 << bit) for bit in range(count.bit_length() - 1)]


def swap(block, dim):
    axis, mask = dim
    return lax.ppermute(block, axis, [(i, i ^ mask) for i in range(lax.axis_size(axis))])


def partner_index(dims, which):
    masks = {}
    for bit, (axis, mask) in enumerate(dims):
        if which >> bit & 1:
            masks[axis] = masks.get(axis, 0) | mask
    return masks


def column_cuts(width, count):
    tiles = width // 128
    return [round(tiles * i / count) * 128 for i in range(count + 1)]


def column_parts(block, count):
    cuts = column_cuts(block.shape[1], count)
    return [block[:, cuts[i] : cuts[i + 1]] for i in range(count)]


def route(which, count):
    bits = [i for i in range(count) if which >> i & 1]
    if len(bits) == 1:
        return bits[0]
    return bits[0] if bits[1] - bits[0] == 1 else bits[1]


def by_size(count):
    return sorted(range(1, 1 << count), key=lambda m: bin(m).count("1"))


def spread(block, dims):
    count = len(dims)
    full = (1 << count) - 1
    pieces = {0: block}
    for which in by_size(count):
        if which == full and count > 1:
            parts = [
                swap(column_parts(pieces[which ^ (1 << i)], count)[i], dims[i])
                for i in range(count)
            ]
            pieces[which] = jnp.concatenate(parts, axis=1)
        else:
            via = route(which, count)
            pieces[which] = swap(pieces[which ^ (1 << via)], dims[via])
    return [pieces[m] for m in range(1 << count)]


def collect(pieces, dims):
    count = len(dims)
    full = (1 << count) - 1
    pieces = list(pieces)
    got = {m: [] for m in range(1 << count)}
    for which in reversed(by_size(count)):
        total = pieces[which]
        if got[which]:
            total = total.astype(f32)
            for part, arrived in got[which]:
                if part is None:
                    total = total + arrived.astype(f32)
                else:
                    cuts = column_cuts(total.shape[1], count)
                    cols = column_parts(total, count)
                    cols[part] = cols[part] + arrived.astype(f32)
                    total = jnp.concatenate(cols, axis=1)
            total = total.astype(bf16)
        if which == full and count > 1:
            for i, cols in enumerate(column_parts(total, count)):
                got[which ^ (1 << i)].append((i, swap(cols, dims[i])))
        else:
            via = route(which, count)
            got[which ^ (1 << via)].append((None, swap(total, dims[via])))
    total = pieces[0].astype(f32)
    for _, arrived in got[0]:
        total = total + arrived.astype(f32)
    return total


def sum_all(table, dims):
    for bit, dim in enumerate(dims):
        there = swap(table, dim)
        order = [m ^ (1 << bit) for m in range(table.shape[0])]
        table = table + jnp.stack([there[m] for m in order])
    return table


def gather_blocks(block, dims, axes):
    pieces = {0: block}
    count = len(dims)
    for bit, dim in enumerate(dims):
        for m in range(1 << bit):
            pieces[m | (1 << bit)] = swap(pieces[m], dim)
    sizes = tuple(lax.axis_size(a) for a in axes)
    whole = jnp.zeros(sizes + block.shape, block.dtype)
    for m in range(1 << count):
        masks = partner_index(dims, m)
        at = tuple(lax.axis_index(a) ^ masks.get(a, 0) for a in axes)
        place = at + (0,) * block.ndim
        whole = lax.dynamic_update_slice(whole, pieces[m][(None,) * len(axes)], place)
    return whole


def scatter_blocks(whole, dims, axes):
    count = len(dims)
    shape = whole.shape[len(axes) :]

    def entry(m):
        masks = partner_index(dims, m)
        at = tuple(lax.axis_index(a) ^ masks.get(a, 0) for a in axes)
        piece = lax.dynamic_slice(whole, at + (0,) * len(shape), (1,) * len(axes) + shape)
        return piece.reshape(shape)

    pieces = [entry(m) for m in range(1 << count)]
    for bit in reversed(range(count)):
        half = 1 << bit
        kept = []
        for m in range(half):
            arrived = swap(pieces[m | half], dims[bit])
            total = pieces[m].astype(f32) + arrived.astype(f32)
            kept.append(total if bit == 0 else total.astype(bf16))
        pieces = kept
    return pieces[0]


def allowed_pairs(row_pos, row_ids, col_pos, col_ids):
    return (row_ids == col_ids) & (row_pos >= col_pos)


def forward_kernel(scale, rp, ri, cp, ci, q, k, v, out, log_total):
    scores = lax.dot_general(q[...], k[...], (((1,), (1,)), ((), ())), preferred_element_type=f32)
    allowed = allowed_pairs(rp[...], ri[...], cp[...], ci[...])
    scores = jnp.where(allowed, scores * scale, masked_score)
    top = jnp.max(scores, axis=-1, keepdims=True)
    expo = jnp.exp(scores - top)
    total = jnp.sum(expo, axis=-1, keepdims=True)
    probability = (expo * (1.0 / total)).astype(bf16)
    out[...] = jnp.dot(probability, v[...], preferred_element_type=f32)
    log_total[0] = top + jnp.log(total)


def backward_kernel(scale, rp, ri, cp, ci, q, k, v, d_out, out, log_total, d_q, d_k, d_v):
    @pl.when(pl.program_id(1) == 0)
    def _():
        d_k[...] = jnp.zeros_like(d_k)
        d_v[...] = jnp.zeros_like(d_v)

    q_blk, k_all, v_all, d_blk = q[...], k[...], v[...], d_out[...]
    scores = lax.dot_general(q_blk, k_all, (((1,), (1,)), ((), ())), preferred_element_type=f32)
    allowed = allowed_pairs(rp[...], ri[...], cp[...], ci[...])
    scores = jnp.where(allowed, scores * scale, masked_score)
    probability = jnp.exp(scores - log_total[0])
    row_dot = jnp.sum(d_blk.astype(f32) * out[...], axis=-1, keepdims=True)
    d_prob = lax.dot_general(d_blk, v_all, (((1,), (1,)), ((), ())), preferred_element_type=f32)
    d_scores = (probability * (d_prob - row_dot)).astype(bf16)
    d_q[...] = jnp.dot(d_scores, k_all, preferred_element_type=f32) * scale
    across = (((0,), (0,)), ((), ()))
    d_k[...] += lax.dot_general(d_scores, q_blk, across, preferred_element_type=f32) * scale
    d_v[...] += lax.dot_general(
        probability.astype(bf16), d_blk, across, preferred_element_type=f32
    )


def attention_specs(tokens, block, head_dim):
    rows = pl.BlockSpec((block, 1), lambda h, b: (b, 0))
    cols = pl.BlockSpec((1, tokens), lambda h, b: (0, 0))
    mine = pl.BlockSpec((block, head_dim), lambda h, b: (b, h))
    every = pl.BlockSpec((tokens, head_dim), lambda h, b: (0, h))
    logs = pl.BlockSpec((1, block, 1), lambda h, b: (h, b, 0))
    return rows, cols, mine, every, logs


def attend(places, q, k, v, heads, block):
    tokens, width = q.shape
    head_dim = width // heads
    rows, cols, mine, every, logs = attention_specs(tokens, block, head_dim)
    return pl.pallas_call(
        functools.partial(forward_kernel, head_dim**-0.5),
        grid=(heads, tokens // block),
        in_specs=[rows, rows, cols, cols, mine, every, every],
        out_specs=[mine, logs],
        out_shape=[
            jax.ShapeDtypeStruct((tokens, width), f32),
            jax.ShapeDtypeStruct((heads, tokens, 1), f32),
        ],
        compiler_params=pltpu.CompilerParams(vmem_limit_bytes=48 * 1024 * 1024),
        cost_estimate=pl.CostEstimate(
            flops=4 * tokens * tokens * width,
            bytes_accessed=14 * tokens * width,
            transcendentals=heads * tokens * tokens,
        ),
        name="attend",
    )(*places, q, k, v)


def attend_back(places, q, k, v, d_out, out, log_total, heads, block):
    tokens, width = q.shape
    head_dim = width // heads
    rows, cols, mine, every, logs = attention_specs(tokens, block, head_dim)
    return pl.pallas_call(
        functools.partial(backward_kernel, head_dim**-0.5),
        grid=(heads, tokens // block),
        in_specs=[rows, rows, cols, cols, mine, every, every, mine, mine, logs],
        out_specs=[mine, every, every],
        out_shape=[jax.ShapeDtypeStruct((tokens, width), f32)] * 3,
        compiler_params=pltpu.CompilerParams(vmem_limit_bytes=48 * 1024 * 1024),
        cost_estimate=pl.CostEstimate(
            flops=10 * tokens * tokens * width,
            bytes_accessed=24 * tokens * width,
            transcendentals=heads * tokens * tokens,
        ),
        name="attend_back",
    )(*places, q, k, v, d_out, out, log_total)


def dot(left, right):
    return jnp.dot(left, right, preferred_element_type=f32)


def dot_t(left, right):
    return lax.dot_general(left, right, (((1,), (1,)), ((), ())), preferred_element_type=f32)


def t_dot(left, right):
    return lax.dot_general(left, right, (((0,), (0,)), ((), ())), preferred_element_type=f32)


def held(block):
    return lax.optimization_barrier(block)


def rope_tables(positions, head_dim):
    half_dim = head_dim // 2
    frequency = rope_base ** (-(jnp.arange(half_dim, dtype=f32) * 2.0 / head_dim))
    angles = positions.astype(f32)[:, None] * frequency[None, :]
    cosine, sine = jnp.cos(angles), jnp.sin(angles)
    return jnp.concatenate([cosine, cosine], 1)[:, None, :], jnp.concatenate([-sine, sine], 1)[:, None, :]


def rotate(values, tables, heads, back=False):
    cosine, sine = tables
    split = values.reshape(values.shape[0], heads, -1)
    half = split.shape[-1] // 2
    other = jnp.concatenate([split[..., half:], split[..., :half]], axis=-1)
    turned = split * cosine - other * sine if back else split * cosine + other * sine
    return turned.reshape(values.shape)


def rms(values):
    inverse = lax.rsqrt(jnp.mean(values * values, axis=-1, keepdims=True) + norm_eps)
    return values * inverse, inverse


def rms_back(grad, normed, inverse, gain):
    scaled = grad * gain
    return (scaled - normed * jnp.mean(scaled * normed, axis=-1, keepdims=True)) * inverse


def per_device(
    tokens,
    segment_ids,
    w_query,
    w_key,
    w_value,
    w_out,
    w_gate,
    w_up,
    w_down,
    query_gain,
    key_gain,
    attn_gain,
    ff_gain,
    cotangent,
):
    inputs = tokens[0]
    tok, width = inputs.shape
    n_seq, n_hi, n_lo, n_core = (lax.axis_size(a) for a in ("seq", "zhi", "zlo", "core"))
    n_dev = n_seq * n_hi * n_lo * n_core
    seq = lax.axis_index("seq")
    heads = HEADS // n_seq
    head_dim = width // HEADS
    part = width // n_seq
    length = n_seq * tok
    d_rows = w_query.shape[0]
    ff_rows = w_down.shape[0]
    units = ff_rows * n_hi * n_core

    seq_dims = dims_of("seq")
    cube_dims = seq_dims + dims_of("zlo")
    z_dims = dims_of("zhi") + dims_of("zlo") + dims_of("core")
    pair_dims = dims_of("zhi") + dims_of("core")

    every = ("seq", "zhi", "zlo", "core")
    gains = jnp.stack([query_gain, key_gain, attn_gain, ff_gain])
    gains = lax.all_gather(gains, every, axis=0, tiled=False)
    gains = jnp.transpose(gains, (1, 0, 2)).reshape(4, width).astype(f32)
    my_cols = lambda row: lax.dynamic_slice(row, (seq * part,), (part,))
    gain_query, gain_key = my_cols(gains[0]), my_cols(gains[1])
    gain_attn, gain_ff = gains[2], gains[3]

    w_qkv = jnp.stack([w_query, w_key, w_value], 1).reshape(d_rows, 3, n_seq, part)
    w_qkv = jnp.transpose(w_qkv, (2, 0, 1, 3)).reshape(n_seq, d_rows, 3 * part)
    w_qkv = lax.all_to_all(w_qkv, "seq", 0, 0, tiled=True)
    w_qkv = gather_blocks(w_qkv, z_dims, ("zhi", "zlo", "core"))
    w_qkv = jnp.transpose(w_qkv, (3, 0, 1, 2, 4, 5)).reshape(width, 3 * part)
    out_weight = gather_blocks(w_out, z_dims, ("zhi", "zlo", "core")).reshape(part, width)

    x_all = jnp.concatenate(spread(inputs, seq_dims), axis=0)
    ids = jnp.concatenate(spread(segment_ids, seq_dims), axis=1) if n_seq == 1 else None
    id_pieces = {0: segment_ids}
    for m in by_size(len(seq_dims)):
        via = route(m, len(seq_dims))
        id_pieces[m] = swap(id_pieces[m ^ (1 << via)], seq_dims[via])
    ids = jnp.concatenate([id_pieces[m] for m in range(n_seq)], axis=1)
    positions = jnp.concatenate(
        [(seq ^ m) * tok + jnp.arange(tok, dtype=jnp.int32) for m in range(n_seq)]
    )
    places = (positions[:, None], ids.reshape(length, 1), positions[None, :], ids)
    tables = rope_tables(positions, head_dim)

    w_gu = jnp.stack([w_gate, w_up], 1).reshape(d_rows, 2, n_seq, n_hi, n_lo, n_core, ff_rows)
    w_gu = jnp.transpose(w_gu, (2, 4, 0, 1, 3, 5, 6)).reshape(n_seq * n_lo, d_rows, 2 * units)
    w_gu = lax.all_to_all(w_gu, ("seq", "zlo"), 0, 0, tiled=True)
    w_gu = w_gu.reshape(n_seq, n_lo, d_rows, 2 * units)
    w_gu = gather_blocks(w_gu, pair_dims, ("zhi", "core"))
    w_gu = jnp.transpose(w_gu, (2, 0, 3, 1, 4, 5)).reshape(width, 2 * units)
    down = gather_blocks(w_down, pair_dims, ("zhi", "core")).reshape(units, width)

    raw = dot(x_all, w_qkv)
    query_raw, key_raw = raw[:, :part], raw[:, part : 2 * part]
    value = raw[:, 2 * part :].astype(bf16)
    squares = jnp.stack(
        [jnp.sum(query_raw * query_raw, -1), jnp.sum(key_raw * key_raw, -1)]
    ).reshape(2, n_seq, tok)
    squares = sum_all(jnp.transpose(squares, (1, 0, 2)), seq_dims)
    inverse = lax.rsqrt(jnp.transpose(squares, (1, 0, 2)).reshape(2, length, 1) / width + norm_eps)
    query_norm, key_norm = query_raw * inverse[0], key_raw * inverse[1]
    query = rotate(query_norm * gain_query, tables, heads).astype(bf16)
    key = rotate(key_norm * gain_key, tables, heads).astype(bf16)

    attended, log_total = attend(places, query, key, value, heads, tok)
    attn_low = attended.astype(bf16)
    rows_of = lambda block, m: block[m * tok : (m + 1) * tok]
    branch = collect(
        [held(dot(rows_of(attn_low, m), out_weight).astype(bf16)) for m in range(n_seq)], seq_dims
    )
    branch_norm, branch_inv = rms(branch)
    hidden = inputs.astype(f32) + branch_norm * gain_attn
    hidden_low = hidden.astype(bf16)

    h_pieces = spread(hidden_low, cube_dims)
    gates, ups, middles, partials = [], [], [], []
    for piece in h_pieces:
        gate_act = dot(piece, w_gu[:, :units])
        up_act = dot(piece, w_gu[:, units:])
        middle = (jax.nn.silu(gate_act) * up_act).astype(bf16)
        gates.append(gate_act)
        ups.append(up_act)
        middles.append(middle)
        partials.append(held(dot(middle, down).astype(bf16)))
    ff_raw = collect(partials, cube_dims)
    ff_norm, ff_inv = rms(ff_raw)
    mixed = (hidden + ff_norm * gain_ff).astype(bf16)

    grad_output = cotangent[0].astype(f32)
    grad_ff_gain = jnp.sum(grad_output * ff_norm, axis=0)
    d_ff = rms_back(grad_output, ff_norm, ff_inv, gain_ff).astype(bf16)
    d_ff_pieces = spread(d_ff, cube_dims)
    d_gus, partials = [], []
    for piece, gate_act, up_act in zip(d_ff_pieces, gates, ups, strict=True):
        d_middle = dot_t(piece, down)
        sig = jax.nn.sigmoid(gate_act)
        d_gate = d_middle * up_act * (sig * (1.0 + gate_act * (1.0 - sig)))
        d_up = d_middle * (gate_act * sig)
        d_gu = jnp.concatenate([d_gate.astype(bf16), d_up.astype(bf16)], axis=1)
        d_gus.append(d_gu)
        partials.append(held(dot_t(d_gu, w_gu).astype(bf16)))
    d_hidden = grad_output + collect(partials, cube_dims)

    d_ff_all = jnp.concatenate(d_ff_pieces, axis=0)
    grad_down = t_dot(jnp.concatenate(middles, axis=0), d_ff_all).astype(bf16)
    grad_down = scatter_blocks(
        grad_down.reshape(n_hi, n_core, ff_rows, width), pair_dims, ("zhi", "core")
    )
    grad_gu = t_dot(jnp.concatenate(h_pieces, axis=0), jnp.concatenate(d_gus, axis=0)).astype(bf16)
    grad_gu = grad_gu.reshape(n_seq, n_hi, n_lo, n_core, d_rows, 2 * units)
    grad_gu = jnp.transpose(grad_gu, (1, 3, 0, 2, 4, 5))
    grad_gu = scatter_blocks(grad_gu, pair_dims, ("zhi", "core")).astype(bf16)
    grad_gu = grad_gu.reshape(n_seq * n_lo, d_rows, 2 * units)
    grad_gu = lax.all_to_all(grad_gu, ("seq", "zlo"), 0, 0, tiled=True)
    grad_gu = grad_gu.reshape(n_seq, n_lo, d_rows, 2, n_hi, n_core, ff_rows)
    grad_gu = jnp.transpose(grad_gu, (3, 2, 0, 4, 1, 5, 6)).reshape(2, d_rows, -1).astype(f32)

    grad_attn_gain = jnp.sum(d_hidden * branch_norm, axis=0)
    d_branch = rms_back(d_hidden, branch_norm, branch_inv, gain_attn).astype(bf16)
    d_branch_all = jnp.concatenate(spread(d_branch, seq_dims), axis=0)
    d_attended = dot_t(d_branch_all, out_weight).astype(bf16)
    grad_out = t_dot(attn_low, d_branch_all).astype(bf16)
    grad_out = scatter_blocks(
        grad_out.reshape(n_hi, n_lo, n_core, d_rows, width), z_dims, ("zhi", "zlo", "core")
    )
    d_query, d_key, d_value = attend_back(
        places, query, key, value, d_attended, attended, log_total, heads, tok
    )
    e_query = rotate(d_query, tables, heads, back=True)
    e_key = rotate(d_key, tables, heads, back=True)
    grad_query_gain = jnp.sum(e_query * query_norm, axis=0)
    grad_key_gain = jnp.sum(e_key * key_norm, axis=0)
    e_query, e_key = e_query * gain_query, e_key * gain_key
    means = jnp.stack(
        [jnp.sum(e_query * query_norm, -1), jnp.sum(e_key * key_norm, -1)]
    ).reshape(2, n_seq, tok)
    means = sum_all(jnp.transpose(means, (1, 0, 2)), seq_dims)
    means = jnp.transpose(means, (1, 0, 2)).reshape(2, length, 1) / width
    d_qkv = jnp.concatenate(
        [
            ((e_query - query_norm * means[0]) * inverse[0]).astype(bf16),
            ((e_key - key_norm * means[1]) * inverse[1]).astype(bf16),
            d_value.astype(bf16),
        ],
        axis=1,
    )
    grad_qkv = t_dot(x_all, d_qkv).astype(bf16)
    grad_qkv = grad_qkv.reshape(n_seq, n_hi, n_lo, n_core, d_rows, 3 * part)
    grad_qkv = jnp.transpose(grad_qkv, (1, 2, 3, 0, 4, 5))
    grad_qkv = scatter_blocks(grad_qkv, z_dims, ("zhi", "zlo", "core")).astype(bf16)
    grad_qkv = lax.all_to_all(grad_qkv, "seq", 0, 0, tiled=True)
    grad_qkv = grad_qkv.reshape(n_seq, d_rows, 3, part)
    grad_qkv = jnp.transpose(grad_qkv, (2, 1, 0, 3)).reshape(3, d_rows, width).astype(f32)

    input_grad = d_hidden + collect(
        [held(dot_t(rows_of(d_qkv, m), w_qkv).astype(bf16)) for m in range(n_seq)], seq_dims
    )

    full_row = lambda cols: lax.dynamic_update_slice(jnp.zeros((width,), f32), cols, (seq * part,))
    rows = jnp.stack(
        [full_row(grad_query_gain), full_row(grad_key_gain), grad_attn_gain, grad_ff_gain]
    )
    rows = jnp.transpose(rows.reshape(4, n_dev, d_rows), (1, 0, 2)).reshape(n_dev, 4 * d_rows)
    rows = lax.psum_scatter(rows, every, scatter_dimension=0, tiled=False).reshape(4, d_rows)

    return (
        mixed[None],
        input_grad[None],
        grad_qkv[0],
        grad_qkv[1],
        grad_qkv[2],
        grad_out,
        grad_gu[0],
        grad_gu[1],
        grad_down,
        rows[0],
        rows[1],
        rows[2],
        rows[3],
    )


def solution(mesh):
    n_seq, n_row = mesh.shape["seq"], mesh.shape["row"]
    n_core = 2
    n_lo = 2
    n_hi = n_row // (n_core * n_lo)
    cut = Mesh(
        mesh.devices.reshape(n_seq, n_hi, n_lo, n_core), ("seq", "zhi", "zlo", "core")
    )
    row = ("zhi", "zlo", "core")
    every = ("seq",) + row
    acts = P(row, "seq", None)
    matrix = P(every, None)
    vector = P(every)
    return jax.shard_map(
        per_device,
        mesh=cut,
        in_specs=(acts, P(row, "seq")) + (matrix,) * 7 + (vector,) * 4 + (acts,),
        out_specs=(acts, acts) + (matrix,) * 7 + (vector,) * 4,
        check_vma=False,
    )
```

```python
import functools
import math

import jax
import jax.numpy as jnp
from jax import lax
from jax.experimental import pallas as pl
from jax.experimental.pallas import tpu as pltpu
from jax.sharding import Mesh
from jax.sharding import PartitionSpec as P

HEADS = 16

rope_base = 500000.0
norm_eps = 1e-06
masked_score = -1e30

bf16 = jnp.bfloat16
f32 = jnp.float32


def dims_of(axis):
    count = lax.axis_size(axis)
    return [(axis, 1 << bit) for bit in range(count.bit_length() - 1)]


def swap(block, dim):
    axis, mask = dim
    return lax.ppermute(block, axis, [(i, i ^ mask) for i in range(lax.axis_size(axis))])


def partner_index(dims, which):
    masks = {}
    for bit, (axis, mask) in enumerate(dims):
        if which >> bit & 1:
            masks[axis] = masks.get(axis, 0) | mask
    return masks


def column_cuts(width, count):
    tiles = width // 128
    return [round(tiles * i / count) * 128 for i in range(count + 1)]


def column_parts(block, count):
    cuts = column_cuts(block.shape[1], count)
    return [block[:, cuts[i] : cuts[i + 1]] for i in range(count)]


def route(which, count):
    bits = [i for i in range(count) if which >> i & 1]
    if len(bits) == 1:
        return bits[0]
    return bits[0] if bits[1] - bits[0] == 1 else bits[1]


def by_size(count):
    return sorted(range(1, 1 << count), key=lambda m: bin(m).count("1"))


class Spread:
    def __init__(self, block, dims, spare_last=False):
        self.dims, self.size, self.pieces, self.new = dims, 0, {0: block}, [0]
        self.spare_last = spare_last and len(dims) == 3

    def light_step(self):
        x, y, _ = self.dims
        half = lambda m, i: column_parts(self.pieces[m], 2)[i]
        if self.size == 2:
            self.new = [3]
            self.pieces[3] = jnp.concatenate([swap(half(2, 0), x), swap(half(1, 1), y)], axis=1)
        elif self.size == 3:
            self.new = [5, 6]
            self.pieces[5], self.pieces[6] = swap(self.pieces[4], x), swap(self.pieces[4], y)
        else:
            self.new = [7]
            self.pieces[7] = jnp.concatenate([swap(half(6, 0), x), swap(half(5, 1), y)], axis=1)

    def step(self):
        self.size += 1
        count = len(self.dims)
        if self.spare_last and self.size > 1:
            self.light_step()
            return self
        self.new = [m for m in by_size(count) if bin(m).count("1") == self.size]
        for which in self.new:
            if self.size == count and count > 1:
                parts = [
                    swap(column_parts(self.pieces[which ^ (1 << i)], count)[i], self.dims[i])
                    for i in range(count)
                ]
                self.pieces[which] = jnp.concatenate(parts, axis=1)
            else:
                via = route(which, count)
                self.pieces[which] = swap(self.pieces[which ^ (1 << via)], self.dims[via])
        return self

    def fresh(self):
        return [self.pieces[m] for m in self.new]

    def renew(self, values):
        self.pieces.update(zip(self.new, values, strict=True))

    def whole(self):
        while self.size < len(self.dims):
            self.step()
        return [self.pieces[m] for m in range(1 << len(self.dims))]


class Collect:
    def __init__(self, pieces, dims):
        self.dims, self.size, self.pieces = dims, len(dims), list(pieces)
        self.got, self.new = {m: [] for m in range(len(self.pieces))}, []

    def step(self):
        count = len(self.dims)
        self.new = []
        for which in by_size(count):
            if bin(which).count("1") != self.size:
                continue
            total = self.total(which)
            if self.size == count and count > 1:
                for i, cols in enumerate(column_parts(total, count)):
                    self.keep(which ^ (1 << i), i, swap(cols, self.dims[i]))
            else:
                via = route(which, count)
                self.keep(which ^ (1 << via), None, swap(total, self.dims[via]))
        self.size -= 1
        return self

    def keep(self, which, part, arrived):
        self.new.append((which, len(self.got[which])))
        self.got[which].append((part, arrived))

    def total(self, which):
        if not self.got[which]:
            return self.pieces[which]
        count = len(self.dims)
        total = self.pieces[which].astype(f32)
        for part, arrived in self.got[which]:
            if part is None:
                total = total + arrived.astype(f32)
            else:
                cols = column_parts(total, count)
                cols[part] = cols[part] + arrived.astype(f32)
                total = jnp.concatenate(cols, axis=1)
        return total.astype(bf16)

    def fresh(self):
        return [self.got[which][i][1] for which, i in self.new]

    def renew(self, values):
        for (which, i), value in zip(self.new, values, strict=True):
            self.got[which][i] = (self.got[which][i][0], value)

    def whole(self):
        while self.size > 0:
            self.step()
        total = self.pieces[0].astype(f32)
        for _, arrived in self.got[0]:
            total = total + arrived.astype(f32)
        return total


def tie(*items):
    steps = (Spread, Collect)
    values = [item.fresh() if isinstance(item, steps) else item for item in items]
    values = lax.optimization_barrier(values)
    rest = []
    for item, value in zip(items, values, strict=True):
        if isinstance(item, steps):
            item.renew(value)
        else:
            rest.append(value)
    return rest


def sum_all(table, dims):
    for bit, dim in enumerate(dims):
        there = swap(table, dim)
        order = [m ^ (1 << bit) for m in range(table.shape[0])]
        table = table + jnp.stack([there[m] for m in order])
    return table


def after(block, *earlier):
    return lax.optimization_barrier((block, earlier))[0]


def block_starts(blocks, rows, dims, axes, order):
    starts = []
    for m in range(1 << len(dims)):
        masks = partner_index(dims, m)
        at = [lax.axis_index(a) ^ masks.get(a, 0) for a in axes]
        starts += [order(block, *at) * rows for block in range(blocks)]
    return jnp.stack(starts).astype(jnp.int32)


def project(x_pieces, w_pieces, starts, out_starts, tok, part):
    n_x, n_w = len(x_pieces), len(w_pieces)
    width = x_pieces[0].shape[1]
    blocks, rows, _ = w_pieces[0].shape
    length = n_x * tok
    number = n_w * blocks

    def kernel(table, out_table, *refs):
        xs, ws = refs[:n_x], refs[n_x : n_x + n_w]
        raw, squares, x_out, w_out, o_out, x_all, w_all, o_all, sems = refs[n_x + n_w :]
        at = pl.program_id(0)
        arrive, later = [], []
        for i in range(n_x):
            source, target = xs[i].at[pl.ds(0, tok)], x_all.at[pl.ds(i * tok, tok)]
            arrive.append(pltpu.make_async_copy(source, target, sems.at[i]))
        for i in range(number):
            piece, block = ws[i // blocks], i % blocks
            here = pl.ds(pl.multiple_of(table[i], rows), rows)
            source = piece.at[block, :, pl.ds(0, 3 * part)]
            arrive.append(pltpu.make_async_copy(source, w_all.at[here], sems.at[n_x + i]))
            here = pl.ds(pl.multiple_of(out_table[i // blocks], rows), rows)
            source = piece.at[block, :, pl.ds(3 * part, part)]
            target = o_all.at[here, pl.ds(block * part, part)]
            later.append(pltpu.make_async_copy(source, target, sems.at[n_x + number + i]))
        sem = n_x + 2 * number
        keep = [
            pltpu.make_async_copy(x_all, x_out, sems.at[sem]),
            pltpu.make_async_copy(w_all, w_out, sems.at[sem + 1]),
        ]
        keep_out = pltpu.make_async_copy(o_all, o_out, sems.at[sem + 2])

        @pl.when(at == 0)
        def _():
            for copy in arrive + later:
                copy.start()
            for copy in arrive:
                copy.wait()
            for copy in keep:
                copy.start()

        for step in range(3):

            @pl.when(at == step)
            def _(step=step):
                product = dot(x_all[...], w_all[:, step * part : (step + 1) * part])
                raw[...] = product
                if step < 2:
                    squares[0] = jnp.sum(product * product, axis=-1, keepdims=True)
                if step == 0:
                    for copy in later:
                        copy.wait()
                    keep_out.start()

        @pl.when(at == 2)
        def _():
            for copy in keep + [keep_out]:
                copy.wait()

    somewhere = pl.BlockSpec(memory_space=pl.ANY)
    scalars = pl.BlockSpec(memory_space=pltpu.SMEM)
    return pl.pallas_call(
        kernel,
        grid=(3,),
        in_specs=[scalars] * 2 + [somewhere] * (n_x + n_w),
        out_specs=[
            pl.BlockSpec((length, part), lambda j: (0, j)),
            pl.BlockSpec((1, length, 1), lambda j: (jnp.minimum(j, 1), 0, 0)),
            somewhere,
            somewhere,
            somewhere,
        ],
        out_shape=[
            jax.ShapeDtypeStruct((length, 3 * part), f32),
            jax.ShapeDtypeStruct((2, length, 1), f32),
            jax.ShapeDtypeStruct((length, width), bf16),
            jax.ShapeDtypeStruct((width, 3 * part), bf16),
            jax.ShapeDtypeStruct((n_w * rows, blocks * part), bf16),
        ],
        scratch_shapes=[
            pltpu.VMEM((length, width), bf16),
            pltpu.VMEM((width, 3 * part), bf16),
            pltpu.VMEM((n_w * rows, blocks * part), bf16),
            pltpu.SemaphoreType.DMA((n_x + 2 * number + 3,)),
        ],
        compiler_params=pltpu.CompilerParams(vmem_limit_bytes=40 * 1024 * 1024),
        cost_estimate=pl.CostEstimate(
            flops=6 * length * width * part, bytes_accessed=20 * length * part, transcendentals=0
        ),
        name="project",
    )(starts, out_starts, *x_pieces, *w_pieces)


def regroup(blocks, order):
    number, rows, width = blocks.shape

    def kernel(ref, out, sems):
        copies = [
            pltpu.make_async_copy(ref.at[at], out.at[pl.ds(i * rows, rows)], sems.at[i])
            for i, at in enumerate(order)
        ]
        for copy in copies:
            copy.start()
        for copy in copies:
            copy.wait()

    return pl.pallas_call(
        kernel,
        in_specs=[pl.BlockSpec(memory_space=pltpu.HBM)],
        out_specs=pl.BlockSpec(memory_space=pltpu.VMEM),
        out_shape=jax.ShapeDtypeStruct((number * rows, width), blocks.dtype),
        scratch_shapes=[pltpu.SemaphoreType.DMA((number,))],
        compiler_params=pltpu.CompilerParams(vmem_limit_bytes=24 * 1024 * 1024),
        name="regroup",
    )(blocks)


def take_blocks(whole, dims, axes):
    shape = whole.shape[len(axes) :]
    pieces = []
    for m in range(1 << len(dims)):
        masks = partner_index(dims, m)
        at = tuple(lax.axis_index(a) ^ masks.get(a, 0) for a in axes)
        piece = lax.dynamic_slice(whole, at + (0,) * len(shape), (1,) * len(axes) + shape)
        pieces.append(piece.reshape(shape))
    return pieces


def add_low(kept, arrived):
    return (kept.astype(f32) + arrived.astype(f32)).astype(bf16)


def gather_row(row, dims):
    for axis, mask in dims:
        there = swap(row, (axis, mask))
        low = (lax.axis_index(axis) & mask) == 0
        row = jnp.concatenate([jnp.where(low, row, there), jnp.where(low, there, row)], axis=0)
    return row


def turned(raw, inverse, gain, cosine, sine):
    scaled = raw * inverse * gain
    return scaled * cosine + pltpu.roll(scaled, scaled.shape[1] // 2, 1) * sine


def turned_back(grad, raw, inverse, gain, cosine, sine):
    back = grad * cosine - pltpu.roll(grad, grad.shape[1] // 2, 1) * sine
    product = back * (raw * inverse)
    return back * gain, jnp.sum(product * gain, -1, keepdims=True), jnp.sum(product, 0, keepdims=True)


def block_scores(scale, last, a, j, q, k, row_ids, col_ids):
    scores = dot_t(q, k) * scale
    allowed = None
    if j == 0 or a == last:
        allowed = row_ids == col_ids
    if j == a:
        shape = scores.shape
        causal = lax.broadcasted_iota(jnp.int32, shape, 0) >= lax.broadcasted_iota(jnp.int32, shape, 1)
        allowed = causal if allowed is None else allowed & causal
    return scores if allowed is None else jnp.where(allowed, scores, masked_score)


def forward_kernel(
    scale, count, tok, place, q_raw, k_raw, v_raw, q_inv, k_inv, q_gain, k_gain, cosine, sine,
    row_ids, col_ids, out, low, log_total, k_all, v_all,
):
    rows = lambda j: pl.ds(pl.multiple_of((place[0] ^ j) * tok, tok), tok)
    cols = lambda j: slice(j * tok, (j + 1) * tok)
    for a in range(count):
        here = rows(a)
        table = (cosine[cols(a), :], sine[cols(a), :])
        k_all[cols(a), :] = turned(k_raw[here, :], k_inv[0, here, :], k_gain[...], *table).astype(bf16)
        v_all[cols(a), :] = v_raw[here, :].astype(bf16)
        q = turned(q_raw[here, :], q_inv[0, here, :], q_gain[...], *table).astype(bf16)
        scores = [
            block_scores(scale, count - 1, a, j, q, k_all[cols(j), :], row_ids[here, :], col_ids[j])
            for j in range(a + 1)
        ]
        top = jnp.max(functools.reduce(jnp.maximum, scores), axis=-1, keepdims=True)
        expo = [jnp.exp2(block - top) for block in scores]
        total = jnp.sum(functools.reduce(jnp.add, expo), axis=-1, keepdims=True)
        parts = [dot(expo[j].astype(bf16), v_all[cols(j), :]) for j in range(a + 1)]
        attended = functools.reduce(jnp.add, parts) * (1.0 / total)
        out[here, :] = attended
        low[here, :] = attended.astype(bf16)
        log_total[0, here, :] = top + jnp.log2(total)


def backward_kernel(
    scale, plain_scale, count, tok, place, q_raw, k_raw, v_raw, q_inv, k_inv, q_gain, k_gain,
    cosine, sine, row_ids, col_ids, d_out, out, log_total,
    e_q, e_k, d_v, q_sum, k_sum, q_gain_grad, k_gain_grad, k_all, v_all, d_k_all, d_v_all,
):
    rows = lambda j: pl.ds(pl.multiple_of((place[0] ^ j) * tok, tok), tok)
    cols = lambda j: slice(j * tok, (j + 1) * tok)
    q_gain_grad[...] = jnp.zeros_like(q_gain_grad)

    @pl.when(pl.program_id(0) == 0)
    def _():
        q_sum[...] = jnp.zeros_like(q_sum)
        k_sum[...] = jnp.zeros_like(k_sum)

    for a in range(count):
        here = rows(a)
        table = (cosine[cols(a), :], sine[cols(a), :])
        k_all[cols(a), :] = turned(k_raw[here, :], k_inv[0, here, :], k_gain[...], *table).astype(bf16)
        v_all[cols(a), :] = v_raw[here, :].astype(bf16)
        q_row, inverse = q_raw[here, :], q_inv[0, here, :]
        q = turned(q_row, inverse, q_gain[...], *table).astype(bf16)
        d_blk = d_out[here, :]
        row_dot = jnp.sum(d_blk.astype(f32) * out[here, :], axis=-1, keepdims=True)
        d_q = []
        for j in range(a + 1):
            k = k_all[cols(j), :]
            scores = block_scores(scale, count - 1, a, j, q, k, row_ids[here, :], col_ids[j])
            probability = jnp.exp2(scores - log_total[0, here, :])
            d_prob = dot_t(d_blk, v_all[cols(j), :])
            d_scores = (probability * (d_prob - row_dot)).astype(bf16)
            d_q.append(dot(d_scores, k))
            d_k = t_dot(d_scores, q)
            d_v_part = t_dot(probability.astype(bf16), d_blk)
            if j == a:
                d_k_all[cols(j), :] = d_k
                d_v_all[cols(j), :] = d_v_part
            else:
                d_k_all[cols(j), :] += d_k
                d_v_all[cols(j), :] += d_v_part
        e_q[here, :], row_sum, gain_grad = turned_back(
            functools.reduce(jnp.add, d_q) * plain_scale, q_row, inverse, q_gain[...], *table
        )
        q_sum[0, here, :] += row_sum
        q_gain_grad[...] += gain_grad
    k_gain_grad[...] = jnp.zeros_like(k_gain_grad)
    for j in range(count):
        here = rows(j)
        e_k[here, :], row_sum, gain_grad = turned_back(
            d_k_all[cols(j), :] * plain_scale, k_raw[here, :], k_inv[0, here, :],
            k_gain[...], cosine[cols(j), :], sine[cols(j), :],
        )
        k_sum[0, here, :] += row_sum
        k_gain_grad[...] += gain_grad
        d_v[here, :] = d_v_all[cols(j), :].astype(bf16)


def attention_specs(tokens, block, heads, head_dim):
    head = lambda i: pl.BlockSpec((tokens, head_dim), lambda h, s: (0, i * heads + h))
    whole = lambda shape: pl.BlockSpec(shape, lambda h, s: (0,) * len(shape))
    vector = pl.BlockSpec((1, head_dim), lambda h, s: (0, h))
    inverse = lambda i: pl.BlockSpec((1, tokens, 1), lambda h, s: (i, 0, 0))
    inputs = [head(0), head(1), head(2), inverse(0), inverse(1), vector, vector]
    inputs += [whole((tokens, head_dim))] * 2
    inputs += [whole((tokens, 1)), whole((tokens // block, 1, block))]
    logs = pl.BlockSpec((1, tokens, 1), lambda h, s: (h, 0, 0))
    return inputs, head(0), logs, vector


def attend(context, heads, block):
    place, raw, inverse, gains, tables, ids = context
    tokens, width = raw.shape[0], raw.shape[1] // 3
    head_dim = width // heads
    inputs, head, logs, _ = attention_specs(tokens, block, heads, head_dim)
    return pl.pallas_call(
        functools.partial(forward_kernel, head_dim**-0.5 * math.log2(math.e), tokens // block, block),
        grid_spec=pltpu.PrefetchScalarGridSpec(
            num_scalar_prefetch=1,
            grid=(heads,),
            in_specs=inputs,
            out_specs=[head, head, logs],
            scratch_shapes=[pltpu.VMEM((tokens, head_dim), bf16)] * 2,
        ),
        out_shape=[
            jax.ShapeDtypeStruct((tokens, width), f32),
            jax.ShapeDtypeStruct((tokens, width), bf16),
            jax.ShapeDtypeStruct((heads, tokens, 1), f32),
        ],
        compiler_params=pltpu.CompilerParams(vmem_limit_bytes=40 * 1024 * 1024),
        cost_estimate=pl.CostEstimate(
            flops=2 * tokens * tokens * width,
            bytes_accessed=18 * tokens * width,
            transcendentals=heads * tokens * tokens // 2,
        ),
        name="attend",
    )(place, raw, raw, raw, inverse, inverse, *gains, *tables, *ids)


def attend_back(context, d_out, out, log_total, heads, block):
    place, raw, inverse, gains, tables, ids = context
    tokens, width = raw.shape[0], raw.shape[1] // 3
    head_dim = width // heads
    inputs, head, logs, vector = attention_specs(tokens, block, heads, head_dim)
    sums = pl.BlockSpec((1, tokens, 1), lambda h, s: (0, 0, 0))
    scale = head_dim**-0.5
    return pl.pallas_call(
        functools.partial(
            backward_kernel, scale * math.log2(math.e), scale, tokens // block, block
        ),
        grid_spec=pltpu.PrefetchScalarGridSpec(
            num_scalar_prefetch=1,
            grid=(heads,),
            in_specs=inputs + [head, head, logs],
            out_specs=[head, head, head, sums, sums, vector, vector],
            scratch_shapes=[pltpu.VMEM((tokens, head_dim), bf16)] * 2
            + [pltpu.VMEM((tokens, head_dim), f32)] * 2,
        ),
        out_shape=[
            jax.ShapeDtypeStruct((tokens, width), f32),
            jax.ShapeDtypeStruct((tokens, width), f32),
            jax.ShapeDtypeStruct((tokens, width), bf16),
        ]
        + [jax.ShapeDtypeStruct((1, tokens, 1), f32)] * 2
        + [jax.ShapeDtypeStruct((1, width), f32)] * 2,
        compiler_params=pltpu.CompilerParams(vmem_limit_bytes=40 * 1024 * 1024),
        cost_estimate=pl.CostEstimate(
            flops=5 * tokens * tokens * width,
            bytes_accessed=30 * tokens * width,
            transcendentals=heads * tokens * tokens // 2,
        ),
        name="attend_back",
    )(place, raw, raw, raw, inverse, inverse, *gains, *tables, *ids, d_out, out, log_total)


def sigmoid(values):
    return 1.0 / (1.0 + jnp.exp(-values))


def feed_kernel(with_down, masks, tok, steps, refs):
    number = len(masks)
    pieces, refs = refs[:number], refs[number:]
    down = refs[2] if with_down else None
    w_gate, w_up, refs = refs[0], refs[1], refs[2 + with_down :]
    h_all, middle_all, refs = refs[0], refs[1], refs[2:]
    gates, ups, refs = refs[:number], refs[number : 2 * number], refs[2 * number :]
    partials, refs = refs[: len(refs) - 3 - with_down], refs[len(refs) - 3 - with_down :]
    held_h, held_middle, sems = refs[0], refs[1], refs[-1]
    held_down = refs[2] if with_down else None
    at = pl.program_id(0)
    part = gates[0].shape[1]
    block = lambda i: pl.ds(i * tok, tok)
    copies = lambda held, whole, first: [
        pltpu.make_async_copy(held.at[block(i)], whole.at[block(m)], sems.at[first + i])
        for i, m in enumerate(masks)
    ]
    arrive = [
        pltpu.make_async_copy(pieces[i], held_h.at[block(i)], sems.at[i]) for i in range(number)
    ]
    keep_h, keep_middle = copies(held_h, h_all, number), copies(held_middle, middle_all, 2 * number)
    weights = [pltpu.make_async_copy(down, held_down, sems.at[3 * number])] if with_down else []

    @pl.when(at == 0)
    def _():
        for copy in arrive + weights:
            copy.start()
        for copy in arrive:
            copy.wait()
        for copy in keep_h:
            copy.start()

    gate_act = dot(held_h[...], w_gate[...])
    up_act = dot(held_h[...], w_up[...])
    middle = (gate_act * sigmoid(gate_act) * up_act).astype(bf16)
    for i in range(number):
        gates[i][...] = gate_act[i * tok : (i + 1) * tok].astype(bf16)
        ups[i][...] = up_act[i * tok : (i + 1) * tok].astype(bf16)
    for step in range(steps):

        @pl.when(at == step)
        def _(step=step):
            held_middle[:, step * part : (step + 1) * part] = middle

    @pl.when(at == steps - 1)
    def _():
        for copy in keep_middle:
            copy.start()
        for copy in weights:
            copy.wait()
        for i, out in enumerate(partials):
            out[...] = dot(held_middle[i * tok : (i + 1) * tok, :], held_down[...]).astype(bf16)
        for copy in keep_h + keep_middle:
            copy.wait()


def feed_back_kernel(masks, tok, steps, refs):
    number = len(masks)
    pieces, refs = refs[:number], refs[number:]
    gates, ups, refs = refs[:number], refs[number : 2 * number], refs[2 * number :]
    down, w_gu, d_ff_all, d_gate_all, d_up_all = refs[:5]
    partials, (held_d, held_gu, held_w, sems) = refs[5 : 5 + number], refs[5 + number :]
    at = pl.program_id(0)
    part = gates[0].shape[1]
    units = steps * part
    block = lambda i: pl.ds(i * tok, tok)
    arrive, keep_d, keep_gu = [], [], []
    for i, m in enumerate(masks):
        arrive.append(pltpu.make_async_copy(pieces[i], held_d.at[block(i)], sems.at[i]))
        keep_d.append(
            pltpu.make_async_copy(held_d.at[block(i)], d_ff_all.at[block(m)], sems.at[number + i])
        )
        for j, whole in enumerate((d_gate_all, d_up_all)):
            source = held_gu.at[block(i), pl.ds(j * units, units)]
            sem = sems.at[(2 + j) * number + i]
            keep_gu.append(pltpu.make_async_copy(source, whole.at[block(m)], sem))
    weights = pltpu.make_async_copy(w_gu, held_w, sems.at[4 * number])

    @pl.when(at == 0)
    def _():
        for copy in arrive:
            copy.start()
        weights.start()
        for copy in arrive:
            copy.wait()
        for copy in keep_d:
            copy.start()

    d_middle_all = dot_t(held_d[...], down[...])
    d_gates, d_ups = [], []
    for i in range(number):
        d_middle = d_middle_all[i * tok : (i + 1) * tok]
        gate_act, up_act = gates[i][...].astype(f32), ups[i][...].astype(f32)
        sig = sigmoid(gate_act)
        d_gates.append((d_middle * up_act * (sig * (1.0 + gate_act * (1.0 - sig)))).astype(bf16))
        d_ups.append((d_middle * (gate_act * sig)).astype(bf16))
    for step in range(steps):

        @pl.when(at == step)
        def _(step=step):
            for i in range(number):
                rows = slice(i * tok, (i + 1) * tok)
                held_gu[rows, step * part : (step + 1) * part] = d_gates[i]
                held_gu[rows, units + step * part : units + (step + 1) * part] = d_ups[i]

    @pl.when(at == steps - 1)
    def _():
        for copy in keep_gu:
            copy.start()
        weights.wait()
        for i in range(number):
            partials[i][...] = dot_t(held_gu[i * tok : (i + 1) * tok, :], held_w[...]).astype(bf16)
        for copy in keep_d + keep_gu:
            copy.wait()


def feed_call(kernel, name, pieces, masks, total, ins, in_specs, earlier, widths, blocks, held):
    number = len(pieces)
    tok, width = pieces[0].shape
    steps, part = blocks
    made, given, scratch = held
    somewhere = pl.BlockSpec(memory_space=pl.ANY)
    rows = number * tok
    first_alias = number + len(ins)

    def body(*refs):
        refs = refs[:first_alias] + refs[first_alias + len(earlier) :]
        kernel(masks, tok, steps, refs)

    return pl.pallas_call(
        body,
        grid=(steps,),
        in_specs=[somewhere] * number + in_specs + [somewhere] * len(earlier),
        out_specs=[somewhere] * len(widths)
        + [pl.BlockSpec((tok, part), lambda j: (0, j))] * made
        + [pl.BlockSpec((tok, width), lambda j: (0, 0))] * given,
        out_shape=[jax.ShapeDtypeStruct((total * tok, w), bf16) for w in widths]
        + [jax.ShapeDtypeStruct((tok, steps * part), bf16)] * made
        + [jax.ShapeDtypeStruct((tok, width), bf16)] * given,
        scratch_shapes=[pltpu.VMEM((rows, width), bf16)]
        + [pltpu.VMEM(shape, bf16) for shape in scratch]
        + [pltpu.SemaphoreType.DMA((4 * number + 1,))],
        input_output_aliases={first_alias + i: i for i in range(len(earlier))},
        compiler_params=pltpu.CompilerParams(vmem_limit_bytes=50 * 1024 * 1024),
        cost_estimate=pl.CostEstimate(
            flops=6 * rows * width * steps * part,
            bytes_accessed=6 * width * steps * part + 10 * rows * width,
            transcendentals=rows * steps * part,
        ),
        name=name,
    )(*pieces, *ins, *earlier)


def feed(pieces, masks, total, w_gu, down, earlier):
    width, units = w_gu.shape[0], w_gu.shape[1] // 2
    part = math.gcd(units, 256)
    steps = units // part
    number = len(pieces)
    rows = number * pieces[0].shape[0]
    specs = [
        pl.BlockSpec((width, part), lambda j: (0, j)),
        pl.BlockSpec((width, part), lambda j: (0, steps + j)),
    ]
    ins, scratch, given = [w_gu, w_gu], [(rows, units)], 0
    if down is not None:
        specs.append(pl.BlockSpec(memory_space=pl.ANY))
        ins, scratch, given = ins + [down], scratch + [(units, width)], number
    outs = feed_call(
        functools.partial(feed_kernel, int(down is not None)), "feed", pieces, masks, total, ins,
        specs, earlier, (width, units), (steps, part), (2 * number, given, scratch),
    )
    acts = list(zip(outs[2 : 2 + number], outs[2 + number : 2 + 2 * number], strict=True))
    return outs[:2], acts, outs[2 + 2 * number :]


def feed_down(middle_all, masks, tok, down):
    units, width = down.shape
    number = len(masks)

    def kernel(at, middle, weight, *outs):
        for i, out in enumerate(outs):

            @pl.when(pl.program_id(0) == i)
            def _(out=out):
                out[...] = dot(middle[...], weight[...]).astype(bf16)

    return pl.pallas_call(
        kernel,
        grid_spec=pltpu.PrefetchScalarGridSpec(
            num_scalar_prefetch=1,
            grid=(number,),
            in_specs=[
                pl.BlockSpec((tok, units), lambda i, at: (at[i], 0)),
                pl.BlockSpec((units, width), lambda i, at: (0, 0)),
            ],
            out_specs=[pl.BlockSpec((tok, width), lambda i, at: (0, 0))] * number,
        ),
        out_shape=[jax.ShapeDtypeStruct((tok, width), bf16)] * number,
        compiler_params=pltpu.CompilerParams(vmem_limit_bytes=40 * 1024 * 1024),
        cost_estimate=pl.CostEstimate(
            flops=2 * number * tok * units * width,
            bytes_accessed=4 * units * width,
            transcendentals=0,
        ),
        name="feed_down",
    )(jnp.array(masks, jnp.int32), middle_all, down)


def feed_back(pieces, masks, total, acts, w_gu, down, earlier):
    units, width = down.shape
    part = math.gcd(units, 256)
    steps = units // part
    number = len(pieces)
    tok = pieces[0].shape[0]
    rows = number * tok
    specs = [pl.BlockSpec((tok, part), lambda j: (0, j))] * (2 * number) + [
        pl.BlockSpec((part, width), lambda j: (j, 0)),
        pl.BlockSpec(memory_space=pl.ANY),
    ]
    ins = [gate for gate, _ in acts] + [up for _, up in acts] + [down, w_gu]
    outs = feed_call(
        feed_back_kernel, "feed_back", pieces, masks, total, ins, specs, earlier,
        (width, units, units), (steps, part), (0, number, [(rows, 2 * units), (width, 2 * units)]),
    )
    return outs[:3], outs[3:]


def owner_grad(h_all, d_act, sizes, rows, which, earlier):
    n_seq, n_hi, n_lo, n_core = sizes
    tokens, width = h_all.shape
    units = d_act.shape[1]
    cols = width // n_seq

    def kernel(h, d, *refs):
        product = t_dot(h[...], d[...]).astype(bf16)
        at = 0
        for hi in range(n_hi):
            for lo in range(n_lo):
                for core in range(n_core):
                    refs[-1][hi, core, 0, lo] = product[at : at + rows]
                    at += rows

    return pl.pallas_call(
        kernel,
        grid=(n_seq,),
        in_specs=[
            pl.BlockSpec((tokens, cols), lambda s: (0, s)),
            pl.BlockSpec((tokens, units), lambda s: (0, 0)),
        ]
        + [pl.BlockSpec(memory_space=pl.ANY)] * len(earlier),
        out_specs=pl.BlockSpec(
            (n_hi, n_core, 1, n_lo, rows, units), lambda s: (0, 0, s, 0, 0, which)
        ),
        out_shape=jax.ShapeDtypeStruct((n_hi, n_core, n_seq, n_lo, rows, 2 * units), bf16),
        input_output_aliases={2: 0} if earlier else {},
        compiler_params=pltpu.CompilerParams(vmem_limit_bytes=40 * 1024 * 1024),
        cost_estimate=pl.CostEstimate(
            flops=2 * tokens * width * units,
            bytes_accessed=2 * (tokens * width + tokens * units + width * units),
            transcendentals=0,
        ),
        name="owner_grad",
    )(h_all, d_act, *earlier)


def pack_columns(weights, count):
    rows, width = weights[0].shape
    part = width // count

    def kernel(*refs):
        for i, ref in enumerate(refs[:-1]):
            refs[-1][0, :, i * part : (i + 1) * part] = ref[...]

    return pl.pallas_call(
        kernel,
        grid=(count,),
        in_specs=[pl.BlockSpec((rows, part), lambda s: (0, s))] * len(weights),
        out_specs=pl.BlockSpec((1, rows, len(weights) * part), lambda s: (s, 0, 0)),
        out_shape=jax.ShapeDtypeStruct((count, rows, len(weights) * part), weights[0].dtype),
        name="pack_columns",
    )(*weights)


def unpack_columns(packed, number):
    count, rows, width = packed.shape
    part = width // number

    def kernel(ref, *outs):
        for i, out in enumerate(outs):
            out[...] = ref[0, :, i * part : (i + 1) * part].astype(f32)

    return pl.pallas_call(
        kernel,
        grid=(count,),
        in_specs=[pl.BlockSpec((1, rows, width), lambda s: (s, 0, 0))],
        out_specs=[pl.BlockSpec((rows, part), lambda s: (0, s))] * number,
        out_shape=[jax.ShapeDtypeStruct((rows, count * part), f32)] * number,
        name="unpack_columns",
    )(packed)


def unit_slices(sizes, unit):
    n_hi, n_lo, n_core = sizes
    return [
        (lo, (hi * n_core + core) * unit, ((hi * n_lo + lo) * n_core + core) * unit)
        for hi in range(n_hi)
        for lo in range(n_lo)
        for core in range(n_core)
    ]


def pack_units(gate, up, n_seq, sizes, unit):
    rows = gate.shape[0]
    n_hi, n_lo, n_core = sizes
    units = n_hi * n_core * unit

    def kernel(gate_ref, up_ref, out):
        for i, ref in enumerate((gate_ref, up_ref)):
            for lo, packed, plain in unit_slices(sizes, unit):
                start = i * units + packed
                out[lo, :, start : start + unit] = ref[:, plain : plain + unit]

    return pl.pallas_call(
        kernel,
        grid=(n_seq,),
        in_specs=[pl.BlockSpec((rows, units * n_lo), lambda s: (0, s))] * 2,
        out_specs=pl.BlockSpec((n_lo, rows, 2 * units), lambda s: (s, 0, 0)),
        out_shape=jax.ShapeDtypeStruct((n_seq * n_lo, rows, 2 * units), gate.dtype),
        name="pack_units",
    )(gate, up)


def unpack_units(packed, n_seq, sizes, unit):
    _, rows, width = packed.shape
    n_lo = sizes[1]
    units = width // 2

    def kernel(ref, *outs):
        for i, out in enumerate(outs):
            for lo, at, plain in unit_slices(sizes, unit):
                start = i * units + at
                out[:, plain : plain + unit] = ref[lo, :, start : start + unit].astype(f32)

    return pl.pallas_call(
        kernel,
        grid=(n_seq,),
        in_specs=[pl.BlockSpec((n_lo, rows, width), lambda s: (s, 0, 0))],
        out_specs=[pl.BlockSpec((rows, units * n_lo), lambda s: (0, s))] * 2,
        out_shape=[jax.ShapeDtypeStruct((rows, n_seq * n_lo * units), f32)] * 2,
        name="unpack_units",
    )(packed)


def finish_kernel(q_in, k_in, q_raw, k_raw, q_inv, k_inv, q_mean, k_mean, d_v, out):
    width = q_in.shape[1]
    for i, (grad, raw, inverse, mean) in enumerate(
        ((q_in, q_raw, q_inv, q_mean), (k_in, k_raw, k_inv, k_mean))
    ):
        normed = raw[...] * inverse[0]
        low = ((grad[...] - normed * mean[0]) * inverse[0]).astype(bf16)
        out[:, i * width : (i + 1) * width] = low
    out[:, 2 * width :] = d_v[...]


def row_specs(block, part):
    cols = lambda i: pl.BlockSpec((block, part), lambda b: (b, i))
    rows = lambda i: pl.BlockSpec((1, block, 1), lambda b: (i, b, 0))
    vector = pl.BlockSpec((1, part), lambda b: (0, 0))
    return cols, rows, vector


def finish(e_query, e_key, raw, inverse, means, d_value, part, block):
    length = raw.shape[0]
    cols, rows, _ = row_specs(block, part)
    return pl.pallas_call(
        finish_kernel,
        grid=(length // block,),
        in_specs=[cols(0), cols(0), cols(0), cols(1)] + [rows(0), rows(1)] * 2 + [cols(0)],
        out_specs=pl.BlockSpec((block, 3 * part), lambda b: (b, 0)),
        out_shape=jax.ShapeDtypeStruct((length, 3 * part), bf16),
        name="finish",
    )(e_query, e_key, raw, raw, inverse, inverse, means, means, d_value)


def dot(left, right):
    return jnp.dot(left, right, preferred_element_type=f32)


def dot_t(left, right):
    return lax.dot_general(left, right, (((1,), (1,)), ((), ())), preferred_element_type=f32)


def t_dot(left, right):
    return lax.dot_general(left, right, (((0,), (0,)), ((), ())), preferred_element_type=f32)


def held(block):
    return lax.optimization_barrier(block)


def rope_tables(positions, head_dim):
    half_dim = head_dim // 2
    frequency = rope_base ** (-(jnp.arange(half_dim, dtype=f32) * 2.0 / head_dim))
    angles = positions.astype(f32)[:, None] * frequency[None, :]
    cosine, sine = jnp.cos(angles), jnp.sin(angles)
    return jnp.concatenate([cosine, cosine], 1), jnp.concatenate([-sine, sine], 1)


def rms(values):
    inverse = lax.rsqrt(jnp.mean(values * values, axis=-1, keepdims=True) + norm_eps)
    return values * inverse, inverse


def rms_back(grad, normed, inverse, gain):
    scaled = grad * gain
    return (scaled - normed * jnp.mean(scaled * normed, axis=-1, keepdims=True)) * inverse


def per_device(
    tokens,
    segment_ids,
    w_query,
    w_key,
    w_value,
    w_out,
    w_gate,
    w_up,
    w_down,
    query_gain,
    key_gain,
    attn_gain,
    ff_gain,
    cotangent,
):
    inputs = tokens[0]
    tok, width = inputs.shape
    n_seq, n_hi, n_lo, n_core = (lax.axis_size(a) for a in ("seq", "zhi", "zlo", "core"))
    n_dev = n_seq * n_hi * n_lo * n_core
    seq = lax.axis_index("seq")
    heads = HEADS // n_seq
    head_dim = width // HEADS
    part = width // n_seq
    length = n_seq * tok
    d_rows = w_query.shape[0]
    ff_rows = w_down.shape[0]
    units = ff_rows * n_hi * n_core

    sizes = (n_hi, n_lo, n_core)
    seq_dims = dims_of("seq")
    lo_dims, hi_dims, core_dims = dims_of("zlo"), dims_of("zhi"), dims_of("core")
    cube_dims = seq_dims + lo_dims
    z_dims = lo_dims + hi_dims
    all_dims = core_dims + lo_dims + hi_dims + seq_dims
    z_axes = ("zhi", "zlo", "core")
    rows_of = lambda block, m: block[m * tok : (m + 1) * tok]

    pair_axes = ("zhi", "core")
    core_swap = lambda piece: swap(piece, core_dims[0])
    lo_order = [
        ((hi * n_core + core) * n_seq + s) * n_lo + lo
        for s in range(n_seq)
        for hi in range(n_hi)
        for lo in range(n_lo)
        for core in range(n_core)
    ]
    hi_order = [lo_order.index(i) for i in range(len(lo_order))]

    qkv_mine = pack_columns((w_query, w_key, w_value), n_seq)
    gains = jnp.stack([query_gain, key_gain, attn_gain, ff_gain])[None]
    gains = gather_row(after(gains, qkv_mine), core_dims + z_dims)
    gains = jnp.transpose(gains, (1, 0, 2)).reshape(1, 4 * part)
    qkv_mine = lax.all_to_all(qkv_mine, "seq", 0, 0, tiled=True).reshape(n_seq * d_rows, 3 * part)
    gu_mine = pack_units(w_gate, w_up, n_seq, sizes, ff_rows)
    qkv_mine, gains, gu_mine = tie(qkv_mine, gains, gu_mine)

    out_mine = jnp.concatenate([w_out[:, i * part : (i + 1) * part] for i in range(n_seq)], axis=0)
    w_z = Spread(jnp.concatenate([qkv_mine, out_mine], axis=1), z_dims).step()
    to_width = lambda row: jnp.pad(row, ((0, 0), (0, width - row.shape[1])))
    ids = to_width(segment_ids.astype(bf16))
    more = jnp.concatenate([ids, to_width(gains), jnp.zeros((14, width), bf16)], axis=0)
    x_spread = Spread(jnp.concatenate([inputs, more], axis=0), seq_dims).step()
    x_pieces = x_spread.whole()
    x_pieces = tie(w_z, *x_pieces)
    w_sib = [core_swap(piece) for piece in (w_z.pieces[0], *w_z.fresh())]
    early = len(w_sib)
    w_z.step()
    (w_sib,) = tie(w_z, w_sib)
    w_z = w_z.whole()
    w_sib = w_sib + [core_swap(piece) for piece in w_z[early:]]

    gu_mine = lax.all_to_all(after(gu_mine, w_z), ("seq", "zlo"), 0, 0, tiled=True)

    row_ids = jnp.concatenate([piece[tok, :tok] for piece in x_pieces]).astype(jnp.int32)
    row_ids = row_ids.reshape(length, 1)
    col_ids = jnp.stack(
        [lax.dynamic_slice(row_ids, ((seq ^ m) * tok, 0), (tok, 1)) for m in range(n_seq)]
    ).reshape(n_seq, 1, tok)
    tables = rope_tables(jnp.arange(length, dtype=jnp.int32), head_dim)
    all_gains = jnp.concatenate([piece[tok + 1 : tok + 2, : 4 * part] for piece in x_pieces], axis=0)
    all_gains = jnp.concatenate(
        [lax.dynamic_slice(all_gains, (seq ^ m, 0), (1, 4 * part)) for m in range(n_seq)], axis=0
    ).reshape(n_seq, 4, part)
    all_gains = jnp.transpose(all_gains, (1, 0, 2)).reshape(4, width).astype(f32)
    my_gains = gains.reshape(4, 1, part).astype(f32)
    qk_gains = (my_gains[0], my_gains[1])
    gain_attn, gain_ff = all_gains[2], all_gains[3]

    raw, squares, x_all, w_qkv, out_weight = project(
        x_pieces,
        [piece.reshape(n_seq, d_rows, 4 * part) for piece in w_z + w_sib],
        block_starts(
            n_seq,
            d_rows,
            z_dims + core_dims,
            z_axes,
            lambda s, hi, lo, core: ((s * n_hi + hi) * n_lo + lo) * n_core + core,
        ),
        block_starts(
            1,
            d_rows,
            z_dims + core_dims,
            z_axes,
            lambda block, hi, lo, core: (hi * n_lo + lo) * n_core + core,
        ),
        tok,
        part,
    )
    squares = squares.reshape(2, n_seq, tok)
    squares = sum_all(jnp.transpose(squares, (1, 0, 2)), seq_dims)
    inverse = lax.rsqrt(jnp.transpose(squares, (1, 0, 2)).reshape(2, length, 1) / width + norm_eps)
    inverse, gu_mine = tie(inverse, gu_mine)
    w_gu = lax.all_gather(gu_mine, pair_axes, axis=0, tiled=True)
    down = lax.all_gather(after(w_down, gu_mine), pair_axes, axis=0, tiled=True)

    context = (seq.astype(jnp.int32).reshape(1), raw, inverse, qk_gains, tables, (row_ids, col_ids))
    attended, attn_low, log_total = attend(context, heads, tok)
    branch = Collect(
        [held(dot(rows_of(attn_low, m), out_weight).astype(bf16)) for m in range(n_seq)], seq_dims
    ).whole()
    branch_norm, branch_inv = rms(branch)
    hidden = inputs.astype(f32) + branch_norm * gain_attn
    hidden_low = hidden.astype(bf16)

    w_gu = regroup(w_gu.reshape(-1, d_rows, 2 * units), lo_order)
    total = 1 << len(cube_dims)
    by_bits = lambda size: [
        m for m in range(total) if bin(m).count("1") == size or (size == 1 and m == 0)
    ]
    fours = lambda masks: [masks[i : i + 4] for i in range(0, len(masks), 4)]
    groups = [masks for size in range(1, len(cube_dims) + 1) for masks in fours(by_bits(size))]
    light = total == 8
    h_spread = Spread(hidden_low, cube_dims, spare_last=light).step()
    acts, partials, kept, late = {}, {}, (), []
    for i, masks in enumerate([[0, 1, 2, 3], [4, 5, 6], [7]] if light else groups):
        while any(m not in h_spread.pieces for m in masks):
            h_spread.step()
        pieces = [h_spread.pieces[m] for m in masks]
        kept, act, sums = feed(pieces, masks, total, w_gu, down if i else None, kept)
        acts.update(zip(masks, act, strict=True))
        late += [] if i else masks
        partials.update(zip(masks if i else [], sums, strict=True))
        if light and i == 0:
            h_spread.pieces[4] = after(h_spread.pieces[4], act)
    h_all, middle_all = kept
    partials.update(zip(late, feed_down(middle_all, late, tok, down), strict=True))
    partials = [partials[m] for m in range(total)]
    ff_raw = Collect(partials, cube_dims).whole()
    ff_norm, ff_inv = rms(ff_raw)
    mixed = (hidden + ff_norm * gain_ff).astype(bf16)

    grad_output = cotangent[0].astype(f32)
    grad_ff_gain = jnp.sum(grad_output * ff_norm, axis=0)
    d_ff = rms_back(grad_output, ff_norm, ff_inv, gain_ff).astype(bf16)
    d_spread = Spread(d_ff, cube_dims).step()
    partials, kept = {}, ()
    for masks in groups:
        while any(m not in d_spread.pieces for m in masks):
            d_spread.step()
        pieces = [d_spread.pieces[m] for m in masks]
        act = [acts[m] for m in masks]
        kept, sums = feed_back(pieces, masks, total, act, w_gu, down, kept)
        partials.update(zip(masks, sums, strict=True))
    d_ff_all, d_gate_all, d_up_all = kept
    partials = [partials[m] for m in range(total)]
    d_hidden = Collect(partials, cube_dims).step()

    owned = lambda grad: lax.psum_scatter(grad, pair_axes, scatter_dimension=0, tiled=True)
    order = (n_seq, n_hi, n_lo, n_core)
    grad_gu = owner_grad(h_all, after(d_gate_all, partials), order, d_rows, 0, [])
    (grad_gu,) = tie(d_hidden, grad_gu)
    d_hidden.step()
    grad_gu = owner_grad(h_all, after(d_up_all, grad_gu), order, d_rows, 1, [grad_gu])
    (grad_gu,) = tie(d_hidden, grad_gu)
    grad_gu = owned(grad_gu.reshape(-1, d_rows, 2 * units))
    d_hidden = d_hidden.whole()

    d_hidden = grad_output + d_hidden
    grad_attn_gain = jnp.sum(d_hidden * branch_norm, axis=0)
    d_branch = rms_back(d_hidden, branch_norm, branch_inv, gain_attn).astype(bf16)
    d_branch_pieces = Spread(d_branch, seq_dims).whole()
    grad_down = t_dot(middle_all, after(d_ff_all, d_branch)).astype(bf16)
    d_branch_pieces, grad_down = tie(d_branch_pieces, grad_down)
    grad_down = owned(grad_down).astype(f32)
    d_attended = jnp.concatenate(
        [dot_t(piece, out_weight).astype(bf16) for piece in d_branch_pieces], axis=0
    )
    e_query, e_key, d_value, q_sum, k_sum, grad_query_gain, grad_key_gain = attend_back(
        context, d_attended, attended, log_total, heads, tok
    )
    means = jnp.stack([q_sum[0], k_sum[0]]).reshape(2, n_seq, tok)
    means = sum_all(jnp.transpose(means, (1, 0, 2)), seq_dims)
    means = jnp.transpose(means, (1, 0, 2)).reshape(2, length, 1) / width

    n_z = n_hi * n_lo
    z_blocks = lambda grad: take_blocks(
        jnp.transpose(
            grad.reshape(n_seq, n_hi, n_lo, n_core, d_rows, grad.shape[1]), (1, 2, 3, 0, 4, 5)
        ),
        z_dims + core_dims,
        z_axes,
    )
    d_branch_all = jnp.concatenate(d_branch_pieces, axis=0)
    grad_out = t_dot(attn_low, after(d_branch_all, d_value)).astype(bf16)
    grad_out = jnp.concatenate([grad_out[:, i * part : (i + 1) * part] for i in range(n_seq)], axis=0)
    means, grad_out = tie(means, grad_out)
    d_qkv = finish(e_query, e_key, raw, inverse, means, d_value, part, tok)
    grad_qkv = t_dot(x_all, d_qkv).astype(bf16)
    both = [
        jnp.concatenate([a, b], axis=-1)
        for a, b in zip(z_blocks(grad_qkv), z_blocks(grad_out), strict=True)
    ]
    theirs = [core_swap(piece) for piece in both[n_z:]]
    low_rows, theirs = tie(d_qkv, theirs)
    input_grad = Collect(
        [held(dot_t(rows_of(low_rows, m), w_qkv).astype(bf16)) for m in range(n_seq)], seq_dims
    )
    both = [
        add_low(a, b).reshape(-1, 4 * part) for a, b in zip(both[:n_z], theirs, strict=True)
    ]
    both = Collect(both, z_dims).step()
    input_grad.step()
    full_row = lambda cols: lax.dynamic_update_slice(jnp.zeros((width,), f32), cols, (seq * part,))
    rows = jnp.stack(
        [full_row(grad_query_gain[0]), full_row(grad_key_gain[0]), grad_attn_gain, grad_ff_gain]
    )
    rows = jnp.transpose(rows.reshape(4, n_dev, d_rows), (1, 0, 2))
    rows = lax.all_to_all(after(rows, low_rows), ("seq",) + z_axes, 0, 0, tiled=True)
    rows, grad_gu = tie(both, input_grad, rows, grad_gu)
    grad_gu = grad_gu.reshape(n_seq * n_lo, d_rows, 2 * units)
    grad_gu = lax.all_to_all(grad_gu, ("seq", "zlo"), 0, 0, tiled=True)
    rows = jnp.sum(rows, axis=0)
    both.step()
    input_grad.step()
    grad_gu, grad_down, rows = tie(both, input_grad, grad_gu, grad_down, rows)
    both = both.whole().astype(bf16).reshape(n_seq, d_rows, 4 * part)
    grad_qkv, grad_out = both[..., : 3 * part], both[..., 3 * part :]
    grad_qkv = lax.all_to_all(grad_qkv, "seq", 0, 0, tiled=True)
    input_grad = d_hidden + input_grad.whole()
    grad_out = jnp.concatenate([grad_out[i] for i in range(n_seq)], axis=1).astype(f32)
    grad_gate, grad_up = unpack_units(grad_gu, n_seq, sizes, ff_rows)
    grad_query, grad_key, grad_value = unpack_columns(grad_qkv, 3)

    return (
        mixed[None],
        input_grad[None],
        grad_query,
        grad_key,
        grad_value,
        grad_out,
        grad_gate,
        grad_up,
        grad_down,
        rows[0],
        rows[1],
        rows[2],
        rows[3],
    )


def solution(mesh):
    n_seq, n_row = mesh.shape["seq"], mesh.shape["row"]
    n_core = 2
    n_lo = 2
    n_hi = n_row // (n_core * n_lo)
    cut = Mesh(
        mesh.devices.reshape(n_seq, n_hi, n_lo, n_core), ("seq", "zhi", "zlo", "core")
    )
    row = ("zhi", "zlo", "core")
    every = ("seq",) + row
    acts = P(row, "seq", None)
    matrix = P(every, None)
    vector = P(every)
    return jax.shard_map(
        per_device,
        mesh=cut,
        in_specs=(acts, P(row, "seq")) + (matrix,) * 7 + (vector,) * 4 + (acts,),
        out_specs=(acts, acts) + (matrix,) * 7 + (vector,) * 4,
        check_vma=False,
    )
```

```python
import functools
import math

import jax
import jax.numpy as jnp
from jax import lax
from jax.experimental import pallas as pl
from jax.experimental.pallas import tpu as pltpu
from jax.sharding import Mesh
from jax.sharding import PartitionSpec as P

HEADS = 16

rope_base = 500000.0
norm_eps = 1e-06
masked_score = -1e30

bf16 = jnp.bfloat16
f32 = jnp.float32


def dims_of(axis):
    count = lax.axis_size(axis)
    return [(axis, 1 << bit) for bit in range(count.bit_length() - 1)]


def swap(block, dim):
    axis, mask = dim
    return lax.ppermute(block, axis, [(i, i ^ mask) for i in range(lax.axis_size(axis))])


def partner_index(dims, which):
    masks = {}
    for bit, (axis, mask) in enumerate(dims):
        if which >> bit & 1:
            masks[axis] = masks.get(axis, 0) | mask
    return masks


def column_cuts(width, count):
    tiles = width // 128
    return [round(tiles * i / count) * 128 for i in range(count + 1)]


def column_parts(block, count):
    cuts = column_cuts(block.shape[1], count)
    return [block[:, cuts[i] : cuts[i + 1]] for i in range(count)]


def route(which, count):
    bits = [i for i in range(count) if which >> i & 1]
    if len(bits) == 1:
        return bits[0]
    return bits[0] if bits[1] - bits[0] == 1 else bits[1]


def by_size(count):
    return sorted(range(1, 1 << count), key=lambda m: bin(m).count("1"))


class Spread:
    def __init__(self, block, dims, spare_last=False):
        self.dims, self.size, self.pieces, self.new = dims, 0, {0: block}, [0]
        self.spare_last = spare_last and len(dims) == 3

    def light_step(self):
        x, y, _ = self.dims
        half = lambda m, i: column_parts(self.pieces[m], 2)[i]
        if self.size == 2:
            self.new = [3]
            self.pieces[3] = jnp.concatenate([swap(half(2, 0), x), swap(half(1, 1), y)], axis=1)
        elif self.size == 3:
            self.new = [5, 6]
            self.pieces[5], self.pieces[6] = swap(self.pieces[4], x), swap(self.pieces[4], y)
        else:
            self.new = [7]
            self.pieces[7] = jnp.concatenate([swap(half(6, 0), x), swap(half(5, 1), y)], axis=1)

    def step(self):
        self.size += 1
        count = len(self.dims)
        if self.spare_last and self.size > 1:
            self.light_step()
            return self
        self.new = [m for m in by_size(count) if bin(m).count("1") == self.size]
        for which in self.new:
            if self.size == count and count > 1:
                parts = [
                    swap(column_parts(self.pieces[which ^ (1 << i)], count)[i], self.dims[i])
                    for i in range(count)
                ]
                self.pieces[which] = jnp.concatenate(parts, axis=1)
            else:
                via = route(which, count)
                self.pieces[which] = swap(self.pieces[which ^ (1 << via)], self.dims[via])
        return self

    def fresh(self):
        return [self.pieces[m] for m in self.new]

    def renew(self, values):
        self.pieces.update(zip(self.new, values, strict=True))

    def whole(self):
        while self.size < len(self.dims):
            self.step()
        return [self.pieces[m] for m in range(1 << len(self.dims))]


class Collect:
    def __init__(self, pieces, dims):
        self.dims, self.size, self.pieces = dims, len(dims), list(pieces)
        self.got, self.new = {m: [] for m in range(len(self.pieces))}, []
        self.sums = None

    def ready(self):
        masks = [m for m in by_size(len(self.dims)) if bin(m).count("1") == self.size]
        self.sums = {m: self.total(m) for m in masks}
        return self

    def step(self):
        count = len(self.dims)
        if self.sums is None:
            self.ready()
        sums, self.sums, self.new = self.sums, None, []
        for which, total in sums.items():
            if self.size == count and count > 1:
                for i, cols in enumerate(column_parts(total, count)):
                    self.keep(which ^ (1 << i), i, swap(cols, self.dims[i]))
            else:
                via = route(which, count)
                self.keep(which ^ (1 << via), None, swap(total, self.dims[via]))
        self.size -= 1
        return self

    def keep(self, which, part, arrived):
        self.new.append((which, len(self.got[which])))
        self.got[which].append((part, arrived))

    def total(self, which):
        if not self.got[which]:
            return self.pieces[which]
        count = len(self.dims)
        total = self.pieces[which].astype(f32)
        for part, arrived in self.got[which]:
            if part is None:
                total = total + arrived.astype(f32)
            else:
                cols = column_parts(total, count)
                cols[part] = cols[part] + arrived.astype(f32)
                total = jnp.concatenate(cols, axis=1)
        return total.astype(bf16)

    def fresh(self):
        if self.sums is not None:
            return list(self.sums.values())
        return [self.got[which][i][1] for which, i in self.new]

    def renew(self, values):
        if self.sums is not None:
            self.sums = dict(zip(self.sums, values, strict=True))
            return
        for (which, i), value in zip(self.new, values, strict=True):
            self.got[which][i] = (self.got[which][i][0], value)

    def whole(self):
        while self.size > 0:
            self.step()
        total = self.pieces[0].astype(f32)
        for _, arrived in self.got[0]:
            total = total + arrived.astype(f32)
        return total


def tie(*items):
    steps = (Spread, Collect)
    values = [item.fresh() if isinstance(item, steps) else item for item in items]
    values = lax.optimization_barrier(values)
    rest = []
    for item, value in zip(items, values, strict=True):
        if isinstance(item, steps):
            item.renew(value)
        else:
            rest.append(value)
    return rest


def sum_all(table, dims):
    for bit, dim in enumerate(dims):
        there = swap(table, dim)
        order = [m ^ (1 << bit) for m in range(table.shape[0])]
        table = table + jnp.stack([there[m] for m in order])
    return table


def after(block, *earlier):
    return lax.optimization_barrier((block, earlier))[0]


def block_starts(blocks, rows, dims, axes, order):
    starts = []
    for m in range(1 << len(dims)):
        masks = partner_index(dims, m)
        at = [lax.axis_index(a) ^ masks.get(a, 0) for a in axes]
        starts += [order(block, *at) * rows for block in range(blocks)]
    return jnp.stack(starts).astype(jnp.int32)


def project(x_pieces, w_pieces, starts, out_starts, tok, part):
    n_x, n_w = len(x_pieces), len(w_pieces)
    width = x_pieces[0].shape[1]
    blocks, rows, _ = w_pieces[0].shape
    length = n_x * tok
    number = n_w * blocks

    def kernel(table, out_table, *refs):
        xs, ws = refs[:n_x], refs[n_x : n_x + n_w]
        raw, squares, x_out, w_out, o_out, x_all, w_all, o_all, sems = refs[n_x + n_w :]
        at = pl.program_id(0)
        arrive, later = [], []
        for i in range(n_x):
            source, target = xs[i].at[pl.ds(0, tok)], x_all.at[pl.ds(i * tok, tok)]
            arrive.append(pltpu.make_async_copy(source, target, sems.at[i]))
        for i in range(number):
            piece, block = ws[i // blocks], i % blocks
            here = pl.ds(pl.multiple_of(table[i], rows), rows)
            source = piece.at[block, :, pl.ds(0, 3 * part)]
            arrive.append(pltpu.make_async_copy(source, w_all.at[here], sems.at[n_x + i]))
            here = pl.ds(pl.multiple_of(out_table[i // blocks], rows), rows)
            source = piece.at[block, :, pl.ds(3 * part, part)]
            target = o_all.at[here, pl.ds(block * part, part)]
            later.append(pltpu.make_async_copy(source, target, sems.at[n_x + number + i]))
        sem = n_x + 2 * number
        keep = [
            pltpu.make_async_copy(x_all, x_out, sems.at[sem]),
            pltpu.make_async_copy(w_all, w_out, sems.at[sem + 1]),
        ]
        keep_out = pltpu.make_async_copy(o_all, o_out, sems.at[sem + 2])

        @pl.when(at == 0)
        def _():
            for copy in arrive + later:
                copy.start()
            for copy in arrive:
                copy.wait()
            for copy in keep:
                copy.start()

        for step in range(3):

            @pl.when(at == step)
            def _(step=step):
                product = dot(x_all[...], w_all[:, step * part : (step + 1) * part])
                raw[...] = product
                if step < 2:
                    squares[0] = jnp.sum(product * product, axis=-1, keepdims=True)
                if step == 0:
                    for copy in later:
                        copy.wait()
                    keep_out.start()

        @pl.when(at == 2)
        def _():
            for copy in keep + [keep_out]:
                copy.wait()

    somewhere = pl.BlockSpec(memory_space=pl.ANY)
    scalars = pl.BlockSpec(memory_space=pltpu.SMEM)
    return pl.pallas_call(
        kernel,
        grid=(3,),
        in_specs=[scalars] * 2 + [somewhere] * (n_x + n_w),
        out_specs=[
            pl.BlockSpec((length, part), lambda j: (0, j)),
            pl.BlockSpec((1, length, 1), lambda j: (jnp.minimum(j, 1), 0, 0)),
            somewhere,
            somewhere,
            somewhere,
        ],
        out_shape=[
            jax.ShapeDtypeStruct((length, 3 * part), f32),
            jax.ShapeDtypeStruct((2, length, 1), f32),
            jax.ShapeDtypeStruct((length, width), bf16),
            jax.ShapeDtypeStruct((width, 3 * part), bf16),
            jax.ShapeDtypeStruct((n_w * rows, blocks * part), bf16),
        ],
        scratch_shapes=[
            pltpu.VMEM((length, width), bf16),
            pltpu.VMEM((width, 3 * part), bf16),
            pltpu.VMEM((n_w * rows, blocks * part), bf16),
            pltpu.SemaphoreType.DMA((n_x + 2 * number + 3,)),
        ],
        compiler_params=pltpu.CompilerParams(vmem_limit_bytes=40 * 1024 * 1024),
        cost_estimate=pl.CostEstimate(
            flops=6 * length * width * part, bytes_accessed=20 * length * part, transcendentals=0
        ),
        name="project",
    )(starts, out_starts, *x_pieces, *w_pieces)


def regroup(blocks, order):
    number, rows, width = blocks.shape

    def kernel(ref, out, sems):
        copies = [
            pltpu.make_async_copy(ref.at[at], out.at[pl.ds(i * rows, rows)], sems.at[i])
            for i, at in enumerate(order)
        ]
        for copy in copies:
            copy.start()
        for copy in copies:
            copy.wait()

    return pl.pallas_call(
        kernel,
        in_specs=[pl.BlockSpec(memory_space=pltpu.HBM)],
        out_specs=pl.BlockSpec(memory_space=pltpu.VMEM),
        out_shape=jax.ShapeDtypeStruct((number * rows, width), blocks.dtype),
        scratch_shapes=[pltpu.SemaphoreType.DMA((number,))],
        compiler_params=pltpu.CompilerParams(vmem_limit_bytes=24 * 1024 * 1024),
        name="regroup",
    )(blocks)


def take_blocks(whole, dims, axes):
    shape = whole.shape[len(axes) :]
    pieces = []
    for m in range(1 << len(dims)):
        masks = partner_index(dims, m)
        at = tuple(lax.axis_index(a) ^ masks.get(a, 0) for a in axes)
        piece = lax.dynamic_slice(whole, at + (0,) * len(shape), (1,) * len(axes) + shape)
        pieces.append(piece.reshape(shape))
    return pieces


def add_low(kept, arrived):
    return (kept.astype(f32) + arrived.astype(f32)).astype(bf16)


def gather_row(row, dims):
    for axis, mask in dims:
        there = swap(row, (axis, mask))
        low = (lax.axis_index(axis) & mask) == 0
        row = jnp.concatenate([jnp.where(low, row, there), jnp.where(low, there, row)], axis=0)
    return row


def turned(raw, inverse, gain, cosine, sine):
    scaled = raw * inverse * gain
    return scaled * cosine + pltpu.roll(scaled, scaled.shape[1] // 2, 1) * sine


def turned_back(grad, raw, inverse, gain, cosine, sine):
    back = grad * cosine - pltpu.roll(grad, grad.shape[1] // 2, 1) * sine
    product = back * (raw * inverse)
    return back * gain, jnp.sum(product * gain, -1, keepdims=True), jnp.sum(product, 0, keepdims=True)


def block_scores(scale, last, a, j, k, q, key_ids, query_ids):
    scores = dot_t(k, q) * scale
    allowed = None
    if j == 0 or a == last:
        allowed = key_ids == query_ids
    if j == a:
        shape = scores.shape
        causal = lax.broadcasted_iota(jnp.int32, shape, 0) <= lax.broadcasted_iota(jnp.int32, shape, 1)
        allowed = causal if allowed is None else allowed & causal
    return scores if allowed is None else jnp.where(allowed, scores, masked_score)


def forward_kernel(
    scale, count, tok, place, q_raw, k_raw, v_raw, q_inv, k_inv, q_gain, k_gain, cosine, sine,
    row_ids, col_ids, out, low, log_total, k_all, v_across,
):
    rows = lambda j: pl.ds(pl.multiple_of((place[0] ^ j) * tok, tok), tok)
    cols = lambda j: slice(j * tok, (j + 1) * tok)
    for a in range(count):
        here = rows(a)
        table = (cosine[cols(a), :], sine[cols(a), :])
        k_all[cols(a), :] = turned(k_raw[here, :], k_inv[0, here, :], k_gain[...], *table).astype(bf16)
        v_across[:, cols(a)] = v_raw[here, :].T.astype(bf16)
        q = turned(q_raw[here, :], q_inv[0, here, :], q_gain[...], *table).astype(bf16)
        scores = [
            block_scores(scale, count - 1, a, j, k_all[cols(j), :], q, row_ids[rows(j), :], col_ids[a])
            for j in range(a + 1)
        ]
        top = jnp.max(functools.reduce(jnp.maximum, scores), axis=0, keepdims=True)
        expo = [jnp.exp2(block - top) for block in scores]
        total = jnp.sum(functools.reduce(jnp.add, expo), axis=0, keepdims=True)
        parts = [dot(v_across[:, cols(j)], expo[j].astype(bf16)) for j in range(a + 1)]
        attended = (functools.reduce(jnp.add, parts) * (1.0 / total)).T
        out[here, :] = attended
        low[here, :] = attended.astype(bf16)
        log_total[0, place[0] ^ a] = top + jnp.log2(total)


def backward_kernel(
    scale, plain_scale, count, tok, place, q_raw, k_raw, v_raw, q_inv, k_inv, q_gain, k_gain,
    cosine, sine, row_ids, col_ids, d_out, out, log_total,
    e_q, e_k, d_v, q_sum, k_sum, q_gain_grad, k_gain_grad, k_all, k_across, v_all, d_k_all, d_v_all,
):
    rows = lambda j: pl.ds(pl.multiple_of((place[0] ^ j) * tok, tok), tok)
    cols = lambda j: slice(j * tok, (j + 1) * tok)
    q_gain_grad[...] = jnp.zeros_like(q_gain_grad)

    @pl.when(pl.program_id(0) == 0)
    def _():
        q_sum[...] = jnp.zeros_like(q_sum)
        k_sum[...] = jnp.zeros_like(k_sum)

    for a in range(count):
        here = rows(a)
        table = (cosine[cols(a), :], sine[cols(a), :])
        k = turned(k_raw[here, :], k_inv[0, here, :], k_gain[...], *table)
        k_all[cols(a), :] = k.astype(bf16)
        k_across[:, cols(a)] = k.T.astype(bf16)
        v_all[cols(a), :] = v_raw[here, :].astype(bf16)
        q_row, inverse = q_raw[here, :], q_inv[0, here, :]
        q = turned(q_row, inverse, q_gain[...], *table).astype(bf16)
        d_blk = d_out[here, :]
        row_dot = jnp.sum(d_blk.astype(f32) * out[here, :], axis=-1, keepdims=True)
        row_dot = jnp.broadcast_to(row_dot, q_row.shape).T[0:1, :]
        log_row = log_total[0, place[0] ^ a]
        d_q = []
        for j in range(a + 1):
            scores = block_scores(
                scale, count - 1, a, j, k_all[cols(j), :], q, row_ids[rows(j), :], col_ids[a]
            )
            probability = jnp.exp2(scores - log_row)
            d_prob = dot_t(v_all[cols(j), :], d_blk)
            d_scores = (probability * (d_prob - row_dot)).astype(bf16)
            d_q.append(dot(k_across[:, cols(j)], d_scores))
            d_k = dot(d_scores, q)
            d_v_part = dot(probability.astype(bf16), d_blk)
            if j == a:
                d_k_all[cols(j), :] = d_k
                d_v_all[cols(j), :] = d_v_part
            else:
                d_k_all[cols(j), :] += d_k
                d_v_all[cols(j), :] += d_v_part
        e_q[here, :], row_sum, gain_grad = turned_back(
            functools.reduce(jnp.add, d_q).T * plain_scale, q_row, inverse, q_gain[...], *table
        )
        q_sum[0, here, :] += row_sum
        q_gain_grad[...] += gain_grad
    k_gain_grad[...] = jnp.zeros_like(k_gain_grad)
    for j in range(count):
        here = rows(j)
        e_k[here, :], row_sum, gain_grad = turned_back(
            d_k_all[cols(j), :] * plain_scale, k_raw[here, :], k_inv[0, here, :],
            k_gain[...], cosine[cols(j), :], sine[cols(j), :],
        )
        k_sum[0, here, :] += row_sum
        k_gain_grad[...] += gain_grad
        d_v[here, :] = d_v_all[cols(j), :].astype(bf16)


def attention_specs(tokens, block, heads, head_dim):
    head = lambda i: pl.BlockSpec((tokens, head_dim), lambda h, s: (0, i * heads + h))
    whole = lambda shape: pl.BlockSpec(shape, lambda h, s: (0,) * len(shape))
    vector = pl.BlockSpec((1, head_dim), lambda h, s: (0, h))
    inverse = lambda i: pl.BlockSpec((1, tokens, 1), lambda h, s: (i, 0, 0))
    inputs = [head(0), head(1), head(2), inverse(0), inverse(1), vector, vector]
    inputs += [whole((tokens, head_dim))] * 2
    inputs += [whole((tokens, 1)), whole((tokens // block, 1, block))]
    logs = pl.BlockSpec((1, tokens // block, 1, block), lambda h, s: (h, 0, 0, 0))
    return inputs, head(0), logs, vector


def attend(context, heads, block):
    place, raw, inverse, gains, tables, ids = context
    tokens, width = raw.shape[0], raw.shape[1] // 3
    head_dim = width // heads
    inputs, head, logs, _ = attention_specs(tokens, block, heads, head_dim)
    return pl.pallas_call(
        functools.partial(forward_kernel, head_dim**-0.5 * math.log2(math.e), tokens // block, block),
        grid_spec=pltpu.PrefetchScalarGridSpec(
            num_scalar_prefetch=1,
            grid=(heads,),
            in_specs=inputs,
            out_specs=[head, head, logs],
            scratch_shapes=[
                pltpu.VMEM((tokens, head_dim), bf16),
                pltpu.VMEM((head_dim, tokens), bf16),
            ],
        ),
        out_shape=[
            jax.ShapeDtypeStruct((tokens, width), f32),
            jax.ShapeDtypeStruct((tokens, width), bf16),
            jax.ShapeDtypeStruct((heads, tokens // block, 1, block), f32),
        ],
        compiler_params=pltpu.CompilerParams(vmem_limit_bytes=40 * 1024 * 1024),
        cost_estimate=pl.CostEstimate(
            flops=2 * tokens * tokens * width,
            bytes_accessed=18 * tokens * width,
            transcendentals=heads * tokens * tokens // 2,
        ),
        name="attend",
    )(place, raw, raw, raw, inverse, inverse, *gains, *tables, *ids)


def attend_back(context, d_out, out, log_total, heads, block):
    place, raw, inverse, gains, tables, ids = context
    tokens, width = raw.shape[0], raw.shape[1] // 3
    head_dim = width // heads
    inputs, head, logs, vector = attention_specs(tokens, block, heads, head_dim)
    sums = pl.BlockSpec((1, tokens, 1), lambda h, s: (0, 0, 0))
    scale = head_dim**-0.5
    return pl.pallas_call(
        functools.partial(
            backward_kernel, scale * math.log2(math.e), scale, tokens // block, block
        ),
        grid_spec=pltpu.PrefetchScalarGridSpec(
            num_scalar_prefetch=1,
            grid=(heads,),
            in_specs=inputs + [head, head, logs],
            out_specs=[head, head, head, sums, sums, vector, vector],
            scratch_shapes=[
                pltpu.VMEM((tokens, head_dim), bf16),
                pltpu.VMEM((head_dim, tokens), bf16),
                pltpu.VMEM((tokens, head_dim), bf16),
                pltpu.VMEM((tokens, head_dim), f32),
                pltpu.VMEM((tokens, head_dim), f32),
            ],
        ),
        out_shape=[
            jax.ShapeDtypeStruct((tokens, width), f32),
            jax.ShapeDtypeStruct((tokens, width), f32),
            jax.ShapeDtypeStruct((tokens, width), bf16),
        ]
        + [jax.ShapeDtypeStruct((1, tokens, 1), f32)] * 2
        + [jax.ShapeDtypeStruct((1, width), f32)] * 2,
        compiler_params=pltpu.CompilerParams(vmem_limit_bytes=40 * 1024 * 1024),
        cost_estimate=pl.CostEstimate(
            flops=5 * tokens * tokens * width,
            bytes_accessed=30 * tokens * width,
            transcendentals=heads * tokens * tokens // 2,
        ),
        name="attend_back",
    )(place, raw, raw, raw, inverse, inverse, *gains, *tables, *ids, d_out, out, log_total)


def sigmoid(values):
    return 1.0 / (1.0 + jnp.exp(-values))


def feed_kernel(masks, tok, steps, refs):
    number = len(masks)
    pieces, refs = refs[:number], refs[number:]
    w_gate, w_up, h_all, middle_all, refs = *refs[:4], refs[4:]
    slopes, silus, refs = refs[:number], refs[number : 2 * number], refs[2 * number :]
    held_h, held_middle, sems = refs
    at = pl.program_id(0)
    part = slopes[0].shape[1]
    block = lambda i: pl.ds(i * tok, tok)
    copies = lambda held, whole, first: [
        pltpu.make_async_copy(held.at[block(i)], whole.at[block(m)], sems.at[first + i])
        for i, m in enumerate(masks)
    ]
    arrive = [
        pltpu.make_async_copy(pieces[i], held_h.at[block(i)], sems.at[i]) for i in range(number)
    ]
    keep_h, keep_middle = copies(held_h, h_all, number), copies(held_middle, middle_all, 2 * number)

    @pl.when(at == 0)
    def _():
        for copy in arrive:
            copy.start()
        for copy in arrive:
            copy.wait()
        for copy in keep_h:
            copy.start()

    gate_act = dot(held_h[...], w_gate[...])
    up_act = dot(held_h[...], w_up[...])
    sig = sigmoid(gate_act)
    silu = gate_act * sig
    middle = (silu * up_act).astype(bf16)
    slope = up_act * (sig + silu * (1.0 - sig))
    for i in range(number):
        slopes[i][...] = slope[i * tok : (i + 1) * tok].astype(bf16)
        silus[i][...] = silu[i * tok : (i + 1) * tok].astype(bf16)
    for step in range(steps):

        @pl.when(at == step)
        def _(step=step):
            held_middle[:, step * part : (step + 1) * part] = middle

    @pl.when(at == steps - 1)
    def _():
        for copy in keep_middle:
            copy.start()
        for copy in keep_h + keep_middle:
            copy.wait()


def feed_back_kernel(masks, tok, steps, refs):
    number = len(masks)
    pieces, refs = refs[:number], refs[number:]
    slopes, silus, refs = refs[:number], refs[number : 2 * number], refs[2 * number :]
    down, w_gu, d_ff_all, d_gate_all, d_up_all = refs[:5]
    partials, (held_d, held_gu, held_w, sems) = refs[5 : 5 + number], refs[5 + number :]
    at = pl.program_id(0)
    part = slopes[0].shape[1]
    units = steps * part
    block = lambda i: pl.ds(i * tok, tok)
    arrive, keep_d, keep_gu = [], [], []
    for i, m in enumerate(masks):
        arrive.append(pltpu.make_async_copy(pieces[i], held_d.at[block(i)], sems.at[i]))
        keep_d.append(
            pltpu.make_async_copy(held_d.at[block(i)], d_ff_all.at[block(m)], sems.at[number + i])
        )
        for j, whole in enumerate((d_gate_all, d_up_all)):
            source = held_gu.at[block(i), pl.ds(j * units, units)]
            sem = sems.at[(2 + j) * number + i]
            keep_gu.append(pltpu.make_async_copy(source, whole.at[block(m)], sem))
    weights = pltpu.make_async_copy(w_gu, held_w, sems.at[4 * number])

    @pl.when(at == 0)
    def _():
        for copy in arrive:
            copy.start()
        weights.start()
        for copy in arrive:
            copy.wait()
        for copy in keep_d:
            copy.start()

    d_middle_all = dot_t(held_d[...], down[...])
    d_gates, d_ups = [], []
    for i in range(number):
        d_middle = d_middle_all[i * tok : (i + 1) * tok]
        d_gates.append((d_middle * slopes[i][...].astype(f32)).astype(bf16))
        d_ups.append((d_middle * silus[i][...].astype(f32)).astype(bf16))
    for step in range(steps):

        @pl.when(at == step)
        def _(step=step):
            for i in range(number):
                rows = slice(i * tok, (i + 1) * tok)
                held_gu[rows, step * part : (step + 1) * part] = d_gates[i]
                held_gu[rows, units + step * part : units + (step + 1) * part] = d_ups[i]

    @pl.when(at == steps - 1)
    def _():
        for copy in keep_gu:
            copy.start()
        weights.wait()
        width = held_d.shape[1]
        cols = math.gcd(width, 512)
        for n in range(0, width, cols):
            product = dot_t(held_gu[...], held_w[n : n + cols, :]).astype(bf16)
            for i, out in enumerate(partials):
                out[:, n : n + cols] = product[i * tok : (i + 1) * tok]
        for copy in keep_d + keep_gu:
            copy.wait()


def feed_call(kernel, name, pieces, masks, total, ins, in_specs, earlier, widths, blocks, held):
    number = len(pieces)
    tok, width = pieces[0].shape
    steps, part = blocks
    made, given, scratch = held
    somewhere = pl.BlockSpec(memory_space=pl.ANY)
    rows = number * tok
    first_alias = number + len(ins)

    def body(*refs):
        refs = refs[:first_alias] + refs[first_alias + len(earlier) :]
        kernel(masks, tok, steps, refs)

    return pl.pallas_call(
        body,
        grid=(steps,),
        in_specs=[somewhere] * number + in_specs + [somewhere] * len(earlier),
        out_specs=[somewhere] * len(widths)
        + [pl.BlockSpec((tok, part), lambda j: (0, j))] * made
        + [pl.BlockSpec((tok, width), lambda j: (0, 0))] * given,
        out_shape=[jax.ShapeDtypeStruct((total * tok, w), bf16) for w in widths]
        + [jax.ShapeDtypeStruct((tok, steps * part), bf16)] * made
        + [jax.ShapeDtypeStruct((tok, width), bf16)] * given,
        scratch_shapes=[pltpu.VMEM((rows, width), bf16)]
        + [pltpu.VMEM(shape, bf16) for shape in scratch]
        + [pltpu.SemaphoreType.DMA((4 * number + 1,))],
        input_output_aliases={first_alias + i: i for i in range(len(earlier))},
        compiler_params=pltpu.CompilerParams(vmem_limit_bytes=50 * 1024 * 1024),
        cost_estimate=pl.CostEstimate(
            flops=6 * rows * width * steps * part,
            bytes_accessed=6 * width * steps * part + 10 * rows * width,
            transcendentals=rows * steps * part,
        ),
        name=name,
    )(*pieces, *ins, *earlier)


def feed(pieces, masks, total, w_gu, earlier):
    width, units = w_gu.shape[0], w_gu.shape[1] // 2
    part = math.gcd(units, 256)
    steps = units // part
    number = len(pieces)
    rows = number * pieces[0].shape[0]
    specs = [
        pl.BlockSpec((width, part), lambda j: (0, j)),
        pl.BlockSpec((width, part), lambda j: (0, steps + j)),
    ]
    outs = feed_call(
        feed_kernel, "feed", pieces, masks, total, [w_gu, w_gu], specs, earlier,
        (width, units), (steps, part), (2 * number, 0, [(rows, units)]),
    )
    return outs[:2], list(zip(outs[2 : 2 + number], outs[2 + number :], strict=True))


def feed_down(middle_all, masks, tok, down):
    units, width = down.shape
    number = len(masks)

    def kernel(at, middle, weight, *outs):
        for i, out in enumerate(outs):

            @pl.when(pl.program_id(0) == i)
            def _(out=out):
                out[...] = dot(middle[...], weight[...]).astype(bf16)

    return pl.pallas_call(
        kernel,
        grid_spec=pltpu.PrefetchScalarGridSpec(
            num_scalar_prefetch=1,
            grid=(number,),
            in_specs=[
                pl.BlockSpec((tok, units), lambda i, at: (at[i], 0)),
                pl.BlockSpec((units, width), lambda i, at: (0, 0)),
            ],
            out_specs=[pl.BlockSpec((tok, width), lambda i, at: (0, 0))] * number,
        ),
        out_shape=[jax.ShapeDtypeStruct((tok, width), bf16)] * number,
        compiler_params=pltpu.CompilerParams(vmem_limit_bytes=40 * 1024 * 1024),
        cost_estimate=pl.CostEstimate(
            flops=2 * number * tok * units * width,
            bytes_accessed=4 * units * width,
            transcendentals=0,
        ),
        name="feed_down",
    )(jnp.array(masks, jnp.int32), middle_all, down)


def feed_back(pieces, masks, total, acts, w_gu, down, earlier):
    units, width = down.shape
    part = math.gcd(units, 256)
    steps = units // part
    number = len(pieces)
    tok = pieces[0].shape[0]
    rows = number * tok
    specs = [pl.BlockSpec((tok, part), lambda j: (0, j))] * (2 * number) + [
        pl.BlockSpec((part, width), lambda j: (j, 0)),
        pl.BlockSpec(memory_space=pl.ANY),
    ]
    ins = [slope for slope, _ in acts] + [silu for _, silu in acts] + [down, w_gu]
    outs = feed_call(
        feed_back_kernel, "feed_back", pieces, masks, total, ins, specs, earlier,
        (width, units, units), (steps, part), (0, number, [(rows, 2 * units), (width, 2 * units)]),
    )
    return outs[:3], outs[3:]


def owner_grad(h_all, d_act, sizes, rows, which, earlier):
    n_seq, n_hi, n_lo, n_core = sizes
    tokens, width = h_all.shape
    units = d_act.shape[1]
    cols = width // n_seq

    def kernel(h, d, *refs):
        product = t_dot(h[...], d[...]).astype(bf16)
        at = 0
        for hi in range(n_hi):
            for lo in range(n_lo):
                for core in range(n_core):
                    refs[-1][hi, core, 0, lo] = product[at : at + rows]
                    at += rows

    return pl.pallas_call(
        kernel,
        grid=(n_seq,),
        in_specs=[
            pl.BlockSpec((tokens, cols), lambda s: (0, s)),
            pl.BlockSpec((tokens, units), lambda s: (0, 0)),
        ]
        + [pl.BlockSpec(memory_space=pl.ANY)] * len(earlier),
        out_specs=pl.BlockSpec(
            (n_hi, n_core, 1, n_lo, rows, units), lambda s: (0, 0, s, 0, 0, which)
        ),
        out_shape=jax.ShapeDtypeStruct((n_hi, n_core, n_seq, n_lo, rows, 2 * units), bf16),
        input_output_aliases={2: 0} if earlier else {},
        compiler_params=pltpu.CompilerParams(vmem_limit_bytes=40 * 1024 * 1024),
        cost_estimate=pl.CostEstimate(
            flops=2 * tokens * width * units,
            bytes_accessed=2 * (tokens * width + tokens * units + width * units),
            transcendentals=0,
        ),
        name="owner_grad",
    )(h_all, d_act, *earlier)


def pack_columns(weights, count):
    rows, width = weights[0].shape
    part = width // count

    def kernel(*refs):
        for i, ref in enumerate(refs[:-1]):
            refs[-1][0, :, i * part : (i + 1) * part] = ref[...]

    return pl.pallas_call(
        kernel,
        grid=(count,),
        in_specs=[pl.BlockSpec((rows, part), lambda s: (0, s))] * len(weights),
        out_specs=pl.BlockSpec((1, rows, len(weights) * part), lambda s: (s, 0, 0)),
        out_shape=jax.ShapeDtypeStruct((count, rows, len(weights) * part), weights[0].dtype),
        name="pack_columns",
    )(*weights)


def unpack_columns(packed, number):
    count, rows, width = packed.shape
    part = width // number

    def kernel(ref, *outs):
        for i, out in enumerate(outs):
            out[...] = ref[0, :, i * part : (i + 1) * part].astype(f32)

    return pl.pallas_call(
        kernel,
        grid=(count,),
        in_specs=[pl.BlockSpec((1, rows, width), lambda s: (s, 0, 0))],
        out_specs=[pl.BlockSpec((rows, part), lambda s: (0, s))] * number,
        out_shape=[jax.ShapeDtypeStruct((rows, count * part), f32)] * number,
        name="unpack_columns",
    )(packed)


def unit_slices(sizes, unit):
    n_hi, n_lo, n_core = sizes
    return [
        (lo, (hi * n_core + core) * unit, ((hi * n_lo + lo) * n_core + core) * unit)
        for hi in range(n_hi)
        for lo in range(n_lo)
        for core in range(n_core)
    ]


def pack_units(gate, up, n_seq, sizes, unit):
    rows = gate.shape[0]
    n_hi, n_lo, n_core = sizes
    units = n_hi * n_core * unit

    def kernel(gate_ref, up_ref, out):
        for i, ref in enumerate((gate_ref, up_ref)):
            for lo, packed, plain in unit_slices(sizes, unit):
                start = i * units + packed
                out[lo, :, start : start + unit] = ref[:, plain : plain + unit]

    return pl.pallas_call(
        kernel,
        grid=(n_seq,),
        in_specs=[pl.BlockSpec((rows, units * n_lo), lambda s: (0, s))] * 2,
        out_specs=pl.BlockSpec((n_lo, rows, 2 * units), lambda s: (s, 0, 0)),
        out_shape=jax.ShapeDtypeStruct((n_seq * n_lo, rows, 2 * units), gate.dtype),
        name="pack_units",
    )(gate, up)


def unpack_units(packed, n_seq, sizes, unit):
    _, rows, width = packed.shape
    n_lo = sizes[1]
    units = width // 2

    def kernel(ref, *outs):
        for i, out in enumerate(outs):
            for lo, at, plain in unit_slices(sizes, unit):
                start = i * units + at
                out[:, plain : plain + unit] = ref[lo, :, start : start + unit].astype(f32)

    return pl.pallas_call(
        kernel,
        grid=(n_seq,),
        in_specs=[pl.BlockSpec((n_lo, rows, width), lambda s: (s, 0, 0))],
        out_specs=[pl.BlockSpec((rows, units * n_lo), lambda s: (0, s))] * 2,
        out_shape=[jax.ShapeDtypeStruct((rows, n_seq * n_lo * units), f32)] * 2,
        name="unpack_units",
    )(packed)


def finish_kernel(q_in, k_in, q_raw, k_raw, q_inv, k_inv, q_mean, k_mean, d_v, out):
    width = q_in.shape[1]
    for i, (grad, raw, inverse, mean) in enumerate(
        ((q_in, q_raw, q_inv, q_mean), (k_in, k_raw, k_inv, k_mean))
    ):
        normed = raw[...] * inverse[0]
        low = ((grad[...] - normed * mean[0]) * inverse[0]).astype(bf16)
        out[:, i * width : (i + 1) * width] = low
    out[:, 2 * width :] = d_v[...]


def row_specs(block, part):
    cols = lambda i: pl.BlockSpec((block, part), lambda b: (b, i))
    rows = lambda i: pl.BlockSpec((1, block, 1), lambda b: (i, b, 0))
    vector = pl.BlockSpec((1, part), lambda b: (0, 0))
    return cols, rows, vector


def finish(e_query, e_key, raw, inverse, means, d_value, part, block):
    length = raw.shape[0]
    cols, rows, _ = row_specs(block, part)
    return pl.pallas_call(
        finish_kernel,
        grid=(length // block,),
        in_specs=[cols(0), cols(0), cols(0), cols(1)] + [rows(0), rows(1)] * 2 + [cols(0)],
        out_specs=pl.BlockSpec((block, 3 * part), lambda b: (b, 0)),
        out_shape=jax.ShapeDtypeStruct((length, 3 * part), bf16),
        name="finish",
    )(e_query, e_key, raw, raw, inverse, inverse, means, means, d_value)


def dot(left, right):
    return jnp.dot(left, right, preferred_element_type=f32)


def dot_t(left, right):
    return lax.dot_general(left, right, (((1,), (1,)), ((), ())), preferred_element_type=f32)


def t_dot(left, right):
    return lax.dot_general(left, right, (((0,), (0,)), ((), ())), preferred_element_type=f32)


def held(block):
    return lax.optimization_barrier(block)


def rope_tables(positions, head_dim):
    half_dim = head_dim // 2
    frequency = rope_base ** (-(jnp.arange(half_dim, dtype=f32) * 2.0 / head_dim))
    angles = positions.astype(f32)[:, None] * frequency[None, :]
    cosine, sine = jnp.cos(angles), jnp.sin(angles)
    return jnp.concatenate([cosine, cosine], 1), jnp.concatenate([-sine, sine], 1)


def rms(values):
    inverse = lax.rsqrt(jnp.mean(values * values, axis=-1, keepdims=True) + norm_eps)
    return values * inverse, inverse


def rms_back(grad, normed, inverse, gain):
    scaled = grad * gain
    return (scaled - normed * jnp.mean(scaled * normed, axis=-1, keepdims=True)) * inverse


def per_device(
    tokens,
    segment_ids,
    w_query,
    w_key,
    w_value,
    w_out,
    w_gate,
    w_up,
    w_down,
    query_gain,
    key_gain,
    attn_gain,
    ff_gain,
    cotangent,
):
    inputs = tokens[0]
    tok, width = inputs.shape
    n_seq, n_hi, n_lo, n_core = (lax.axis_size(a) for a in ("seq", "zhi", "zlo", "core"))
    n_dev = n_seq * n_hi * n_lo * n_core
    seq = lax.axis_index("seq")
    heads = HEADS // n_seq
    head_dim = width // HEADS
    part = width // n_seq
    length = n_seq * tok
    d_rows = w_query.shape[0]
    ff_rows = w_down.shape[0]
    units = ff_rows * n_hi * n_core

    sizes = (n_hi, n_lo, n_core)
    seq_dims = dims_of("seq")
    lo_dims, hi_dims, core_dims = dims_of("zlo"), dims_of("zhi"), dims_of("core")
    cube_dims = seq_dims + lo_dims
    z_dims = lo_dims + hi_dims
    all_dims = core_dims + lo_dims + hi_dims + seq_dims
    z_axes = ("zhi", "zlo", "core")
    rows_of = lambda block, m: block[m * tok : (m + 1) * tok]

    pair_axes = ("zhi", "core")
    core_swap = lambda piece: swap(piece, core_dims[0])
    lo_order = [
        ((hi * n_core + core) * n_seq + s) * n_lo + lo
        for s in range(n_seq)
        for hi in range(n_hi)
        for lo in range(n_lo)
        for core in range(n_core)
    ]
    hi_order = [lo_order.index(i) for i in range(len(lo_order))]

    tables = rope_tables(jnp.arange(length, dtype=jnp.int32), head_dim)

    qkv_mine = pack_columns((w_query, w_key, w_value), n_seq)
    gains = jnp.stack([query_gain, key_gain, attn_gain, ff_gain])[None]
    gains = gather_row(after(gains, qkv_mine), core_dims + z_dims)
    gains = jnp.transpose(gains, (1, 0, 2)).reshape(1, 4 * part)
    qkv_mine = lax.all_to_all(qkv_mine, "seq", 0, 0, tiled=True).reshape(n_seq * d_rows, 3 * part)
    gu_mine = pack_units(w_gate, w_up, n_seq, sizes, ff_rows)
    qkv_mine, gains, gu_mine = tie(qkv_mine, gains, gu_mine)

    out_mine = jnp.concatenate([w_out[:, i * part : (i + 1) * part] for i in range(n_seq)], axis=0)
    w_z = Spread(jnp.concatenate([qkv_mine, out_mine], axis=1), z_dims).step()
    to_width = lambda row: jnp.pad(row, ((0, 0), (0, width - row.shape[1])))
    ids = to_width(segment_ids.astype(bf16))
    more = jnp.concatenate([ids, to_width(gains), jnp.zeros((14, width), bf16)], axis=0)
    x_spread = Spread(jnp.concatenate([inputs, more], axis=0), seq_dims).step()
    x_pieces = x_spread.whole()
    tables, *x_pieces = tie(w_z, tables, *x_pieces)
    w_sib = [core_swap(piece) for piece in (w_z.pieces[0], *w_z.fresh())]
    early = len(w_sib)
    w_z.step()
    small = after(x_pieces, w_z.fresh())
    row_ids = jnp.concatenate([piece[tok, :tok] for piece in small]).astype(jnp.int32)
    row_ids = row_ids.reshape(length, 1)
    col_ids = jnp.stack(
        [lax.dynamic_slice(row_ids, ((seq ^ m) * tok, 0), (tok, 1)) for m in range(n_seq)]
    ).reshape(n_seq, 1, tok)
    all_gains = jnp.concatenate([piece[tok + 1 : tok + 2, : 4 * part] for piece in small], axis=0)
    all_gains = jnp.concatenate(
        [lax.dynamic_slice(all_gains, (seq ^ m, 0), (1, 4 * part)) for m in range(n_seq)], axis=0
    ).reshape(n_seq, 4, part)
    all_gains = jnp.transpose(all_gains, (1, 0, 2)).reshape(4, width).astype(f32)
    my_gains = gains.reshape(4, 1, part).astype(f32)
    qk_gains = (my_gains[0], my_gains[1])
    (w_sib,) = tie(w_z, w_sib)
    gain_attn, gain_ff = all_gains[2], all_gains[3]
    w_z = w_z.whole()
    w_sib = w_sib + [core_swap(piece) for piece in w_z[early:]]

    gu_mine = lax.all_to_all(after(gu_mine, w_z), ("seq", "zlo"), 0, 0, tiled=True)

    raw, squares, x_all, w_qkv, out_weight = project(
        x_pieces,
        [piece.reshape(n_seq, d_rows, 4 * part) for piece in w_z + w_sib],
        block_starts(
            n_seq,
            d_rows,
            z_dims + core_dims,
            z_axes,
            lambda s, hi, lo, core: ((s * n_hi + hi) * n_lo + lo) * n_core + core,
        ),
        block_starts(
            1,
            d_rows,
            z_dims + core_dims,
            z_axes,
            lambda block, hi, lo, core: (hi * n_lo + lo) * n_core + core,
        ),
        tok,
        part,
    )
    squares, gu_mine = tie(squares, gu_mine)
    w_gu = lax.all_gather(gu_mine, pair_axes, axis=0, tiled=True)
    squares = squares.reshape(2, n_seq, tok)
    squares = sum_all(jnp.transpose(squares, (1, 0, 2)), seq_dims)
    inverse = lax.rsqrt(jnp.transpose(squares, (1, 0, 2)).reshape(2, length, 1) / width + norm_eps)

    context = (seq.astype(jnp.int32).reshape(1), raw, inverse, qk_gains, tables, (row_ids, col_ids))
    attended, attn_low, log_total = attend(context, heads, tok)
    branch = Collect(
        [held(dot(rows_of(attn_low, m), out_weight).astype(bf16)) for m in range(n_seq)], seq_dims
    ).whole()
    branch_norm, branch_inv = rms(branch)
    hidden = inputs.astype(f32) + branch_norm * gain_attn
    hidden_low = hidden.astype(bf16)

    w_gu = regroup(w_gu.reshape(-1, d_rows, 2 * units), lo_order)
    total = 1 << len(cube_dims)
    by_bits = lambda size: [
        m for m in range(total) if bin(m).count("1") == size or (size == 1 and m == 0)
    ]
    fours = lambda masks: [masks[i : i + 4] for i in range(0, len(masks), 4)]
    groups = [masks for size in range(1, len(cube_dims) + 1) for masks in fours(by_bits(size))]
    light = total == 8
    h_spread = Spread(hidden_low, cube_dims, spare_last=light).step()
    if light:
        h_spread.step()
        near = [h_spread.pieces[m] for m in (1, 2, 3)]
        near, w_gu = tie(near, w_gu)
        h_spread.pieces.update(zip((1, 2, 3), near, strict=True))
    acts, partials, kept = {}, {}, ()
    order = [[0, 1], [2, 3], [4, 5, 6], [7]] if light else groups
    for i, masks in enumerate(order):
        while any(m not in h_spread.pieces for m in masks):
            h_spread.step()
        pieces = [h_spread.pieces[m] for m in masks]
        kept, act = feed(pieces, masks, total, w_gu, kept)
        if i == 0:
            last = h_spread.pieces[total // 2] = after(h_spread.pieces[total // 2], act)
            down = lax.all_gather(after(w_down, last), pair_axes, axis=0, tiled=True)
        if light and i == 1:
            (act,) = tie(h_spread.step(), act)
        acts.update(zip(masks, act, strict=True))
    h_all, middle_all = kept
    for masks in fours(sorted(range(total), key=lambda m: -bin(m).count("1"))):
        sums = feed_down(middle_all, masks, tok, down)
        partials.update(zip(masks, sums, strict=True))
    partials = [partials[m] for m in range(total)]
    ff_raw = Collect(partials, cube_dims).whole()
    ff_norm, ff_inv = rms(ff_raw)
    mixed = (hidden + ff_norm * gain_ff).astype(bf16)

    grad_output = cotangent[0].astype(f32)
    grad_ff_gain = jnp.sum(grad_output * ff_norm, axis=0)
    d_ff = rms_back(grad_output, ff_norm, ff_inv, gain_ff).astype(bf16)
    d_spread = Spread(d_ff, cube_dims).step()
    partials, kept = {}, ()
    for masks in groups:
        while any(m not in d_spread.pieces for m in masks):
            d_spread.step()
        pieces = [d_spread.pieces[m] for m in masks]
        act = [acts[m] for m in masks]
        kept, sums = feed_back(pieces, masks, total, act, w_gu, down, kept)
        partials.update(zip(masks, sums, strict=True))
    d_ff_all, d_gate_all, d_up_all = kept
    partials = [partials[m] for m in range(total)]
    d_hidden = Collect(partials, cube_dims).step()

    owned = lambda grad: lax.psum_scatter(grad, pair_axes, scatter_dimension=0, tiled=True)
    grad_down = t_dot(middle_all, after(d_ff_all, partials)).astype(bf16)
    (grad_down,) = tie(d_hidden, grad_down)
    grad_down = owned(grad_down)
    order = (n_seq, n_hi, n_lo, n_core)
    d_hidden.step()
    grad_gu = owner_grad(h_all, d_gate_all, order, d_rows, 0, [])
    (grad_gu,) = tie(d_hidden, grad_gu)
    d_hidden.step()
    grad_gu = owner_grad(h_all, after(d_up_all, grad_gu), order, d_rows, 1, [grad_gu])
    (grad_gu,) = tie(d_hidden, grad_gu)
    grad_gu = owned(grad_gu.reshape(-1, d_rows, 2 * units))
    d_hidden = d_hidden.whole()

    d_hidden = grad_output + d_hidden
    grad_attn_gain = jnp.sum(d_hidden * branch_norm, axis=0)
    d_branch = rms_back(d_hidden, branch_norm, branch_inv, gain_attn).astype(bf16)
    d_branch_pieces = Spread(d_branch, seq_dims).whole()
    d_branch_pieces, grad_down = tie(d_branch_pieces, grad_down)
    d_attended = jnp.concatenate(
        [dot_t(piece, out_weight).astype(bf16) for piece in d_branch_pieces], axis=0
    )
    e_query, e_key, d_value, q_sum, k_sum, grad_query_gain, grad_key_gain = attend_back(
        context, d_attended, attended, log_total, heads, tok
    )
    means = jnp.stack([q_sum[0], k_sum[0]]).reshape(2, n_seq, tok)
    means = sum_all(jnp.transpose(means, (1, 0, 2)), seq_dims)
    means = jnp.transpose(means, (1, 0, 2)).reshape(2, length, 1) / width

    n_z = n_hi * n_lo
    z_blocks = lambda grad: take_blocks(
        jnp.transpose(
            grad.reshape(n_seq, n_hi, n_lo, n_core, d_rows, grad.shape[1]), (1, 2, 3, 0, 4, 5)
        ),
        z_dims + core_dims,
        z_axes,
    )
    def to_core(grad):
        blocks = z_blocks(grad)
        theirs = [core_swap(piece) for piece in blocks[n_z:]]
        return [
            add_low(a, b).reshape(-1, a.shape[-1]) for a, b in zip(blocks[:n_z], theirs, strict=True)
        ]

    d_qkv = finish(e_query, e_key, raw, inverse, means, d_value, part, tok)
    grad_qkv = t_dot(x_all, d_qkv).astype(bf16)
    back = lambda rows, m: held(dot_t(rows_of(rows, m), w_qkv).astype(bf16))
    far = back(after(d_qkv, grad_qkv), n_seq - 1)
    grad_qkv, far, low_rows = tie(to_core(grad_qkv), far, d_qkv)
    grad_qkv = Collect(grad_qkv, z_dims).step()
    low_rows, far = tie(grad_qkv, low_rows, far)
    low_rows, far = tie(grad_qkv.ready(), low_rows, far)
    grad_qkv.step()
    input_grad = Collect([back(low_rows, m) for m in range(n_seq - 1)] + [far], seq_dims)
    input_grad.step()
    full_row = lambda cols: lax.dynamic_update_slice(jnp.zeros((width,), f32), cols, (seq * part,))
    rows = jnp.stack(
        [full_row(grad_query_gain[0]), full_row(grad_key_gain[0]), grad_attn_gain, grad_ff_gain]
    )
    rows = jnp.transpose(rows.reshape(4, n_dev, d_rows), (1, 0, 2))
    grad_gu = after(grad_gu, low_rows).reshape(n_seq * n_lo, d_rows, 2 * units)
    grad_gu = lax.all_to_all(grad_gu, ("seq", "zlo"), 0, 0, tiled=True)
    d_branch_all = jnp.concatenate(after(d_branch_pieces, low_rows), axis=0)
    grad_out = t_dot(attn_low, d_branch_all).astype(bf16)
    grad_out = jnp.concatenate([grad_out[:, i * part : (i + 1) * part] for i in range(n_seq)], axis=0)
    grad_out, grad_gu = tie(grad_qkv, input_grad, to_core(grad_out), grad_gu)
    input_grad.step()
    grad_qkv = grad_qkv.whole().astype(bf16).reshape(n_seq, d_rows, 3 * part)
    grad_qkv = lax.all_to_all(grad_qkv, "seq", 0, 0, tiled=True)
    grad_out = Collect(grad_out, z_dims).step()
    rows = lax.all_to_all(after(rows, grad_qkv), ("seq",) + z_axes, 0, 0, tiled=True)
    input_grad = d_hidden + input_grad.whole()
    grad_down = after(grad_down, grad_qkv).astype(f32)
    grad_out = grad_out.whole().reshape(n_seq, d_rows, part)
    grad_gate, grad_up = unpack_units(grad_gu, n_seq, sizes, ff_rows)
    grad_query, grad_key, grad_value = unpack_columns(grad_qkv, 3)
    rows = jnp.sum(rows, axis=0)
    grad_out = jnp.concatenate([grad_out[i] for i in range(n_seq)], axis=1)

    return (
        mixed[None],
        input_grad[None],
        grad_query,
        grad_key,
        grad_value,
        grad_out,
        grad_gate,
        grad_up,
        grad_down,
        rows[0],
        rows[1],
        rows[2],
        rows[3],
    )


def solution(mesh):
    n_seq, n_row = mesh.shape["seq"], mesh.shape["row"]
    n_core = 2
    n_lo = 2
    n_hi = n_row // (n_core * n_lo)
    cut = Mesh(
        mesh.devices.reshape(n_seq, n_hi, n_lo, n_core), ("seq", "zhi", "zlo", "core")
    )
    row = ("zhi", "zlo", "core")
    every = ("seq",) + row
    acts = P(row, "seq", None)
    matrix = P(every, None)
    vector = P(every)
    return jax.shard_map(
        per_device,
        mesh=cut,
        in_specs=(acts, P(row, "seq")) + (matrix,) * 7 + (vector,) * 4 + (acts,),
        out_specs=(acts, acts) + (matrix,) * 7 + (vector,) * 4,
        check_vma=False,
    )
```

```python
import functools
import math

import jax
import jax.numpy as jnp
from jax import lax
from jax.experimental import pallas as pl
from jax.experimental.pallas import tpu as pltpu
from jax.sharding import Mesh
from jax.sharding import PartitionSpec as P

HEADS = 16

rope_base = 500000.0
norm_eps = 1e-06
masked_score = -1e30

bf16 = jnp.bfloat16
f32 = jnp.float32


def dims_of(axis):
    count = lax.axis_size(axis)
    return [(axis, 1 << bit) for bit in range(count.bit_length() - 1)]


def swap(block, dim):
    axis, mask = dim
    return lax.ppermute(block, axis, [(i, i ^ mask) for i in range(lax.axis_size(axis))])


def partner_index(dims, which):
    masks = {}
    for bit, (axis, mask) in enumerate(dims):
        if which >> bit & 1:
            masks[axis] = masks.get(axis, 0) | mask
    return masks


def column_cuts(width, count):
    tiles = width // 128
    return [round(tiles * i / count) * 128 for i in range(count + 1)]


def column_parts(block, count):
    cuts = column_cuts(block.shape[1], count)
    return [block[:, cuts[i] : cuts[i + 1]] for i in range(count)]


def route(which, count):
    bits = [i for i in range(count) if which >> i & 1]
    if len(bits) == 1:
        return bits[0]
    return bits[0] if bits[1] - bits[0] == 1 else bits[1]


def by_size(count):
    return sorted(range(1, 1 << count), key=lambda m: bin(m).count("1"))


class Spread:
    def __init__(self, block, dims, spare_last=False):
        self.dims, self.size, self.pieces, self.new = dims, 0, {0: block}, [0]
        self.spare_last = spare_last and len(dims) == 3

    def light_step(self):
        x, y, _ = self.dims
        half = lambda m, i: column_parts(self.pieces[m], 2)[i]
        if self.size == 2:
            self.new = [3]
            self.pieces[3] = jnp.concatenate([swap(half(2, 0), x), swap(half(1, 1), y)], axis=1)
        elif self.size == 3:
            self.new = [5, 6]
            self.pieces[5], self.pieces[6] = swap(self.pieces[4], x), swap(self.pieces[4], y)
        else:
            self.new = [7]
            self.pieces[7] = jnp.concatenate([swap(half(6, 0), x), swap(half(5, 1), y)], axis=1)

    def step(self):
        self.size += 1
        count = len(self.dims)
        if self.spare_last and self.size > 1:
            self.light_step()
            return self
        self.new = [m for m in by_size(count) if bin(m).count("1") == self.size]
        for which in self.new:
            if self.size == count and count > 1:
                parts = [
                    swap(column_parts(self.pieces[which ^ (1 << i)], count)[i], self.dims[i])
                    for i in range(count)
                ]
                self.pieces[which] = jnp.concatenate(parts, axis=1)
            else:
                via = route(which, count)
                self.pieces[which] = swap(self.pieces[which ^ (1 << via)], self.dims[via])
        return self

    def fresh(self):
        return [self.pieces[m] for m in self.new]

    def renew(self, values):
        self.pieces.update(zip(self.new, values, strict=True))

    def whole(self):
        while self.size < len(self.dims):
            self.step()
        return [self.pieces[m] for m in range(1 << len(self.dims))]


class Collect:
    def __init__(self, pieces, dims):
        self.dims, self.size, self.pieces = dims, len(dims), list(pieces)
        self.got, self.new = {m: [] for m in range(len(self.pieces))}, []
        self.sums = None

    def ready(self):
        masks = [m for m in by_size(len(self.dims)) if bin(m).count("1") == self.size]
        self.sums = {m: self.total(m) for m in masks}
        return self

    def step(self):
        count = len(self.dims)
        if self.sums is None:
            self.ready()
        sums, self.sums, self.new = self.sums, None, []
        for which, total in sums.items():
            if self.size == count and count > 1:
                for i, cols in enumerate(column_parts(total, count)):
                    self.keep(which ^ (1 << i), i, swap(cols, self.dims[i]))
            else:
                via = route(which, count)
                self.keep(which ^ (1 << via), None, swap(total, self.dims[via]))
        self.size -= 1
        return self

    def keep(self, which, part, arrived):
        self.new.append((which, len(self.got[which])))
        self.got[which].append((part, arrived))

    def total(self, which):
        if not self.got[which]:
            return self.pieces[which]
        count = len(self.dims)
        total = self.pieces[which].astype(f32)
        for part, arrived in self.got[which]:
            if part is None:
                total = total + arrived.astype(f32)
            else:
                cols = column_parts(total, count)
                cols[part] = cols[part] + arrived.astype(f32)
                total = jnp.concatenate(cols, axis=1)
        return total.astype(bf16)

    def fresh(self):
        if self.sums is not None:
            return list(self.sums.values())
        return [self.got[which][i][1] for which, i in self.new]

    def renew(self, values):
        if self.sums is not None:
            self.sums = dict(zip(self.sums, values, strict=True))
            return
        for (which, i), value in zip(self.new, values, strict=True):
            self.got[which][i] = (self.got[which][i][0], value)

    def whole(self):
        while self.size > 0:
            self.step()
        total = self.pieces[0].astype(f32)
        for _, arrived in self.got[0]:
            total = total + arrived.astype(f32)
        return total


def tie(*items):
    steps = (Spread, Collect)
    values = [item.fresh() if isinstance(item, steps) else item for item in items]
    values = lax.optimization_barrier(values)
    rest = []
    for item, value in zip(items, values, strict=True):
        if isinstance(item, steps):
            item.renew(value)
        else:
            rest.append(value)
    return rest


def sum_all(table, dims):
    for bit, dim in enumerate(dims):
        there = swap(table, dim)
        order = [m ^ (1 << bit) for m in range(table.shape[0])]
        table = table + jnp.stack([there[m] for m in order])
    return table


def after(block, *earlier):
    return lax.optimization_barrier((block, earlier))[0]


def block_starts(blocks, rows, dims, axes, order):
    starts = []
    for m in range(1 << len(dims)):
        masks = partner_index(dims, m)
        at = [lax.axis_index(a) ^ masks.get(a, 0) for a in axes]
        starts += [order(block, *at) * rows for block in range(blocks)]
    return jnp.stack(starts).astype(jnp.int32)


def project(x_pieces, w_pieces, starts, out_starts, tok, part):
    n_x, n_w = len(x_pieces), len(w_pieces)
    width = x_pieces[0].shape[1]
    blocks, rows, _ = w_pieces[0].shape
    length = n_x * tok
    number = n_w * blocks

    def kernel(table, out_table, *refs):
        xs, ws = refs[:n_x], refs[n_x : n_x + n_w]
        raw, squares, x_out, w_out, o_out, x_all, w_all, o_all, sems = refs[n_x + n_w :]
        at = pl.program_id(0)
        arrive, later = [], []
        for i in range(n_x):
            source, target = xs[i].at[pl.ds(0, tok)], x_all.at[pl.ds(i * tok, tok)]
            arrive.append(pltpu.make_async_copy(source, target, sems.at[i]))
        for i in range(number):
            piece, block = ws[i // blocks], i % blocks
            here = pl.ds(pl.multiple_of(table[i], rows), rows)
            source = piece.at[block, :, pl.ds(0, 3 * part)]
            arrive.append(pltpu.make_async_copy(source, w_all.at[here], sems.at[n_x + i]))
            here = pl.ds(pl.multiple_of(out_table[i // blocks], rows), rows)
            source = piece.at[block, :, pl.ds(3 * part, part)]
            target = o_all.at[here, pl.ds(block * part, part)]
            later.append(pltpu.make_async_copy(source, target, sems.at[n_x + number + i]))
        sem = n_x + 2 * number
        keep = [
            pltpu.make_async_copy(x_all, x_out, sems.at[sem]),
            pltpu.make_async_copy(w_all, w_out, sems.at[sem + 1]),
        ]
        keep_out = pltpu.make_async_copy(o_all, o_out, sems.at[sem + 2])

        @pl.when(at == 0)
        def _():
            for copy in arrive + later:
                copy.start()
            for copy in arrive:
                copy.wait()
            for copy in keep:
                copy.start()

        for step in range(3):

            @pl.when(at == step)
            def _(step=step):
                product = dot(x_all[...], w_all[:, step * part : (step + 1) * part])
                raw[...] = product
                if step < 2:
                    squares[0] = jnp.sum(product * product, axis=-1, keepdims=True)
                if step == 0:
                    for copy in later:
                        copy.wait()
                    keep_out.start()

        @pl.when(at == 2)
        def _():
            for copy in keep + [keep_out]:
                copy.wait()

    somewhere = pl.BlockSpec(memory_space=pl.ANY)
    scalars = pl.BlockSpec(memory_space=pltpu.SMEM)
    return pl.pallas_call(
        kernel,
        grid=(3,),
        in_specs=[scalars] * 2 + [somewhere] * (n_x + n_w),
        out_specs=[
            pl.BlockSpec((length, part), lambda j: (0, j)),
            pl.BlockSpec((1, length, 1), lambda j: (jnp.minimum(j, 1), 0, 0)),
            somewhere,
            somewhere,
            somewhere,
        ],
        out_shape=[
            jax.ShapeDtypeStruct((length, 3 * part), f32),
            jax.ShapeDtypeStruct((2, length, 1), f32),
            jax.ShapeDtypeStruct((length, width), bf16),
            jax.ShapeDtypeStruct((width, 3 * part), bf16),
            jax.ShapeDtypeStruct((n_w * rows, blocks * part), bf16),
        ],
        scratch_shapes=[
            pltpu.VMEM((length, width), bf16),
            pltpu.VMEM((width, 3 * part), bf16),
            pltpu.VMEM((n_w * rows, blocks * part), bf16),
            pltpu.SemaphoreType.DMA((n_x + 2 * number + 3,)),
        ],
        compiler_params=pltpu.CompilerParams(vmem_limit_bytes=56 * 1024 * 1024),
        cost_estimate=pl.CostEstimate(
            flops=6 * length * width * part, bytes_accessed=20 * length * part, transcendentals=0
        ),
        name="project",
    )(starts, out_starts, *x_pieces, *w_pieces)


def regroup(blocks, order):
    number, rows, width = blocks.shape

    def kernel(ref, out, sems):
        copies = [
            pltpu.make_async_copy(ref.at[at], out.at[pl.ds(i * rows, rows)], sems.at[i])
            for i, at in enumerate(order)
        ]
        for copy in copies:
            copy.start()
        for copy in copies:
            copy.wait()

    return pl.pallas_call(
        kernel,
        in_specs=[pl.BlockSpec(memory_space=pltpu.HBM)],
        out_specs=pl.BlockSpec(memory_space=pltpu.VMEM),
        out_shape=jax.ShapeDtypeStruct((number * rows, width), blocks.dtype),
        scratch_shapes=[pltpu.SemaphoreType.DMA((number,))],
        compiler_params=pltpu.CompilerParams(vmem_limit_bytes=24 * 1024 * 1024),
        name="regroup",
    )(blocks)


def take_blocks(whole, dims, axes):
    shape = whole.shape[len(axes) :]
    pieces = []
    for m in range(1 << len(dims)):
        masks = partner_index(dims, m)
        at = tuple(lax.axis_index(a) ^ masks.get(a, 0) for a in axes)
        piece = lax.dynamic_slice(whole, at + (0,) * len(shape), (1,) * len(axes) + shape)
        pieces.append(piece.reshape(shape))
    return pieces


def add_low(kept, arrived):
    return (kept.astype(f32) + arrived.astype(f32)).astype(bf16)


def gather_row(row, dims):
    for axis, mask in dims:
        there = swap(row, (axis, mask))
        low = (lax.axis_index(axis) & mask) == 0
        row = jnp.concatenate([jnp.where(low, row, there), jnp.where(low, there, row)], axis=0)
    return row


def turned(raw, inverse, gain, cosine, sine):
    scaled = raw * inverse * gain
    return scaled * cosine + pltpu.roll(scaled, scaled.shape[1] // 2, 1) * sine


def turned_back(grad, raw, inverse, gain, cosine, sine):
    back = grad * cosine - pltpu.roll(grad, grad.shape[1] // 2, 1) * sine
    product = back * (raw * inverse)
    return back * gain, jnp.sum(product * gain, -1, keepdims=True), jnp.sum(product, 0, keepdims=True)


def block_scores(scale, last, a, j, k, q, key_ids, query_ids):
    scores = dot_t(k, q) * scale
    allowed = None
    if j == 0 or a == last:
        allowed = key_ids == query_ids
    if j == a:
        shape = scores.shape
        causal = lax.broadcasted_iota(jnp.int32, shape, 0) <= lax.broadcasted_iota(jnp.int32, shape, 1)
        allowed = causal if allowed is None else allowed & causal
    return scores if allowed is None else jnp.where(allowed, scores, masked_score)


def forward_kernel(
    scale, count, tok, place, q_raw, k_raw, v_raw, q_inv, k_inv, q_gain, k_gain, cosine, sine,
    row_ids, col_ids, out, low, log_total, k_all, v_across,
):
    rows = lambda j: pl.ds(pl.multiple_of((place[0] ^ j) * tok, tok), tok)
    cols = lambda j: slice(j * tok, (j + 1) * tok)
    for a in range(count):
        here = rows(a)
        table = (cosine[cols(a), :], sine[cols(a), :])
        k_all[cols(a), :] = turned(k_raw[here, :], k_inv[0, here, :], k_gain[...], *table).astype(bf16)
        v_across[:, cols(a)] = v_raw[here, :].T.astype(bf16)
        q = turned(q_raw[here, :], q_inv[0, here, :], q_gain[...], *table).astype(bf16)
        scores = [
            block_scores(scale, count - 1, a, j, k_all[cols(j), :], q, row_ids[rows(j), :], col_ids[a])
            for j in range(a + 1)
        ]
        top = jnp.max(functools.reduce(jnp.maximum, scores), axis=0, keepdims=True)
        expo = [jnp.exp2(block - top) for block in scores]
        total = jnp.sum(functools.reduce(jnp.add, expo), axis=0, keepdims=True)
        parts = [dot(v_across[:, cols(j)], expo[j].astype(bf16)) for j in range(a + 1)]
        attended = (functools.reduce(jnp.add, parts) * (1.0 / total)).T
        out[here, :] = attended
        low[here, :] = attended.astype(bf16)
        log_total[0, place[0] ^ a] = top + jnp.log2(total)


def backward_kernel(
    scale, plain_scale, count, tok, place, q_raw, k_raw, v_raw, q_inv, k_inv, q_gain, k_gain,
    cosine, sine, row_ids, col_ids, d_out, out, log_total,
    e_q, e_k, d_v, q_sum, k_sum, q_gain_grad, k_gain_grad, k_all, k_across, v_all, d_k_all, d_v_all,
):
    rows = lambda j: pl.ds(pl.multiple_of((place[0] ^ j) * tok, tok), tok)
    cols = lambda j: slice(j * tok, (j + 1) * tok)
    q_gain_grad[...] = jnp.zeros_like(q_gain_grad)

    @pl.when(pl.program_id(0) == 0)
    def _():
        q_sum[...] = jnp.zeros_like(q_sum)
        k_sum[...] = jnp.zeros_like(k_sum)

    for a in range(count):
        here = rows(a)
        table = (cosine[cols(a), :], sine[cols(a), :])
        k = turned(k_raw[here, :], k_inv[0, here, :], k_gain[...], *table)
        k_all[cols(a), :] = k.astype(bf16)
        k_across[:, cols(a)] = k.T.astype(bf16)
        v_all[cols(a), :] = v_raw[here, :].astype(bf16)
        q_row, inverse = q_raw[here, :], q_inv[0, here, :]
        q = turned(q_row, inverse, q_gain[...], *table).astype(bf16)
        d_blk = d_out[here, :]
        row_dot = jnp.sum(d_blk.astype(f32) * out[here, :], axis=-1, keepdims=True)
        row_dot = jnp.broadcast_to(row_dot, q_row.shape).T[0:1, :]
        log_row = log_total[0, place[0] ^ a]
        d_q = []
        for j in range(a + 1):
            scores = block_scores(
                scale, count - 1, a, j, k_all[cols(j), :], q, row_ids[rows(j), :], col_ids[a]
            )
            probability = jnp.exp2(scores - log_row)
            d_prob = dot_t(v_all[cols(j), :], d_blk)
            d_scores = (probability * (d_prob - row_dot)).astype(bf16)
            d_q.append(dot(k_across[:, cols(j)], d_scores))
            d_k = dot(d_scores, q)
            d_v_part = dot(probability.astype(bf16), d_blk)
            if j == a:
                d_k_all[cols(j), :] = d_k
                d_v_all[cols(j), :] = d_v_part
            else:
                d_k_all[cols(j), :] += d_k
                d_v_all[cols(j), :] += d_v_part
        e_q[here, :], row_sum, gain_grad = turned_back(
            functools.reduce(jnp.add, d_q).T * plain_scale, q_row, inverse, q_gain[...], *table
        )
        q_sum[0, here, :] += row_sum
        q_gain_grad[...] += gain_grad
    k_gain_grad[...] = jnp.zeros_like(k_gain_grad)
    for j in range(count):
        here = rows(j)
        e_k[here, :], row_sum, gain_grad = turned_back(
            d_k_all[cols(j), :] * plain_scale, k_raw[here, :], k_inv[0, here, :],
            k_gain[...], cosine[cols(j), :], sine[cols(j), :],
        )
        k_sum[0, here, :] += row_sum
        k_gain_grad[...] += gain_grad
        d_v[here, :] = d_v_all[cols(j), :].astype(bf16)


def attention_specs(tokens, block, heads, head_dim):
    head = lambda i: pl.BlockSpec((tokens, head_dim), lambda h, s: (0, i * heads + h))
    whole = lambda shape: pl.BlockSpec(shape, lambda h, s: (0,) * len(shape))
    vector = pl.BlockSpec((1, head_dim), lambda h, s: (0, h))
    inverse = lambda i: pl.BlockSpec((1, tokens, 1), lambda h, s: (i, 0, 0))
    inputs = [head(0), head(1), head(2), inverse(0), inverse(1), vector, vector]
    inputs += [whole((tokens, head_dim))] * 2
    inputs += [whole((tokens, 1)), whole((tokens // block, 1, block))]
    logs = pl.BlockSpec((1, tokens // block, 1, block), lambda h, s: (h, 0, 0, 0))
    return inputs, head(0), logs, vector


def attend(context, heads, block):
    place, raw, inverse, gains, tables, ids = context
    tokens, width = raw.shape[0], raw.shape[1] // 3
    head_dim = width // heads
    inputs, head, logs, _ = attention_specs(tokens, block, heads, head_dim)
    return pl.pallas_call(
        functools.partial(forward_kernel, head_dim**-0.5 * math.log2(math.e), tokens // block, block),
        grid_spec=pltpu.PrefetchScalarGridSpec(
            num_scalar_prefetch=1,
            grid=(heads,),
            in_specs=inputs,
            out_specs=[head, head, logs],
            scratch_shapes=[
                pltpu.VMEM((tokens, head_dim), bf16),
                pltpu.VMEM((head_dim, tokens), bf16),
            ],
        ),
        out_shape=[
            jax.ShapeDtypeStruct((tokens, width), f32),
            jax.ShapeDtypeStruct((tokens, width), bf16),
            jax.ShapeDtypeStruct((heads, tokens // block, 1, block), f32),
        ],
        compiler_params=pltpu.CompilerParams(vmem_limit_bytes=40 * 1024 * 1024),
        cost_estimate=pl.CostEstimate(
            flops=2 * tokens * tokens * width,
            bytes_accessed=18 * tokens * width,
            transcendentals=heads * tokens * tokens // 2,
        ),
        name="attend",
    )(place, raw, raw, raw, inverse, inverse, *gains, *tables, *ids)


def attend_back(context, d_out, out, log_total, heads, block):
    place, raw, inverse, gains, tables, ids = context
    tokens, width = raw.shape[0], raw.shape[1] // 3
    head_dim = width // heads
    inputs, head, logs, vector = attention_specs(tokens, block, heads, head_dim)
    sums = pl.BlockSpec((1, tokens, 1), lambda h, s: (0, 0, 0))
    scale = head_dim**-0.5
    return pl.pallas_call(
        functools.partial(
            backward_kernel, scale * math.log2(math.e), scale, tokens // block, block
        ),
        grid_spec=pltpu.PrefetchScalarGridSpec(
            num_scalar_prefetch=1,
            grid=(heads,),
            in_specs=inputs + [head, head, logs],
            out_specs=[head, head, head, sums, sums, vector, vector],
            scratch_shapes=[
                pltpu.VMEM((tokens, head_dim), bf16),
                pltpu.VMEM((head_dim, tokens), bf16),
                pltpu.VMEM((tokens, head_dim), bf16),
                pltpu.VMEM((tokens, head_dim), f32),
                pltpu.VMEM((tokens, head_dim), f32),
            ],
        ),
        out_shape=[
            jax.ShapeDtypeStruct((tokens, width), f32),
            jax.ShapeDtypeStruct((tokens, width), f32),
            jax.ShapeDtypeStruct((tokens, width), bf16),
        ]
        + [jax.ShapeDtypeStruct((1, tokens, 1), f32)] * 2
        + [jax.ShapeDtypeStruct((1, width), f32)] * 2,
        compiler_params=pltpu.CompilerParams(vmem_limit_bytes=56 * 1024 * 1024),
        cost_estimate=pl.CostEstimate(
            flops=5 * tokens * tokens * width,
            bytes_accessed=30 * tokens * width,
            transcendentals=heads * tokens * tokens // 2,
        ),
        name="attend_back",
    )(place, raw, raw, raw, inverse, inverse, *gains, *tables, *ids, d_out, out, log_total)


def sigmoid(values):
    return 1.0 / (1.0 + jnp.exp(-values))


def feed_kernel(masks, tok, steps, refs):
    number = len(masks)
    pieces, refs = refs[:number], refs[number:]
    w_gate, w_up, h_all, middle_all, refs = *refs[:4], refs[4:]
    slopes, silus, refs = refs[:number], refs[number : 2 * number], refs[2 * number :]
    held_h, held_middle, sems = refs
    at = pl.program_id(0)
    part = slopes[0].shape[1]
    block = lambda i: pl.ds(i * tok, tok)
    copies = lambda held, whole, first: [
        pltpu.make_async_copy(held.at[block(i)], whole.at[block(m)], sems.at[first + i])
        for i, m in enumerate(masks)
    ]
    arrive = [
        pltpu.make_async_copy(pieces[i], held_h.at[block(i)], sems.at[i]) for i in range(number)
    ]
    keep_h, keep_middle = copies(held_h, h_all, number), copies(held_middle, middle_all, 2 * number)

    @pl.when(at == 0)
    def _():
        for copy in arrive:
            copy.start()
        for copy in arrive:
            copy.wait()
        for copy in keep_h:
            copy.start()

    gate_act = dot(held_h[...], w_gate[...])
    up_act = dot(held_h[...], w_up[...])
    sig = sigmoid(gate_act)
    silu = gate_act * sig
    middle = (silu * up_act).astype(bf16)
    slope = up_act * (sig + silu * (1.0 - sig))
    for i in range(number):
        slopes[i][...] = slope[i * tok : (i + 1) * tok].astype(bf16)
        silus[i][...] = silu[i * tok : (i + 1) * tok].astype(bf16)
    for step in range(steps):

        @pl.when(at == step)
        def _(step=step):
            held_middle[:, step * part : (step + 1) * part] = middle

    @pl.when(at == steps - 1)
    def _():
        for copy in keep_middle:
            copy.start()
        for copy in keep_h + keep_middle:
            copy.wait()


def feed_back_kernel(masks, tok, steps, refs):
    number = len(masks)
    pieces, refs = refs[:number], refs[number:]
    slopes, silus, refs = refs[:number], refs[number : 2 * number], refs[2 * number :]
    down, w_gu, d_ff_all, d_gate_all, d_up_all = refs[:5]
    partials, (held_d, held_gu, held_w, sems) = refs[5 : 5 + number], refs[5 + number :]
    at = pl.program_id(0)
    part = slopes[0].shape[1]
    units = steps * part
    block = lambda i: pl.ds(i * tok, tok)
    arrive, keep_d, keep_gu = [], [], []
    for i, m in enumerate(masks):
        arrive.append(pltpu.make_async_copy(pieces[i], held_d.at[block(i)], sems.at[i]))
        keep_d.append(
            pltpu.make_async_copy(held_d.at[block(i)], d_ff_all.at[block(m)], sems.at[number + i])
        )
        for j, whole in enumerate((d_gate_all, d_up_all)):
            source = held_gu.at[block(i), pl.ds(j * units, units)]
            sem = sems.at[(2 + j) * number + i]
            keep_gu.append(pltpu.make_async_copy(source, whole.at[block(m)], sem))
    weights = pltpu.make_async_copy(w_gu, held_w, sems.at[4 * number])

    @pl.when(at == 0)
    def _():
        for copy in arrive:
            copy.start()
        weights.start()
        for copy in arrive:
            copy.wait()
        for copy in keep_d:
            copy.start()

    d_middle_all = dot_t(held_d[...], down[...])
    d_gates, d_ups = [], []
    for i in range(number):
        d_middle = d_middle_all[i * tok : (i + 1) * tok]
        d_gates.append((d_middle * slopes[i][...].astype(f32)).astype(bf16))
        d_ups.append((d_middle * silus[i][...].astype(f32)).astype(bf16))
    for step in range(steps):

        @pl.when(at == step)
        def _(step=step):
            for i in range(number):
                rows = slice(i * tok, (i + 1) * tok)
                held_gu[rows, step * part : (step + 1) * part] = d_gates[i]
                held_gu[rows, units + step * part : units + (step + 1) * part] = d_ups[i]

    @pl.when(at == steps - 1)
    def _():
        for copy in keep_gu:
            copy.start()
        weights.wait()
        width = held_d.shape[1]
        cols = math.gcd(width, 1024)
        for n in range(0, width, cols):
            product = dot_t(held_gu[...], held_w[n : n + cols, :]).astype(bf16)
            for i, out in enumerate(partials):
                out[:, n : n + cols] = product[i * tok : (i + 1) * tok]
        for copy in keep_d + keep_gu:
            copy.wait()


def feed_call(kernel, name, pieces, masks, total, ins, in_specs, earlier, widths, blocks, held):
    number = len(pieces)
    tok, width = pieces[0].shape
    steps, part = blocks
    made, given, scratch = held
    somewhere = pl.BlockSpec(memory_space=pl.ANY)
    rows = number * tok
    first_alias = number + len(ins)

    def body(*refs):
        refs = refs[:first_alias] + refs[first_alias + len(earlier) :]
        kernel(masks, tok, steps, refs)

    return pl.pallas_call(
        body,
        grid=(steps,),
        in_specs=[somewhere] * number + in_specs + [somewhere] * len(earlier),
        out_specs=[somewhere] * len(widths)
        + [pl.BlockSpec((tok, part), lambda j: (0, j))] * made
        + [pl.BlockSpec((tok, width), lambda j: (0, 0))] * given,
        out_shape=[jax.ShapeDtypeStruct((total * tok, w), bf16) for w in widths]
        + [jax.ShapeDtypeStruct((tok, steps * part), bf16)] * made
        + [jax.ShapeDtypeStruct((tok, width), bf16)] * given,
        scratch_shapes=[pltpu.VMEM((rows, width), bf16)]
        + [pltpu.VMEM(shape, bf16) for shape in scratch]
        + [pltpu.SemaphoreType.DMA((4 * number + 1,))],
        input_output_aliases={first_alias + i: i for i in range(len(earlier))},
        compiler_params=pltpu.CompilerParams(vmem_limit_bytes=50 * 1024 * 1024),
        cost_estimate=pl.CostEstimate(
            flops=6 * rows * width * steps * part,
            bytes_accessed=6 * width * steps * part + 10 * rows * width,
            transcendentals=rows * steps * part,
        ),
        name=name,
    )(*pieces, *ins, *earlier)


def feed(pieces, masks, total, w_gu, earlier):
    width, units = w_gu.shape[0], w_gu.shape[1] // 2
    part = math.gcd(units, 512)
    steps = units // part
    number = len(pieces)
    rows = number * pieces[0].shape[0]
    specs = [
        pl.BlockSpec((width, part), lambda j: (0, j)),
        pl.BlockSpec((width, part), lambda j: (0, steps + j)),
    ]
    outs = feed_call(
        feed_kernel, "feed", pieces, masks, total, [w_gu, w_gu], specs, earlier,
        (width, units), (steps, part), (2 * number, 0, [(rows, units)]),
    )
    return outs[:2], list(zip(outs[2 : 2 + number], outs[2 + number :], strict=True))


def feed_down(middle_all, masks, tok, down):
    units, width = down.shape
    number = len(masks)

    def kernel(at, middle, weight, *outs):
        for i, out in enumerate(outs):

            @pl.when(pl.program_id(0) == i)
            def _(out=out):
                out[...] = dot(middle[...], weight[...]).astype(bf16)

    return pl.pallas_call(
        kernel,
        grid_spec=pltpu.PrefetchScalarGridSpec(
            num_scalar_prefetch=1,
            grid=(number,),
            in_specs=[
                pl.BlockSpec((tok, units), lambda i, at: (at[i], 0)),
                pl.BlockSpec((units, width), lambda i, at: (0, 0)),
            ],
            out_specs=[pl.BlockSpec((tok, width), lambda i, at: (0, 0))] * number,
        ),
        out_shape=[jax.ShapeDtypeStruct((tok, width), bf16)] * number,
        compiler_params=pltpu.CompilerParams(vmem_limit_bytes=40 * 1024 * 1024),
        cost_estimate=pl.CostEstimate(
            flops=2 * number * tok * units * width,
            bytes_accessed=4 * units * width,
            transcendentals=0,
        ),
        name="feed_down",
    )(jnp.array(masks, jnp.int32), middle_all, down)


def feed_back(pieces, masks, total, acts, w_gu, down, earlier):
    units, width = down.shape
    part = math.gcd(units, 512)
    steps = units // part
    number = len(pieces)
    tok = pieces[0].shape[0]
    rows = number * tok
    specs = [pl.BlockSpec((tok, part), lambda j: (0, j))] * (2 * number) + [
        pl.BlockSpec((part, width), lambda j: (j, 0)),
        pl.BlockSpec(memory_space=pl.ANY),
    ]
    ins = [slope for slope, _ in acts] + [silu for _, silu in acts] + [down, w_gu]
    outs = feed_call(
        feed_back_kernel, "feed_back", pieces, masks, total, ins, specs, earlier,
        (width, units, units), (steps, part), (0, number, [(rows, 2 * units), (width, 2 * units)]),
    )
    return outs[:3], outs[3:]


def owner_grad(h_all, d_act, sizes, rows, which, earlier):
    n_seq, n_hi, n_lo, n_core = sizes
    tokens, width = h_all.shape
    units = d_act.shape[1]
    cols = width // n_seq

    def kernel(h, d, *refs):
        product = t_dot(h[...], d[...]).astype(bf16)
        at = 0
        for hi in range(n_hi):
            for lo in range(n_lo):
                for core in range(n_core):
                    refs[-1][hi, core, 0, lo] = product[at : at + rows]
                    at += rows

    return pl.pallas_call(
        kernel,
        grid=(n_seq,),
        in_specs=[
            pl.BlockSpec((tokens, cols), lambda s: (0, s)),
            pl.BlockSpec((tokens, units), lambda s: (0, 0)),
        ]
        + [pl.BlockSpec(memory_space=pl.ANY)] * len(earlier),
        out_specs=pl.BlockSpec(
            (n_hi, n_core, 1, n_lo, rows, units), lambda s: (0, 0, s, 0, 0, which)
        ),
        out_shape=jax.ShapeDtypeStruct((n_hi, n_core, n_seq, n_lo, rows, 2 * units), bf16),
        input_output_aliases={2: 0} if earlier else {},
        compiler_params=pltpu.CompilerParams(vmem_limit_bytes=40 * 1024 * 1024),
        cost_estimate=pl.CostEstimate(
            flops=2 * tokens * width * units,
            bytes_accessed=2 * (tokens * width + tokens * units + width * units),
            transcendentals=0,
        ),
        name="owner_grad",
    )(h_all, d_act, *earlier)


def pack_columns(weights, count):
    rows, width = weights[0].shape
    part = width // count

    def kernel(*refs):
        for i, ref in enumerate(refs[:-1]):
            refs[-1][0, :, i * part : (i + 1) * part] = ref[...]

    return pl.pallas_call(
        kernel,
        grid=(count,),
        in_specs=[pl.BlockSpec((rows, part), lambda s: (0, s))] * len(weights),
        out_specs=pl.BlockSpec((1, rows, len(weights) * part), lambda s: (s, 0, 0)),
        out_shape=jax.ShapeDtypeStruct((count, rows, len(weights) * part), weights[0].dtype),
        name="pack_columns",
    )(*weights)


def unpack_columns(packed, number):
    count, rows, width = packed.shape
    part = width // number

    def kernel(ref, *outs):
        for i, out in enumerate(outs):
            out[...] = ref[0, :, i * part : (i + 1) * part].astype(f32)

    return pl.pallas_call(
        kernel,
        grid=(count,),
        in_specs=[pl.BlockSpec((1, rows, width), lambda s: (s, 0, 0))],
        out_specs=[pl.BlockSpec((rows, part), lambda s: (0, s))] * number,
        out_shape=[jax.ShapeDtypeStruct((rows, count * part), f32)] * number,
        name="unpack_columns",
    )(packed)


def unit_slices(sizes, unit):
    n_hi, n_lo, n_core = sizes
    return [
        (lo, (hi * n_core + core) * unit, ((hi * n_lo + lo) * n_core + core) * unit)
        for hi in range(n_hi)
        for lo in range(n_lo)
        for core in range(n_core)
    ]


def pack_units(gate, up, n_seq, sizes, unit):
    rows = gate.shape[0]
    n_hi, n_lo, n_core = sizes
    units = n_hi * n_core * unit

    def kernel(gate_ref, up_ref, out):
        for i, ref in enumerate((gate_ref, up_ref)):
            for lo, packed, plain in unit_slices(sizes, unit):
                start = i * units + packed
                out[lo, :, start : start + unit] = ref[:, plain : plain + unit]

    return pl.pallas_call(
        kernel,
        grid=(n_seq,),
        in_specs=[pl.BlockSpec((rows, units * n_lo), lambda s: (0, s))] * 2,
        out_specs=pl.BlockSpec((n_lo, rows, 2 * units), lambda s: (s, 0, 0)),
        out_shape=jax.ShapeDtypeStruct((n_seq * n_lo, rows, 2 * units), gate.dtype),
        name="pack_units",
    )(gate, up)


def unpack_units(packed, n_seq, sizes, unit):
    _, rows, width = packed.shape
    n_lo = sizes[1]
    units = width // 2

    def kernel(ref, *outs):
        for i, out in enumerate(outs):
            for lo, at, plain in unit_slices(sizes, unit):
                start = i * units + at
                out[:, plain : plain + unit] = ref[lo, :, start : start + unit].astype(f32)

    return pl.pallas_call(
        kernel,
        grid=(n_seq,),
        in_specs=[pl.BlockSpec((n_lo, rows, width), lambda s: (s, 0, 0))],
        out_specs=[pl.BlockSpec((rows, units * n_lo), lambda s: (0, s))] * 2,
        out_shape=[jax.ShapeDtypeStruct((rows, n_seq * n_lo * units), f32)] * 2,
        name="unpack_units",
    )(packed)


def finish_kernel(q_in, k_in, q_raw, k_raw, q_inv, k_inv, q_mean, k_mean, d_v, out):
    width = q_in.shape[1]
    for i, (grad, raw, inverse, mean) in enumerate(
        ((q_in, q_raw, q_inv, q_mean), (k_in, k_raw, k_inv, k_mean))
    ):
        normed = raw[...] * inverse[0]
        low = ((grad[...] - normed * mean[0]) * inverse[0]).astype(bf16)
        out[:, i * width : (i + 1) * width] = low
    out[:, 2 * width :] = d_v[...]


def row_specs(block, part):
    cols = lambda i: pl.BlockSpec((block, part), lambda b: (b, i))
    rows = lambda i: pl.BlockSpec((1, block, 1), lambda b: (i, b, 0))
    vector = pl.BlockSpec((1, part), lambda b: (0, 0))
    return cols, rows, vector


def finish(e_query, e_key, raw, inverse, means, d_value, part, block):
    length = raw.shape[0]
    cols, rows, _ = row_specs(block, part)
    return pl.pallas_call(
        finish_kernel,
        grid=(length // block,),
        in_specs=[cols(0), cols(0), cols(0), cols(1)] + [rows(0), rows(1)] * 2 + [cols(0)],
        out_specs=pl.BlockSpec((block, 3 * part), lambda b: (b, 0)),
        out_shape=jax.ShapeDtypeStruct((length, 3 * part), bf16),
        compiler_params=pltpu.CompilerParams(vmem_limit_bytes=56 * 1024 * 1024),
        name="finish",
    )(e_query, e_key, raw, raw, inverse, inverse, means, means, d_value)


def dot(left, right):
    return jnp.dot(left, right, preferred_element_type=f32)


def dot_t(left, right):
    return lax.dot_general(left, right, (((1,), (1,)), ((), ())), preferred_element_type=f32)


def t_dot(left, right):
    return lax.dot_general(left, right, (((0,), (0,)), ((), ())), preferred_element_type=f32)


def held(block):
    return lax.optimization_barrier(block)


def rope_tables(positions, head_dim):
    half_dim = head_dim // 2
    frequency = rope_base ** (-(jnp.arange(half_dim, dtype=f32) * 2.0 / head_dim))
    angles = positions.astype(f32)[:, None] * frequency[None, :]
    cosine, sine = jnp.cos(angles), jnp.sin(angles)
    return jnp.concatenate([cosine, cosine], 1), jnp.concatenate([-sine, sine], 1)


def rms(values):
    inverse = lax.rsqrt(jnp.mean(values * values, axis=-1, keepdims=True) + norm_eps)
    return values * inverse, inverse


def rms_back(grad, normed, inverse, gain):
    scaled = grad * gain
    return (scaled - normed * jnp.mean(scaled * normed, axis=-1, keepdims=True)) * inverse


def per_device(
    tokens,
    segment_ids,
    w_query,
    w_key,
    w_value,
    w_out,
    w_gate,
    w_up,
    w_down,
    query_gain,
    key_gain,
    attn_gain,
    ff_gain,
    cotangent,
):
    inputs = tokens[0]
    tok, width = inputs.shape
    n_seq, n_hi, n_lo, n_core = (lax.axis_size(a) for a in ("seq", "zhi", "zlo", "core"))
    n_dev = n_seq * n_hi * n_lo * n_core
    seq = lax.axis_index("seq")
    heads = HEADS // n_seq
    head_dim = width // HEADS
    part = width // n_seq
    length = n_seq * tok
    d_rows = w_query.shape[0]
    ff_rows = w_down.shape[0]
    units = ff_rows * n_hi * n_core

    sizes = (n_hi, n_lo, n_core)
    seq_dims = dims_of("seq")
    lo_dims, hi_dims, core_dims = dims_of("zlo"), dims_of("zhi"), dims_of("core")
    cube_dims = seq_dims + lo_dims
    z_dims = lo_dims + hi_dims
    all_dims = core_dims + lo_dims + hi_dims + seq_dims
    z_axes = ("zhi", "zlo", "core")
    rows_of = lambda block, m: block[m * tok : (m + 1) * tok]

    pair_axes = ("zhi", "core")
    core_swap = lambda piece: swap(piece, core_dims[0])
    lo_order = [
        ((hi * n_core + core) * n_seq + s) * n_lo + lo
        for s in range(n_seq)
        for hi in range(n_hi)
        for lo in range(n_lo)
        for core in range(n_core)
    ]
    hi_order = [lo_order.index(i) for i in range(len(lo_order))]

    tables = rope_tables(jnp.arange(length, dtype=jnp.int32), head_dim)

    qkv_mine = pack_columns((w_query, w_key, w_value), n_seq)
    gains = jnp.stack([query_gain, key_gain, attn_gain, ff_gain])[None]
    gains = gather_row(after(gains, qkv_mine), core_dims + z_dims)
    gains = jnp.transpose(gains, (1, 0, 2)).reshape(1, 4 * part)
    qkv_mine = lax.all_to_all(qkv_mine, "seq", 0, 0, tiled=True).reshape(n_seq * d_rows, 3 * part)
    gu_mine = pack_units(w_gate, w_up, n_seq, sizes, ff_rows)
    qkv_mine, gains, gu_mine = tie(qkv_mine, gains, gu_mine)

    out_mine = jnp.concatenate([w_out[:, i * part : (i + 1) * part] for i in range(n_seq)], axis=0)
    w_z = Spread(jnp.concatenate([qkv_mine, out_mine], axis=1), z_dims).step()
    to_width = lambda row: jnp.pad(row, ((0, 0), (0, width - row.shape[1])))
    ids = to_width(segment_ids.astype(bf16))
    more = jnp.concatenate([ids, to_width(gains), jnp.zeros((14, width), bf16)], axis=0)
    x_spread = Spread(jnp.concatenate([inputs, more], axis=0), seq_dims).step()
    x_pieces = x_spread.whole()
    tables, *x_pieces = tie(w_z, tables, *x_pieces)
    w_sib = [core_swap(piece) for piece in (w_z.pieces[0], *w_z.fresh())]
    early = len(w_sib)
    w_z.step()
    small = after(x_pieces, w_z.fresh())
    row_ids = jnp.concatenate([piece[tok, :tok] for piece in small]).astype(jnp.int32)
    row_ids = row_ids.reshape(length, 1)
    col_ids = jnp.stack(
        [lax.dynamic_slice(row_ids, ((seq ^ m) * tok, 0), (tok, 1)) for m in range(n_seq)]
    ).reshape(n_seq, 1, tok)
    all_gains = jnp.concatenate([piece[tok + 1 : tok + 2, : 4 * part] for piece in small], axis=0)
    all_gains = jnp.concatenate(
        [lax.dynamic_slice(all_gains, (seq ^ m, 0), (1, 4 * part)) for m in range(n_seq)], axis=0
    ).reshape(n_seq, 4, part)
    all_gains = jnp.transpose(all_gains, (1, 0, 2)).reshape(4, width).astype(f32)
    my_gains = gains.reshape(4, 1, part).astype(f32)
    qk_gains = (my_gains[0], my_gains[1])
    (w_sib,) = tie(w_z, w_sib)
    gain_attn, gain_ff = all_gains[2], all_gains[3]
    w_z = w_z.whole()
    w_sib = w_sib + [core_swap(piece) for piece in w_z[early:]]

    gu_mine = lax.all_to_all(after(gu_mine, w_z), ("seq", "zlo"), 0, 0, tiled=True)

    raw, squares, x_all, w_qkv, out_weight = project(
        x_pieces,
        [piece.reshape(n_seq, d_rows, 4 * part) for piece in w_z + w_sib],
        block_starts(
            n_seq,
            d_rows,
            z_dims + core_dims,
            z_axes,
            lambda s, hi, lo, core: ((s * n_hi + hi) * n_lo + lo) * n_core + core,
        ),
        block_starts(
            1,
            d_rows,
            z_dims + core_dims,
            z_axes,
            lambda block, hi, lo, core: (hi * n_lo + lo) * n_core + core,
        ),
        tok,
        part,
    )
    squares, gu_mine = tie(squares, gu_mine)
    w_gu = lax.all_gather(gu_mine, pair_axes, axis=0, tiled=True)
    squares = squares.reshape(2, n_seq, tok)
    squares = sum_all(jnp.transpose(squares, (1, 0, 2)), seq_dims)
    inverse = lax.rsqrt(jnp.transpose(squares, (1, 0, 2)).reshape(2, length, 1) / width + norm_eps)

    context = (seq.astype(jnp.int32).reshape(1), raw, inverse, qk_gains, tables, (row_ids, col_ids))
    attended, attn_low, log_total = attend(context, heads, tok)
    branch = Collect(
        [held(dot(rows_of(attn_low, m), out_weight).astype(bf16)) for m in range(n_seq)], seq_dims
    ).whole()
    branch_norm, branch_inv = rms(branch)
    hidden = inputs.astype(f32) + branch_norm * gain_attn
    hidden_low = hidden.astype(bf16)

    w_gu = regroup(w_gu.reshape(-1, d_rows, 2 * units), lo_order)
    total = 1 << len(cube_dims)
    by_bits = lambda size: [
        m for m in range(total) if bin(m).count("1") == size or (size == 1 and m == 0)
    ]
    fours = lambda masks: [masks[i : i + 4] for i in range(0, len(masks), 4)]
    groups = [masks for size in range(1, len(cube_dims) + 1) for masks in fours(by_bits(size))]
    light = total == 8
    h_spread = Spread(hidden_low, cube_dims, spare_last=light).step()
    if light:
        h_spread.step()
        near = [h_spread.pieces[m] for m in (1, 2, 3)]
        near, w_gu = tie(near, w_gu)
        h_spread.pieces.update(zip((1, 2, 3), near, strict=True))
    acts, partials, kept = {}, {}, ()
    order = [[0, 1], [2, 3], [4, 5, 6], [7]] if light else groups
    for i, masks in enumerate(order):
        while any(m not in h_spread.pieces for m in masks):
            h_spread.step()
        pieces = [h_spread.pieces[m] for m in masks]
        kept, act = feed(pieces, masks, total, w_gu, kept)
        if i == 0:
            last = h_spread.pieces[total // 2] = after(h_spread.pieces[total // 2], act)
            down = lax.all_gather(after(w_down, last), pair_axes, axis=0, tiled=True)
        if light and i == 1:
            (act,) = tie(h_spread.step(), act)
        acts.update(zip(masks, act, strict=True))
    h_all, middle_all = kept
    for masks in fours(sorted(range(total), key=lambda m: -bin(m).count("1"))):
        sums = feed_down(middle_all, masks, tok, down)
        partials.update(zip(masks, sums, strict=True))
    partials = [partials[m] for m in range(total)]
    ff_raw = Collect(partials, cube_dims).whole()
    ff_norm, ff_inv = rms(ff_raw)
    mixed = (hidden + ff_norm * gain_ff).astype(bf16)

    grad_output = cotangent[0].astype(f32)
    grad_ff_gain = jnp.sum(grad_output * ff_norm, axis=0)
    d_ff = rms_back(grad_output, ff_norm, ff_inv, gain_ff).astype(bf16)
    d_spread = Spread(d_ff, cube_dims).step()
    partials, kept = {}, ()
    for masks in groups:
        while any(m not in d_spread.pieces for m in masks):
            d_spread.step()
        pieces = [d_spread.pieces[m] for m in masks]
        act = [acts[m] for m in masks]
        kept, sums = feed_back(pieces, masks, total, act, w_gu, down, kept)
        partials.update(zip(masks, sums, strict=True))
    d_ff_all, d_gate_all, d_up_all = kept
    partials = [partials[m] for m in range(total)]
    d_hidden = Collect(partials, cube_dims).step()

    owned = lambda grad: lax.psum_scatter(grad, pair_axes, scatter_dimension=0, tiled=True)
    grad_down = t_dot(middle_all, after(d_ff_all, partials)).astype(bf16)
    (grad_down,) = tie(d_hidden, grad_down)
    grad_down = owned(grad_down)
    order = (n_seq, n_hi, n_lo, n_core)
    d_hidden.step()
    grad_gu = owner_grad(h_all, d_gate_all, order, d_rows, 0, [])
    (grad_gu,) = tie(d_hidden, grad_gu)
    d_hidden.step()
    grad_gu = owner_grad(h_all, after(d_up_all, grad_gu), order, d_rows, 1, [grad_gu])
    (grad_gu,) = tie(d_hidden, grad_gu)
    grad_gu = owned(grad_gu.reshape(-1, d_rows, 2 * units))
    d_hidden = d_hidden.whole()

    d_hidden = grad_output + d_hidden
    grad_attn_gain = jnp.sum(d_hidden * branch_norm, axis=0)
    d_branch = rms_back(d_hidden, branch_norm, branch_inv, gain_attn).astype(bf16)
    d_branch_pieces = Spread(d_branch, seq_dims).whole()
    d_branch_pieces, grad_down = tie(d_branch_pieces, grad_down)
    d_attended = jnp.concatenate(
        [dot_t(piece, out_weight).astype(bf16) for piece in d_branch_pieces], axis=0
    )
    e_query, e_key, d_value, q_sum, k_sum, grad_query_gain, grad_key_gain = attend_back(
        context, d_attended, attended, log_total, heads, tok
    )
    means = jnp.stack([q_sum[0], k_sum[0]]).reshape(2, n_seq, tok)
    means = sum_all(jnp.transpose(means, (1, 0, 2)), seq_dims)
    means = jnp.transpose(means, (1, 0, 2)).reshape(2, length, 1) / width

    n_z = n_hi * n_lo
    z_blocks = lambda grad: take_blocks(
        jnp.transpose(
            grad.reshape(n_seq, n_hi, n_lo, n_core, d_rows, grad.shape[1]), (1, 2, 3, 0, 4, 5)
        ),
        z_dims + core_dims,
        z_axes,
    )
    def to_core(grad):
        blocks = z_blocks(grad)
        theirs = [core_swap(piece) for piece in blocks[n_z:]]
        return [
            add_low(a, b).reshape(-1, a.shape[-1]) for a, b in zip(blocks[:n_z], theirs, strict=True)
        ]

    d_qkv = finish(e_query, e_key, raw, inverse, means, d_value, part, tok)
    grad_qkv = t_dot(x_all, d_qkv).astype(bf16)
    back = lambda rows, m: held(dot_t(rows_of(rows, m), w_qkv).astype(bf16))
    far = back(after(d_qkv, grad_qkv), n_seq - 1)
    grad_qkv, far, low_rows = tie(to_core(grad_qkv), far, d_qkv)
    grad_qkv = Collect(grad_qkv, z_dims).step()
    low_rows, far = tie(grad_qkv, low_rows, far)
    low_rows, far = tie(grad_qkv.ready(), low_rows, far)
    grad_qkv.step()
    input_grad = Collect([back(low_rows, m) for m in range(n_seq - 1)] + [far], seq_dims)
    input_grad.step()
    full_row = lambda cols: lax.dynamic_update_slice(jnp.zeros((width,), f32), cols, (seq * part,))
    rows = jnp.stack(
        [full_row(grad_query_gain[0]), full_row(grad_key_gain[0]), grad_attn_gain, grad_ff_gain]
    )
    rows = jnp.transpose(rows.reshape(4, n_dev, d_rows), (1, 0, 2))
    grad_gu = after(grad_gu, low_rows).reshape(n_seq * n_lo, d_rows, 2 * units)
    grad_gu = lax.all_to_all(grad_gu, ("seq", "zlo"), 0, 0, tiled=True)
    d_branch_all = jnp.concatenate(after(d_branch_pieces, low_rows), axis=0)
    grad_out = t_dot(attn_low, d_branch_all).astype(bf16)
    grad_out = jnp.concatenate([grad_out[:, i * part : (i + 1) * part] for i in range(n_seq)], axis=0)
    grad_out, grad_gu = tie(grad_qkv, input_grad, to_core(grad_out), grad_gu)
    input_grad.step()
    grad_qkv = grad_qkv.whole().astype(bf16).reshape(n_seq, d_rows, 3 * part)
    grad_qkv = lax.all_to_all(grad_qkv, "seq", 0, 0, tiled=True)
    grad_out = Collect(grad_out, z_dims).step()
    rows = lax.all_to_all(after(rows, grad_qkv), ("seq",) + z_axes, 0, 0, tiled=True)
    input_grad = d_hidden + input_grad.whole()
    grad_down = after(grad_down, grad_qkv).astype(f32)
    grad_out = grad_out.whole().reshape(n_seq, d_rows, part)
    grad_gate, grad_up = unpack_units(grad_gu, n_seq, sizes, ff_rows)
    grad_query, grad_key, grad_value = unpack_columns(grad_qkv, 3)
    rows = jnp.sum(rows, axis=0)
    grad_out = jnp.concatenate([grad_out[i] for i in range(n_seq)], axis=1)

    return (
        mixed[None],
        input_grad[None],
        grad_query,
        grad_key,
        grad_value,
        grad_out,
        grad_gate,
        grad_up,
        grad_down,
        rows[0],
        rows[1],
        rows[2],
        rows[3],
    )


def solution(mesh):
    n_seq, n_row = mesh.shape["seq"], mesh.shape["row"]
    n_core = 2
    n_lo = 2
    n_hi = n_row // (n_core * n_lo)
    cut = Mesh(
        mesh.devices.reshape(n_seq, n_hi, n_lo, n_core), ("seq", "zhi", "zlo", "core")
    )
    row = ("zhi", "zlo", "core")
    every = ("seq",) + row
    acts = P(row, "seq", None)
    matrix = P(every, None)
    vector = P(every)
    return jax.shard_map(
        per_device,
        mesh=cut,
        in_specs=(acts, P(row, "seq")) + (matrix,) * 7 + (vector,) * 4 + (acts,),
        out_specs=(acts, acts) + (matrix,) * 7 + (vector,) * 4,
        check_vma=False,
    )
```

```python
import functools
import math

import jax
import jax.numpy as jnp
from jax import lax
from jax.experimental import pallas as pl
from jax.experimental.pallas import tpu as pltpu
from jax.sharding import Mesh
from jax.sharding import PartitionSpec as P

HEADS = 16

rope_base = 500000.0
norm_eps = 1e-06
masked_score = -1e30

bf16 = jnp.bfloat16
f32 = jnp.float32


def dims_of(axis):
    count = lax.axis_size(axis)
    return [(axis, 1 << bit) for bit in range(count.bit_length() - 1)]


def swap(block, dim):
    axis, mask = dim
    return lax.ppermute(block, axis, [(i, i ^ mask) for i in range(lax.axis_size(axis))])


def partner_index(dims, which):
    masks = {}
    for bit, (axis, mask) in enumerate(dims):
        if which >> bit & 1:
            masks[axis] = masks.get(axis, 0) | mask
    return masks


def column_cuts(width, count):
    tiles = width // 128
    return [round(tiles * i / count) * 128 for i in range(count + 1)]


def column_parts(block, count):
    cuts = column_cuts(block.shape[1], count)
    return [block[:, cuts[i] : cuts[i + 1]] for i in range(count)]


def route(which, count):
    bits = [i for i in range(count) if which >> i & 1]
    if len(bits) == 1:
        return bits[0]
    return bits[0] if bits[1] - bits[0] == 1 else bits[1]


def by_size(count):
    return sorted(range(1, 1 << count), key=lambda m: bin(m).count("1"))


class Spread:
    def __init__(self, block, dims, spare_last=False):
        self.dims, self.size, self.pieces, self.new = dims, 0, {0: block}, [0]
        self.spare_last = spare_last and len(dims) == 3

    def light_step(self):
        x, y, _ = self.dims
        half = lambda m, i: column_parts(self.pieces[m], 2)[i]
        if self.size == 2:
            self.new = [3]
            self.pieces[3] = jnp.concatenate([swap(half(2, 0), x), swap(half(1, 1), y)], axis=1)
        elif self.size == 3:
            self.new = [5, 6]
            self.pieces[5], self.pieces[6] = swap(self.pieces[4], x), swap(self.pieces[4], y)
        else:
            self.new = [7]
            self.pieces[7] = jnp.concatenate([swap(half(6, 0), x), swap(half(5, 1), y)], axis=1)

    def step(self):
        self.size += 1
        count = len(self.dims)
        if self.spare_last and self.size > 1:
            self.light_step()
            return self
        self.new = [m for m in by_size(count) if bin(m).count("1") == self.size]
        for which in self.new:
            if self.size == count and count > 1:
                parts = [
                    swap(column_parts(self.pieces[which ^ (1 << i)], count)[i], self.dims[i])
                    for i in range(count)
                ]
                self.pieces[which] = jnp.concatenate(parts, axis=1)
            else:
                via = route(which, count)
                self.pieces[which] = swap(self.pieces[which ^ (1 << via)], self.dims[via])
        return self

    def fresh(self):
        return [self.pieces[m] for m in self.new]

    def renew(self, values):
        self.pieces.update(zip(self.new, values, strict=True))

    def whole(self):
        while self.size < len(self.dims):
            self.step()
        return [self.pieces[m] for m in range(1 << len(self.dims))]


class Collect:
    def __init__(self, pieces, dims):
        self.dims, self.size, self.pieces = dims, len(dims), list(pieces)
        self.got, self.new = {m: [] for m in range(len(self.pieces))}, []
        self.sums = None

    def ready(self):
        masks = [m for m in by_size(len(self.dims)) if bin(m).count("1") == self.size]
        self.sums = {m: self.total(m) for m in masks}
        return self

    def step(self):
        count = len(self.dims)
        if self.sums is None:
            self.ready()
        sums, self.sums, self.new = self.sums, None, []
        for which, total in sums.items():
            if self.size == count and count > 1:
                for i, cols in enumerate(column_parts(total, count)):
                    self.keep(which ^ (1 << i), i, swap(cols, self.dims[i]))
            else:
                via = route(which, count)
                self.keep(which ^ (1 << via), None, swap(total, self.dims[via]))
        self.size -= 1
        return self

    def keep(self, which, part, arrived):
        self.new.append((which, len(self.got[which])))
        self.got[which].append((part, arrived))

    def total(self, which):
        if not self.got[which]:
            return self.pieces[which]
        count = len(self.dims)
        total = self.pieces[which].astype(f32)
        for part, arrived in self.got[which]:
            if part is None:
                total = total + arrived.astype(f32)
            else:
                cols = column_parts(total, count)
                cols[part] = cols[part] + arrived.astype(f32)
                total = jnp.concatenate(cols, axis=1)
        return total.astype(bf16)

    def fresh(self):
        if self.sums is not None:
            return list(self.sums.values())
        return [self.got[which][i][1] for which, i in self.new]

    def renew(self, values):
        if self.sums is not None:
            self.sums = dict(zip(self.sums, values, strict=True))
            return
        for (which, i), value in zip(self.new, values, strict=True):
            self.got[which][i] = (self.got[which][i][0], value)

    def whole(self):
        while self.size > 0:
            self.step()
        total = self.pieces[0].astype(f32)
        for _, arrived in self.got[0]:
            total = total + arrived.astype(f32)
        return total


def tie(*items):
    steps = (Spread, Collect)
    values = [item.fresh() if isinstance(item, steps) else item for item in items]
    values = lax.optimization_barrier(values)
    rest = []
    for item, value in zip(items, values, strict=True):
        if isinstance(item, steps):
            item.renew(value)
        else:
            rest.append(value)
    return rest


def sum_all(table, dims):
    for bit, dim in enumerate(dims):
        there = swap(table, dim)
        order = [m ^ (1 << bit) for m in range(table.shape[0])]
        table = table + jnp.stack([there[m] for m in order])
    return table


def after(block, *earlier):
    return lax.optimization_barrier((block, earlier))[0]


def block_starts(blocks, rows, dims, axes, order):
    starts = []
    for m in range(1 << len(dims)):
        masks = partner_index(dims, m)
        at = [lax.axis_index(a) ^ masks.get(a, 0) for a in axes]
        starts += [order(block, *at) * rows for block in range(blocks)]
    return jnp.stack(starts).astype(jnp.int32)


def project(x_pieces, w_pieces, starts, out_starts, tok, part):
    n_x, n_w = len(x_pieces), len(w_pieces)
    width = x_pieces[0].shape[1]
    blocks, rows, _ = w_pieces[0].shape
    length = n_x * tok
    number = n_w * blocks

    def kernel(table, out_table, *refs):
        xs, ws = refs[:n_x], refs[n_x : n_x + n_w]
        raw, squares, x_out, w_out, o_out, x_all, w_all, o_all, sems = refs[n_x + n_w :]
        at = pl.program_id(0)
        arrive, later = [], []
        for i in range(n_x):
            source, target = xs[i].at[pl.ds(0, tok)], x_all.at[pl.ds(i * tok, tok)]
            arrive.append(pltpu.make_async_copy(source, target, sems.at[i]))
        for i in range(number):
            piece, block = ws[i // blocks], i % blocks
            here = pl.ds(pl.multiple_of(table[i], rows), rows)
            source = piece.at[block, :, pl.ds(0, 3 * part)]
            arrive.append(pltpu.make_async_copy(source, w_all.at[here], sems.at[n_x + i]))
            here = pl.ds(pl.multiple_of(out_table[i // blocks], rows), rows)
            source = piece.at[block, :, pl.ds(3 * part, part)]
            target = o_all.at[here, pl.ds(block * part, part)]
            later.append(pltpu.make_async_copy(source, target, sems.at[n_x + number + i]))
        sem = n_x + 2 * number
        keep = [
            pltpu.make_async_copy(x_all, x_out, sems.at[sem]),
            pltpu.make_async_copy(w_all, w_out, sems.at[sem + 1]),
        ]
        keep_out = pltpu.make_async_copy(o_all, o_out, sems.at[sem + 2])

        @pl.when(at == 0)
        def _():
            for copy in arrive + later:
                copy.start()
            for copy in arrive:
                copy.wait()
            for copy in keep:
                copy.start()

        for step in range(3):

            @pl.when(at == step)
            def _(step=step):
                product = dot(x_all[...], w_all[:, step * part : (step + 1) * part])
                raw[...] = product
                if step < 2:
                    squares[0] = jnp.sum(product * product, axis=-1, keepdims=True)
                if step == 0:
                    for copy in later:
                        copy.wait()
                    keep_out.start()

        @pl.when(at == 2)
        def _():
            for copy in keep + [keep_out]:
                copy.wait()

    somewhere = pl.BlockSpec(memory_space=pl.ANY)
    scalars = pl.BlockSpec(memory_space=pltpu.SMEM)
    return pl.pallas_call(
        kernel,
        grid=(3,),
        in_specs=[scalars] * 2 + [somewhere] * (n_x + n_w),
        out_specs=[
            pl.BlockSpec((length, part), lambda j: (0, j)),
            pl.BlockSpec((1, length, 1), lambda j: (jnp.minimum(j, 1), 0, 0)),
            somewhere,
            somewhere,
            somewhere,
        ],
        out_shape=[
            jax.ShapeDtypeStruct((length, 3 * part), f32),
            jax.ShapeDtypeStruct((2, length, 1), f32),
            jax.ShapeDtypeStruct((length, width), bf16),
            jax.ShapeDtypeStruct((width, 3 * part), bf16),
            jax.ShapeDtypeStruct((n_w * rows, blocks * part), bf16),
        ],
        scratch_shapes=[
            pltpu.VMEM((length, width), bf16),
            pltpu.VMEM((width, 3 * part), bf16),
            pltpu.VMEM((n_w * rows, blocks * part), bf16),
            pltpu.SemaphoreType.DMA((n_x + 2 * number + 3,)),
        ],
        compiler_params=pltpu.CompilerParams(vmem_limit_bytes=56 * 1024 * 1024),
        cost_estimate=pl.CostEstimate(
            flops=6 * length * width * part, bytes_accessed=20 * length * part, transcendentals=0
        ),
        name="project",
    )(starts, out_starts, *x_pieces, *w_pieces)


def regroup(blocks, order):
    number, rows, width = blocks.shape
    group = math.gcd(number, 8)

    def kernel(ref, out, held, sems):
        arrive = [
            pltpu.make_async_copy(ref.at[at], held.at[pl.ds(i * rows, rows)], sems.at[i])
            for i, at in enumerate(order)
        ]
        leave = []
        for i in range(0, number, group):
            here = pl.ds(i * rows, group * rows)
            sem = sems.at[number + i // group]
            leave.append(pltpu.make_async_copy(held.at[here], out.at[here], sem))
        for copy in arrive:
            copy.start()
        for i, copy in enumerate(leave):
            for piece in arrive[i * group : (i + 1) * group]:
                piece.wait()
            copy.start()
        for copy in leave:
            copy.wait()

    return pl.pallas_call(
        kernel,
        in_specs=[pl.BlockSpec(memory_space=pl.ANY)],
        out_specs=pl.BlockSpec(memory_space=pl.ANY),
        out_shape=jax.ShapeDtypeStruct((number * rows, width), blocks.dtype),
        scratch_shapes=[
            pltpu.VMEM((number * rows, width), blocks.dtype),
            pltpu.SemaphoreType.DMA((number + number // group,)),
        ],
        compiler_params=pltpu.CompilerParams(vmem_limit_bytes=56 * 1024 * 1024),
        name="regroup",
    )(blocks)


def take_blocks(whole, dims, axes):
    shape = whole.shape[len(axes) :]
    pieces = []
    for m in range(1 << len(dims)):
        masks = partner_index(dims, m)
        at = tuple(lax.axis_index(a) ^ masks.get(a, 0) for a in axes)
        piece = lax.dynamic_slice(whole, at + (0,) * len(shape), (1,) * len(axes) + shape)
        pieces.append(piece.reshape(shape))
    return pieces


def add_low(kept, arrived):
    return (kept.astype(f32) + arrived.astype(f32)).astype(bf16)


def gather_row(row, dims):
    for axis, mask in dims:
        there = swap(row, (axis, mask))
        low = (lax.axis_index(axis) & mask) == 0
        row = jnp.concatenate([jnp.where(low, row, there), jnp.where(low, there, row)], axis=0)
    return row


def turned(raw, inverse, gain, cosine, sine):
    scaled = raw * inverse * gain
    return scaled * cosine + pltpu.roll(scaled, scaled.shape[1] // 2, 1) * sine


def turned_back(grad, raw, inverse, gain, cosine, sine):
    back = grad * cosine - pltpu.roll(grad, grad.shape[1] // 2, 1) * sine
    product = back * (raw * inverse)
    return back * gain, jnp.sum(product * gain, -1, keepdims=True), jnp.sum(product, 0, keepdims=True)


def block_scores(scale, last, a, j, k, q, key_ids, query_ids):
    scores = dot_t(k, q) * scale
    allowed = None
    if j == 0 or a == last:
        allowed = key_ids == query_ids
    if j == a:
        shape = scores.shape
        causal = lax.broadcasted_iota(jnp.int32, shape, 0) <= lax.broadcasted_iota(jnp.int32, shape, 1)
        allowed = causal if allowed is None else allowed & causal
    return scores if allowed is None else jnp.where(allowed, scores, masked_score)


def forward_kernel(
    scale, count, tok, place, q_raw, k_raw, v_raw, q_inv, k_inv, q_gain, k_gain, cosine, sine,
    row_ids, col_ids, out, low, log_total, k_all, v_across,
):
    rows = lambda j: pl.ds(pl.multiple_of((place[0] ^ j) * tok, tok), tok)
    cols = lambda j: slice(j * tok, (j + 1) * tok)
    for a in range(count):
        here = rows(a)
        table = (cosine[cols(a), :], sine[cols(a), :])
        k_all[cols(a), :] = turned(k_raw[here, :], k_inv[0, here, :], k_gain[...], *table).astype(bf16)
        v_across[:, cols(a)] = v_raw[here, :].T.astype(bf16)
        q = turned(q_raw[here, :], q_inv[0, here, :], q_gain[...], *table).astype(bf16)
        scores = [
            block_scores(scale, count - 1, a, j, k_all[cols(j), :], q, row_ids[rows(j), :], col_ids[a])
            for j in range(a + 1)
        ]
        top = jnp.max(functools.reduce(jnp.maximum, scores), axis=0, keepdims=True)
        expo = [jnp.exp2(block - top) for block in scores]
        total = jnp.sum(functools.reduce(jnp.add, expo), axis=0, keepdims=True)
        parts = [dot(v_across[:, cols(j)], expo[j].astype(bf16)) for j in range(a + 1)]
        attended = (functools.reduce(jnp.add, parts) * (1.0 / total)).T
        out[here, :] = attended
        low[here, :] = attended.astype(bf16)
        log_total[0, place[0] ^ a] = top + jnp.log2(total)


def backward_kernel(
    scale, plain_scale, count, tok, place, q_raw, k_raw, v_raw, q_inv, k_inv, q_gain, k_gain,
    cosine, sine, row_ids, col_ids, d_out, out, log_total,
    e_q, e_k, d_v, q_sum, k_sum, q_gain_grad, k_gain_grad, k_all, k_across, v_all, d_k_all, d_v_all,
):
    rows = lambda j: pl.ds(pl.multiple_of((place[0] ^ j) * tok, tok), tok)
    cols = lambda j: slice(j * tok, (j + 1) * tok)
    q_gain_grad[...] = jnp.zeros_like(q_gain_grad)

    @pl.when(pl.program_id(0) == 0)
    def _():
        q_sum[...] = jnp.zeros_like(q_sum)
        k_sum[...] = jnp.zeros_like(k_sum)

    for a in range(count):
        here = rows(a)
        table = (cosine[cols(a), :], sine[cols(a), :])
        k = turned(k_raw[here, :], k_inv[0, here, :], k_gain[...], *table)
        k_all[cols(a), :] = k.astype(bf16)
        k_across[:, cols(a)] = k.T.astype(bf16)
        v_all[cols(a), :] = v_raw[here, :].astype(bf16)
        q_row, inverse = q_raw[here, :], q_inv[0, here, :]
        q = turned(q_row, inverse, q_gain[...], *table).astype(bf16)
        d_blk = d_out[here, :]
        row_dot = jnp.sum(d_blk.astype(f32) * out[here, :], axis=-1, keepdims=True)
        row_dot = jnp.broadcast_to(row_dot, q_row.shape).T[0:1, :]
        log_row = log_total[0, place[0] ^ a]
        d_q = []
        for j in range(a + 1):
            scores = block_scores(
                scale, count - 1, a, j, k_all[cols(j), :], q, row_ids[rows(j), :], col_ids[a]
            )
            probability = jnp.exp2(scores - log_row)
            d_prob = dot_t(v_all[cols(j), :], d_blk)
            d_scores = (probability * (d_prob - row_dot)).astype(bf16)
            d_q.append(dot(k_across[:, cols(j)], d_scores))
            d_k = dot(d_scores, q)
            d_v_part = dot(probability.astype(bf16), d_blk)
            if j == a:
                d_k_all[cols(j), :] = d_k
                d_v_all[cols(j), :] = d_v_part
            else:
                d_k_all[cols(j), :] += d_k
                d_v_all[cols(j), :] += d_v_part
        e_q[here, :], row_sum, gain_grad = turned_back(
            functools.reduce(jnp.add, d_q).T * plain_scale, q_row, inverse, q_gain[...], *table
        )
        q_sum[0, here, :] += row_sum
        q_gain_grad[...] += gain_grad
    k_gain_grad[...] = jnp.zeros_like(k_gain_grad)
    for j in range(count):
        here = rows(j)
        e_k[here, :], row_sum, gain_grad = turned_back(
            d_k_all[cols(j), :] * plain_scale, k_raw[here, :], k_inv[0, here, :],
            k_gain[...], cosine[cols(j), :], sine[cols(j), :],
        )
        k_sum[0, here, :] += row_sum
        k_gain_grad[...] += gain_grad
        d_v[here, :] = d_v_all[cols(j), :].astype(bf16)


def attention_specs(tokens, block, heads, head_dim):
    head = lambda i: pl.BlockSpec((tokens, head_dim), lambda h, s: (0, i * heads + h))
    whole = lambda shape: pl.BlockSpec(shape, lambda h, s: (0,) * len(shape))
    vector = pl.BlockSpec((1, head_dim), lambda h, s: (0, h))
    inverse = lambda i: pl.BlockSpec((1, tokens, 1), lambda h, s: (i, 0, 0))
    inputs = [head(0), head(1), head(2), inverse(0), inverse(1), vector, vector]
    inputs += [whole((tokens, head_dim))] * 2
    inputs += [whole((tokens, 1)), whole((tokens // block, 1, block))]
    logs = pl.BlockSpec((1, tokens // block, 1, block), lambda h, s: (h, 0, 0, 0))
    return inputs, head(0), logs, vector


def attend(context, heads, block):
    place, raw, inverse, gains, tables, ids = context
    tokens, width = raw.shape[0], raw.shape[1] // 3
    head_dim = width // heads
    inputs, head, logs, _ = attention_specs(tokens, block, heads, head_dim)
    return pl.pallas_call(
        functools.partial(forward_kernel, head_dim**-0.5 * math.log2(math.e), tokens // block, block),
        grid_spec=pltpu.PrefetchScalarGridSpec(
            num_scalar_prefetch=1,
            grid=(heads,),
            in_specs=inputs,
            out_specs=[head, head, logs],
            scratch_shapes=[
                pltpu.VMEM((tokens, head_dim), bf16),
                pltpu.VMEM((head_dim, tokens), bf16),
            ],
        ),
        out_shape=[
            jax.ShapeDtypeStruct((tokens, width), f32),
            jax.ShapeDtypeStruct((tokens, width), bf16),
            jax.ShapeDtypeStruct((heads, tokens // block, 1, block), f32),
        ],
        compiler_params=pltpu.CompilerParams(vmem_limit_bytes=40 * 1024 * 1024),
        cost_estimate=pl.CostEstimate(
            flops=2 * tokens * tokens * width,
            bytes_accessed=18 * tokens * width,
            transcendentals=heads * tokens * tokens // 2,
        ),
        name="attend",
    )(place, raw, raw, raw, inverse, inverse, *gains, *tables, *ids)


def attend_back(context, d_out, out, log_total, heads, block):
    place, raw, inverse, gains, tables, ids = context
    tokens, width = raw.shape[0], raw.shape[1] // 3
    head_dim = width // heads
    inputs, head, logs, vector = attention_specs(tokens, block, heads, head_dim)
    sums = pl.BlockSpec((1, tokens, 1), lambda h, s: (0, 0, 0))
    scale = head_dim**-0.5
    return pl.pallas_call(
        functools.partial(
            backward_kernel, scale * math.log2(math.e), scale, tokens // block, block
        ),
        grid_spec=pltpu.PrefetchScalarGridSpec(
            num_scalar_prefetch=1,
            grid=(heads,),
            in_specs=inputs + [head, head, logs],
            out_specs=[head, head, head, sums, sums, vector, vector],
            scratch_shapes=[
                pltpu.VMEM((tokens, head_dim), bf16),
                pltpu.VMEM((head_dim, tokens), bf16),
                pltpu.VMEM((tokens, head_dim), bf16),
                pltpu.VMEM((tokens, head_dim), f32),
                pltpu.VMEM((tokens, head_dim), f32),
            ],
        ),
        out_shape=[
            jax.ShapeDtypeStruct((tokens, width), f32),
            jax.ShapeDtypeStruct((tokens, width), f32),
            jax.ShapeDtypeStruct((tokens, width), bf16),
        ]
        + [jax.ShapeDtypeStruct((1, tokens, 1), f32)] * 2
        + [jax.ShapeDtypeStruct((1, width), f32)] * 2,
        compiler_params=pltpu.CompilerParams(vmem_limit_bytes=56 * 1024 * 1024),
        cost_estimate=pl.CostEstimate(
            flops=5 * tokens * tokens * width,
            bytes_accessed=30 * tokens * width,
            transcendentals=heads * tokens * tokens // 2,
        ),
        name="attend_back",
    )(place, raw, raw, raw, inverse, inverse, *gains, *tables, *ids, d_out, out, log_total)


def sigmoid(values):
    return 1.0 / (1.0 + jnp.exp(-values))


def feed_kernel(masks, tok, steps, refs):
    number = len(masks)
    pieces, refs = refs[:number], refs[number:]
    w_gate, w_up, h_all, middle_all, refs = *refs[:4], refs[4:]
    slopes, silus, refs = refs[:number], refs[number : 2 * number], refs[2 * number :]
    held_h, held_middle, sems = refs
    at = pl.program_id(0)
    part = slopes[0].shape[1]
    block = lambda i: pl.ds(i * tok, tok)
    copies = lambda held, whole, first: [
        pltpu.make_async_copy(held.at[block(i)], whole.at[block(m)], sems.at[first + i])
        for i, m in enumerate(masks)
    ]
    arrive = [
        pltpu.make_async_copy(pieces[i], held_h.at[block(i)], sems.at[i]) for i in range(number)
    ]
    keep_h, keep_middle = copies(held_h, h_all, number), copies(held_middle, middle_all, 2 * number)

    @pl.when(at == 0)
    def _():
        for copy in arrive:
            copy.start()
        for copy in arrive:
            copy.wait()
        for copy in keep_h:
            copy.start()

    gate_act = dot(held_h[...], w_gate[...])
    up_act = dot(held_h[...], w_up[...])
    sig = sigmoid(gate_act)
    silu = gate_act * sig
    middle = (silu * up_act).astype(bf16)
    slope = up_act * (sig + silu * (1.0 - sig))
    for i in range(number):
        slopes[i][...] = slope[i * tok : (i + 1) * tok].astype(bf16)
        silus[i][...] = silu[i * tok : (i + 1) * tok].astype(bf16)
    for step in range(steps):

        @pl.when(at == step)
        def _(step=step):
            held_middle[:, step * part : (step + 1) * part] = middle

    @pl.when(at == steps - 1)
    def _():
        for copy in keep_middle:
            copy.start()
        for copy in keep_h + keep_middle:
            copy.wait()


def feed_back_kernel(masks, tok, steps, refs):
    number = len(masks)
    pieces, refs = refs[:number], refs[number:]
    slopes, silus, refs = refs[:number], refs[number : 2 * number], refs[2 * number :]
    down, w_gu, d_ff_all, d_gate_all, d_up_all = refs[:5]
    partials, (held_d, held_gu, held_w, sems) = refs[5 : 5 + number], refs[5 + number :]
    at = pl.program_id(0)
    part = slopes[0].shape[1]
    units = steps * part
    block = lambda i: pl.ds(i * tok, tok)
    arrive, keep_d, keep_gu = [], [], []
    for i, m in enumerate(masks):
        arrive.append(pltpu.make_async_copy(pieces[i], held_d.at[block(i)], sems.at[i]))
        keep_d.append(
            pltpu.make_async_copy(held_d.at[block(i)], d_ff_all.at[block(m)], sems.at[number + i])
        )
        for j, whole in enumerate((d_gate_all, d_up_all)):
            source = held_gu.at[block(i), pl.ds(j * units, units)]
            sem = sems.at[(2 + j) * number + i]
            keep_gu.append(pltpu.make_async_copy(source, whole.at[block(m)], sem))
    weights = pltpu.make_async_copy(w_gu, held_w, sems.at[4 * number])

    @pl.when(at == 0)
    def _():
        for copy in arrive:
            copy.start()
        weights.start()
        for copy in arrive:
            copy.wait()
        for copy in keep_d:
            copy.start()

    d_middle_all = dot_t(held_d[...], down[...])
    d_gates, d_ups = [], []
    for i in range(number):
        d_middle = d_middle_all[i * tok : (i + 1) * tok]
        d_gates.append((d_middle * slopes[i][...].astype(f32)).astype(bf16))
        d_ups.append((d_middle * silus[i][...].astype(f32)).astype(bf16))
    for step in range(steps):

        @pl.when(at == step)
        def _(step=step):
            for i in range(number):
                rows = slice(i * tok, (i + 1) * tok)
                held_gu[rows, step * part : (step + 1) * part] = d_gates[i]
                held_gu[rows, units + step * part : units + (step + 1) * part] = d_ups[i]

    @pl.when(at == steps - 1)
    def _():
        for copy in keep_gu:
            copy.start()
        weights.wait()
        width = held_d.shape[1]
        cols = math.gcd(width, 1024)
        for n in range(0, width, cols):
            product = dot_t(held_gu[...], held_w[n : n + cols, :]).astype(bf16)
            for i, out in enumerate(partials):
                out[:, n : n + cols] = product[i * tok : (i + 1) * tok]
        for copy in keep_d + keep_gu:
            copy.wait()


def feed_call(kernel, name, pieces, masks, total, ins, in_specs, earlier, widths, blocks, held):
    number = len(pieces)
    tok, width = pieces[0].shape
    steps, part = blocks
    made, given, scratch = held
    somewhere = pl.BlockSpec(memory_space=pl.ANY)
    rows = number * tok
    first_alias = number + len(ins)

    def body(*refs):
        refs = refs[:first_alias] + refs[first_alias + len(earlier) :]
        kernel(masks, tok, steps, refs)

    return pl.pallas_call(
        body,
        grid=(steps,),
        in_specs=[somewhere] * number + in_specs + [somewhere] * len(earlier),
        out_specs=[somewhere] * len(widths)
        + [pl.BlockSpec((tok, part), lambda j: (0, j))] * made
        + [pl.BlockSpec((tok, width), lambda j: (0, 0))] * given,
        out_shape=[jax.ShapeDtypeStruct((total * tok, w), bf16) for w in widths]
        + [jax.ShapeDtypeStruct((tok, steps * part), bf16)] * made
        + [jax.ShapeDtypeStruct((tok, width), bf16)] * given,
        scratch_shapes=[pltpu.VMEM((rows, width), bf16)]
        + [pltpu.VMEM(shape, bf16) for shape in scratch]
        + [pltpu.SemaphoreType.DMA((4 * number + 1,))],
        input_output_aliases={first_alias + i: i for i in range(len(earlier))},
        compiler_params=pltpu.CompilerParams(vmem_limit_bytes=50 * 1024 * 1024),
        cost_estimate=pl.CostEstimate(
            flops=6 * rows * width * steps * part,
            bytes_accessed=6 * width * steps * part + 10 * rows * width,
            transcendentals=rows * steps * part,
        ),
        name=name,
    )(*pieces, *ins, *earlier)


def feed(pieces, masks, total, w_gu, earlier):
    width, units = w_gu.shape[0], w_gu.shape[1] // 2
    part = math.gcd(units, 512)
    steps = units // part
    number = len(pieces)
    rows = number * pieces[0].shape[0]
    specs = [
        pl.BlockSpec((width, part), lambda j: (0, j)),
        pl.BlockSpec((width, part), lambda j: (0, steps + j)),
    ]
    outs = feed_call(
        feed_kernel, "feed", pieces, masks, total, [w_gu, w_gu], specs, earlier,
        (width, units), (steps, part), (2 * number, 0, [(rows, units)]),
    )
    return outs[:2], list(zip(outs[2 : 2 + number], outs[2 + number :], strict=True))


def feed_down(middle_all, masks, tok, down):
    units, width = down.shape
    number = len(masks)

    def kernel(at, middle, weight, *outs):
        for i, out in enumerate(outs):

            @pl.when(pl.program_id(0) == i)
            def _(out=out):
                out[...] = dot(middle[...], weight[...]).astype(bf16)

    return pl.pallas_call(
        kernel,
        grid_spec=pltpu.PrefetchScalarGridSpec(
            num_scalar_prefetch=1,
            grid=(number,),
            in_specs=[
                pl.BlockSpec((tok, units), lambda i, at: (at[i], 0)),
                pl.BlockSpec((units, width), lambda i, at: (0, 0)),
            ],
            out_specs=[pl.BlockSpec((tok, width), lambda i, at: (0, 0))] * number,
        ),
        out_shape=[jax.ShapeDtypeStruct((tok, width), bf16)] * number,
        compiler_params=pltpu.CompilerParams(vmem_limit_bytes=40 * 1024 * 1024),
        cost_estimate=pl.CostEstimate(
            flops=2 * number * tok * units * width,
            bytes_accessed=4 * units * width,
            transcendentals=0,
        ),
        name="feed_down",
    )(jnp.array(masks, jnp.int32), middle_all, down)


def feed_back(pieces, masks, total, acts, w_gu, down, earlier):
    units, width = down.shape
    part = math.gcd(units, 512)
    steps = units // part
    number = len(pieces)
    tok = pieces[0].shape[0]
    rows = number * tok
    specs = [pl.BlockSpec((tok, part), lambda j: (0, j))] * (2 * number) + [
        pl.BlockSpec((part, width), lambda j: (j, 0)),
        pl.BlockSpec(memory_space=pl.ANY),
    ]
    ins = [slope for slope, _ in acts] + [silu for _, silu in acts] + [down, w_gu]
    outs = feed_call(
        feed_back_kernel, "feed_back", pieces, masks, total, ins, specs, earlier,
        (width, units, units), (steps, part), (0, number, [(rows, 2 * units), (width, 2 * units)]),
    )
    return outs[:3], outs[3:]


def owner_grad(h_all, d_act, sizes, rows, which, earlier):
    n_seq, n_hi, n_lo, n_core = sizes
    tokens, width = h_all.shape
    units = d_act.shape[1]
    cols = width // n_seq

    def kernel(h, d, *refs):
        product = t_dot(h[...], d[...]).astype(bf16)
        at = 0
        for hi in range(n_hi):
            for lo in range(n_lo):
                for core in range(n_core):
                    refs[-1][hi, core, 0, lo] = product[at : at + rows]
                    at += rows

    return pl.pallas_call(
        kernel,
        grid=(n_seq,),
        in_specs=[
            pl.BlockSpec((tokens, cols), lambda s: (0, s)),
            pl.BlockSpec((tokens, units), lambda s: (0, 0)),
        ]
        + [pl.BlockSpec(memory_space=pl.ANY)] * len(earlier),
        out_specs=pl.BlockSpec(
            (n_hi, n_core, 1, n_lo, rows, units), lambda s: (0, 0, s, 0, 0, which)
        ),
        out_shape=jax.ShapeDtypeStruct((n_hi, n_core, n_seq, n_lo, rows, 2 * units), bf16),
        input_output_aliases={2: 0} if earlier else {},
        compiler_params=pltpu.CompilerParams(vmem_limit_bytes=40 * 1024 * 1024),
        cost_estimate=pl.CostEstimate(
            flops=2 * tokens * width * units,
            bytes_accessed=2 * (tokens * width + tokens * units + width * units),
            transcendentals=0,
        ),
        name="owner_grad",
    )(h_all, d_act, *earlier)


def pack_columns(weights, count):
    rows, width = weights[0].shape
    part = width // count

    def kernel(*refs):
        for i, ref in enumerate(refs[:-1]):
            refs[-1][0, :, i * part : (i + 1) * part] = ref[...]

    return pl.pallas_call(
        kernel,
        grid=(count,),
        in_specs=[pl.BlockSpec((rows, part), lambda s: (0, s))] * len(weights),
        out_specs=pl.BlockSpec((1, rows, len(weights) * part), lambda s: (s, 0, 0)),
        out_shape=jax.ShapeDtypeStruct((count, rows, len(weights) * part), weights[0].dtype),
        name="pack_columns",
    )(*weights)


def unpack_columns(packed, number):
    count, rows, width = packed.shape
    part = width // number

    def kernel(ref, *outs):
        for i, out in enumerate(outs):
            out[...] = ref[0, :, i * part : (i + 1) * part].astype(f32)

    return pl.pallas_call(
        kernel,
        grid=(count,),
        in_specs=[pl.BlockSpec((1, rows, width), lambda s: (s, 0, 0))],
        out_specs=[pl.BlockSpec((rows, part), lambda s: (0, s))] * number,
        out_shape=[jax.ShapeDtypeStruct((rows, count * part), f32)] * number,
        name="unpack_columns",
    )(packed)


def unit_slices(sizes, unit):
    n_hi, n_lo, n_core = sizes
    return [
        (lo, (hi * n_core + core) * unit, ((hi * n_lo + lo) * n_core + core) * unit)
        for hi in range(n_hi)
        for lo in range(n_lo)
        for core in range(n_core)
    ]


def pack_units(gate, up, n_seq, sizes, unit):
    rows = gate.shape[0]
    n_hi, n_lo, n_core = sizes
    units = n_hi * n_core * unit

    def kernel(gate_ref, up_ref, out):
        for i, ref in enumerate((gate_ref, up_ref)):
            for lo, packed, plain in unit_slices(sizes, unit):
                start = i * units + packed
                out[lo, :, start : start + unit] = ref[:, plain : plain + unit]

    return pl.pallas_call(
        kernel,
        grid=(n_seq,),
        in_specs=[pl.BlockSpec((rows, units * n_lo), lambda s: (0, s))] * 2,
        out_specs=pl.BlockSpec((n_lo, rows, 2 * units), lambda s: (s, 0, 0)),
        out_shape=jax.ShapeDtypeStruct((n_seq * n_lo, rows, 2 * units), gate.dtype),
        name="pack_units",
    )(gate, up)


def unpack_units(packed, n_seq, sizes, unit):
    _, rows, width = packed.shape
    n_lo = sizes[1]
    units = width // 2

    def kernel(ref, *outs):
        for i, out in enumerate(outs):
            for lo, at, plain in unit_slices(sizes, unit):
                start = i * units + at
                out[:, plain : plain + unit] = ref[lo, :, start : start + unit].astype(f32)

    return pl.pallas_call(
        kernel,
        grid=(n_seq,),
        in_specs=[pl.BlockSpec((n_lo, rows, width), lambda s: (s, 0, 0))],
        out_specs=[pl.BlockSpec((rows, units * n_lo), lambda s: (0, s))] * 2,
        out_shape=[jax.ShapeDtypeStruct((rows, n_seq * n_lo * units), f32)] * 2,
        name="unpack_units",
    )(packed)


def finish_kernel(q_in, k_in, q_raw, k_raw, q_inv, k_inv, q_mean, k_mean, d_v, out):
    width = q_in.shape[1]
    for i, (grad, raw, inverse, mean) in enumerate(
        ((q_in, q_raw, q_inv, q_mean), (k_in, k_raw, k_inv, k_mean))
    ):
        normed = raw[...] * inverse[0]
        low = ((grad[...] - normed * mean[0]) * inverse[0]).astype(bf16)
        out[:, i * width : (i + 1) * width] = low
    out[:, 2 * width :] = d_v[...]


def row_specs(block, part):
    cols = lambda i: pl.BlockSpec((block, part), lambda b: (b, i))
    rows = lambda i: pl.BlockSpec((1, block, 1), lambda b: (i, b, 0))
    vector = pl.BlockSpec((1, part), lambda b: (0, 0))
    return cols, rows, vector


def finish(e_query, e_key, raw, inverse, means, d_value, part, block):
    length = raw.shape[0]
    cols, rows, _ = row_specs(block, part)
    return pl.pallas_call(
        finish_kernel,
        grid=(length // block,),
        in_specs=[cols(0), cols(0), cols(0), cols(1)] + [rows(0), rows(1)] * 2 + [cols(0)],
        out_specs=pl.BlockSpec((block, 3 * part), lambda b: (b, 0)),
        out_shape=jax.ShapeDtypeStruct((length, 3 * part), bf16),
        compiler_params=pltpu.CompilerParams(vmem_limit_bytes=56 * 1024 * 1024),
        name="finish",
    )(e_query, e_key, raw, raw, inverse, inverse, means, means, d_value)


def dot(left, right):
    return jnp.dot(left, right, preferred_element_type=f32)


def dot_t(left, right):
    return lax.dot_general(left, right, (((1,), (1,)), ((), ())), preferred_element_type=f32)


def t_dot(left, right):
    return lax.dot_general(left, right, (((0,), (0,)), ((), ())), preferred_element_type=f32)


def held(block):
    return lax.optimization_barrier(block)


def rope_tables(positions, head_dim):
    half_dim = head_dim // 2
    frequency = rope_base ** (-(jnp.arange(half_dim, dtype=f32) * 2.0 / head_dim))
    angles = positions.astype(f32)[:, None] * frequency[None, :]
    cosine, sine = jnp.cos(angles), jnp.sin(angles)
    return jnp.concatenate([cosine, cosine], 1), jnp.concatenate([-sine, sine], 1)


def rms(values):
    inverse = lax.rsqrt(jnp.mean(values * values, axis=-1, keepdims=True) + norm_eps)
    return values * inverse, inverse


def rms_back(grad, normed, inverse, gain):
    scaled = grad * gain
    return (scaled - normed * jnp.mean(scaled * normed, axis=-1, keepdims=True)) * inverse


def per_device(
    tokens,
    segment_ids,
    w_query,
    w_key,
    w_value,
    w_out,
    w_gate,
    w_up,
    w_down,
    query_gain,
    key_gain,
    attn_gain,
    ff_gain,
    cotangent,
):
    inputs = tokens[0]
    tok, width = inputs.shape
    n_seq, n_hi, n_lo, n_core = (lax.axis_size(a) for a in ("seq", "zhi", "zlo", "core"))
    n_dev = n_seq * n_hi * n_lo * n_core
    seq = lax.axis_index("seq")
    heads = HEADS // n_seq
    head_dim = width // HEADS
    part = width // n_seq
    length = n_seq * tok
    d_rows = w_query.shape[0]
    ff_rows = w_down.shape[0]
    units = ff_rows * n_hi * n_core

    sizes = (n_hi, n_lo, n_core)
    seq_dims = dims_of("seq")
    lo_dims, hi_dims, core_dims = dims_of("zlo"), dims_of("zhi"), dims_of("core")
    cube_dims = seq_dims + lo_dims
    z_dims = lo_dims + hi_dims
    all_dims = core_dims + lo_dims + hi_dims + seq_dims
    z_axes = ("zhi", "zlo", "core")
    rows_of = lambda block, m: block[m * tok : (m + 1) * tok]

    pair_axes = ("zhi", "core")
    core_swap = lambda piece: swap(piece, core_dims[0])
    lo_order = [
        ((hi * n_core + core) * n_seq + s) * n_lo + lo
        for s in range(n_seq)
        for hi in range(n_hi)
        for lo in range(n_lo)
        for core in range(n_core)
    ]
    hi_order = [lo_order.index(i) for i in range(len(lo_order))]

    tables = rope_tables(jnp.arange(length, dtype=jnp.int32), head_dim)

    qkv_mine = pack_columns((w_query, w_key, w_value), n_seq)
    gains = jnp.stack([query_gain, key_gain, attn_gain, ff_gain])[None]
    gains = gather_row(after(gains, qkv_mine), core_dims + z_dims)
    gains = jnp.transpose(gains, (1, 0, 2)).reshape(1, 4 * part)
    qkv_mine = lax.all_to_all(qkv_mine, "seq", 0, 0, tiled=True).reshape(n_seq * d_rows, 3 * part)
    gu_mine = pack_units(w_gate, w_up, n_seq, sizes, ff_rows)
    qkv_mine, gains, gu_mine = tie(qkv_mine, gains, gu_mine)

    out_mine = jnp.concatenate([w_out[:, i * part : (i + 1) * part] for i in range(n_seq)], axis=0)
    w_z = Spread(jnp.concatenate([qkv_mine, out_mine], axis=1), z_dims).step()
    to_width = lambda row: jnp.pad(row, ((0, 0), (0, width - row.shape[1])))
    ids = to_width(segment_ids.astype(bf16))
    more = jnp.concatenate([ids, to_width(gains), jnp.zeros((14, width), bf16)], axis=0)
    x_spread = Spread(jnp.concatenate([inputs, more], axis=0), seq_dims).step()
    x_pieces = x_spread.whole()
    tables, *x_pieces = tie(w_z, tables, *x_pieces)
    w_sib = [core_swap(piece) for piece in (w_z.pieces[0], *w_z.fresh())]
    early = len(w_sib)
    w_z.step()
    small = after(x_pieces, w_z.fresh())
    row_ids = jnp.concatenate([piece[tok, :tok] for piece in small]).astype(jnp.int32)
    row_ids = row_ids.reshape(length, 1)
    col_ids = jnp.stack(
        [lax.dynamic_slice(row_ids, ((seq ^ m) * tok, 0), (tok, 1)) for m in range(n_seq)]
    ).reshape(n_seq, 1, tok)
    all_gains = jnp.concatenate([piece[tok + 1 : tok + 2, : 4 * part] for piece in small], axis=0)
    all_gains = jnp.concatenate(
        [lax.dynamic_slice(all_gains, (seq ^ m, 0), (1, 4 * part)) for m in range(n_seq)], axis=0
    ).reshape(n_seq, 4, part)
    all_gains = jnp.transpose(all_gains, (1, 0, 2)).reshape(4, width).astype(f32)
    my_gains = gains.reshape(4, 1, part).astype(f32)
    qk_gains = (my_gains[0], my_gains[1])
    (w_sib,) = tie(w_z, w_sib)
    gain_attn, gain_ff = all_gains[2], all_gains[3]
    w_z = w_z.whole()
    w_sib = w_sib + [core_swap(piece) for piece in w_z[early:]]

    gu_mine = lax.all_to_all(after(gu_mine, w_z), ("seq", "zlo"), 0, 0, tiled=True)

    raw, squares, x_all, w_qkv, out_weight = project(
        x_pieces,
        [piece.reshape(n_seq, d_rows, 4 * part) for piece in w_z + w_sib],
        block_starts(
            n_seq,
            d_rows,
            z_dims + core_dims,
            z_axes,
            lambda s, hi, lo, core: ((s * n_hi + hi) * n_lo + lo) * n_core + core,
        ),
        block_starts(
            1,
            d_rows,
            z_dims + core_dims,
            z_axes,
            lambda block, hi, lo, core: (hi * n_lo + lo) * n_core + core,
        ),
        tok,
        part,
    )
    squares, gu_mine = tie(squares, gu_mine)
    w_gu = lax.all_gather(gu_mine, pair_axes, axis=0, tiled=True)
    squares = squares.reshape(2, n_seq, tok)
    squares = sum_all(jnp.transpose(squares, (1, 0, 2)), seq_dims)
    inverse = lax.rsqrt(jnp.transpose(squares, (1, 0, 2)).reshape(2, length, 1) / width + norm_eps)

    context = (seq.astype(jnp.int32).reshape(1), raw, inverse, qk_gains, tables, (row_ids, col_ids))
    attended, attn_low, log_total = attend(context, heads, tok)
    branch = Collect(
        [held(dot(rows_of(attn_low, m), out_weight).astype(bf16)) for m in range(n_seq)], seq_dims
    ).whole()
    branch_norm, branch_inv = rms(branch)
    hidden = inputs.astype(f32) + branch_norm * gain_attn
    hidden_low = hidden.astype(bf16)

    w_gu = regroup(w_gu.reshape(-1, d_rows, 2 * units), lo_order)
    total = 1 << len(cube_dims)
    by_bits = lambda size: [
        m for m in range(total) if bin(m).count("1") == size or (size == 1 and m == 0)
    ]
    fours = lambda masks: [masks[i : i + 4] for i in range(0, len(masks), 4)]
    groups = [masks for size in range(1, len(cube_dims) + 1) for masks in fours(by_bits(size))]
    light = total == 8
    h_spread = Spread(hidden_low, cube_dims, spare_last=light).step()
    if light:
        h_spread.step()
        near = [h_spread.pieces[m] for m in (1, 2, 3)]
        near, w_gu = tie(near, w_gu)
        h_spread.pieces.update(zip((1, 2, 3), near, strict=True))
    acts, partials, kept = {}, {}, ()
    order = [[0, 1], [2, 3], [4, 5, 6], [7]] if light else groups
    for i, masks in enumerate(order):
        while any(m not in h_spread.pieces for m in masks):
            h_spread.step()
        pieces = [h_spread.pieces[m] for m in masks]
        kept, act = feed(pieces, masks, total, w_gu, kept)
        if i == 0:
            last = h_spread.pieces[total // 2] = after(h_spread.pieces[total // 2], act)
            down = lax.all_gather(after(w_down, last), pair_axes, axis=0, tiled=True)
        if light and i == 1:
            (act,) = tie(h_spread.step(), act)
        acts.update(zip(masks, act, strict=True))
    h_all, middle_all = kept
    for masks in fours(sorted(range(total), key=lambda m: -bin(m).count("1"))):
        sums = feed_down(middle_all, masks, tok, down)
        partials.update(zip(masks, sums, strict=True))
    partials = [partials[m] for m in range(total)]
    ff_raw = Collect(partials, cube_dims).whole()
    ff_norm, ff_inv = rms(ff_raw)
    mixed = (hidden + ff_norm * gain_ff).astype(bf16)

    grad_output = cotangent[0].astype(f32)
    grad_ff_gain = jnp.sum(grad_output * ff_norm, axis=0)
    d_ff = rms_back(grad_output, ff_norm, ff_inv, gain_ff).astype(bf16)
    d_spread = Spread(d_ff, cube_dims).step()
    partials, kept = {}, ()
    for masks in groups:
        while any(m not in d_spread.pieces for m in masks):
            d_spread.step()
        pieces = [d_spread.pieces[m] for m in masks]
        act = [acts[m] for m in masks]
        kept, sums = feed_back(pieces, masks, total, act, w_gu, down, kept)
        partials.update(zip(masks, sums, strict=True))
    d_ff_all, d_gate_all, d_up_all = kept
    partials = [partials[m] for m in range(total)]
    d_hidden = Collect(partials, cube_dims).step()

    owned = lambda grad: lax.psum_scatter(grad, pair_axes, scatter_dimension=0, tiled=True)
    grad_down = t_dot(middle_all, after(d_ff_all, partials)).astype(bf16)
    (grad_down,) = tie(d_hidden, grad_down)
    grad_down = owned(grad_down)
    order = (n_seq, n_hi, n_lo, n_core)
    d_hidden.step()
    grad_gu = owner_grad(h_all, d_gate_all, order, d_rows, 0, [])
    (grad_gu,) = tie(d_hidden, grad_gu)
    d_hidden.step()
    grad_gu = owner_grad(h_all, after(d_up_all, grad_gu), order, d_rows, 1, [grad_gu])
    (grad_gu,) = tie(d_hidden, grad_gu)
    grad_gu = owned(grad_gu.reshape(-1, d_rows, 2 * units))
    d_hidden = d_hidden.whole()

    d_hidden = grad_output + d_hidden
    grad_attn_gain = jnp.sum(d_hidden * branch_norm, axis=0)
    d_branch = rms_back(d_hidden, branch_norm, branch_inv, gain_attn).astype(bf16)
    d_branch_pieces = Spread(d_branch, seq_dims).whole()
    d_branch_pieces, grad_down = tie(d_branch_pieces, grad_down)
    d_attended = jnp.concatenate(
        [dot_t(piece, out_weight).astype(bf16) for piece in d_branch_pieces], axis=0
    )
    e_query, e_key, d_value, q_sum, k_sum, grad_query_gain, grad_key_gain = attend_back(
        context, d_attended, attended, log_total, heads, tok
    )
    means = jnp.stack([q_sum[0], k_sum[0]]).reshape(2, n_seq, tok)
    means = sum_all(jnp.transpose(means, (1, 0, 2)), seq_dims)
    means = jnp.transpose(means, (1, 0, 2)).reshape(2, length, 1) / width

    n_z = n_hi * n_lo
    z_blocks = lambda grad: take_blocks(
        jnp.transpose(
            grad.reshape(n_seq, n_hi, n_lo, n_core, d_rows, grad.shape[1]), (1, 2, 3, 0, 4, 5)
        ),
        z_dims + core_dims,
        z_axes,
    )
    def to_core(grad):
        blocks = z_blocks(grad)
        theirs = [core_swap(piece) for piece in blocks[n_z:]]
        return [
            add_low(a, b).reshape(-1, a.shape[-1]) for a, b in zip(blocks[:n_z], theirs, strict=True)
        ]

    d_qkv = finish(e_query, e_key, raw, inverse, means, d_value, part, tok)
    grad_qkv = t_dot(x_all, d_qkv).astype(bf16)
    back = lambda rows, m: held(dot_t(rows_of(rows, m), w_qkv).astype(bf16))
    far = back(after(d_qkv, grad_qkv), n_seq - 1)
    grad_qkv, far, low_rows = tie(to_core(grad_qkv), far, d_qkv)
    grad_qkv = Collect(grad_qkv, z_dims).step()
    low_rows, far = tie(grad_qkv, low_rows, far)
    low_rows, far = tie(grad_qkv.ready(), low_rows, far)
    grad_qkv.step()
    input_grad = Collect([back(low_rows, m) for m in range(n_seq - 1)] + [far], seq_dims)
    input_grad.step()
    full_row = lambda cols: lax.dynamic_update_slice(jnp.zeros((width,), f32), cols, (seq * part,))
    rows = jnp.stack(
        [full_row(grad_query_gain[0]), full_row(grad_key_gain[0]), grad_attn_gain, grad_ff_gain]
    )
    rows = jnp.transpose(rows.reshape(4, n_dev, d_rows), (1, 0, 2))
    grad_gu = after(grad_gu, low_rows).reshape(n_seq * n_lo, d_rows, 2 * units)
    grad_gu = lax.all_to_all(grad_gu, ("seq", "zlo"), 0, 0, tiled=True)
    d_branch_all = jnp.concatenate(after(d_branch_pieces, low_rows), axis=0)
    grad_out = t_dot(attn_low, d_branch_all).astype(bf16)
    grad_out = jnp.concatenate([grad_out[:, i * part : (i + 1) * part] for i in range(n_seq)], axis=0)
    grad_out, grad_gu = tie(grad_qkv, input_grad, to_core(grad_out), grad_gu)
    input_grad.step()
    grad_qkv = grad_qkv.whole().astype(bf16).reshape(n_seq, d_rows, 3 * part)
    grad_qkv = lax.all_to_all(grad_qkv, "seq", 0, 0, tiled=True)
    grad_out = Collect(grad_out, z_dims).step()
    rows = lax.all_to_all(after(rows, grad_qkv), ("seq",) + z_axes, 0, 0, tiled=True)
    input_grad = d_hidden + input_grad.whole()
    grad_down = after(grad_down, grad_qkv).astype(f32)
    grad_out = grad_out.whole().reshape(n_seq, d_rows, part)
    grad_gate, grad_up = unpack_units(grad_gu, n_seq, sizes, ff_rows)
    grad_query, grad_key, grad_value = unpack_columns(grad_qkv, 3)
    rows = jnp.sum(rows, axis=0)
    grad_out = jnp.concatenate([grad_out[i] for i in range(n_seq)], axis=1)

    return (
        mixed[None],
        input_grad[None],
        grad_query,
        grad_key,
        grad_value,
        grad_out,
        grad_gate,
        grad_up,
        grad_down,
        rows[0],
        rows[1],
        rows[2],
        rows[3],
    )


def solution(mesh):
    n_seq, n_row = mesh.shape["seq"], mesh.shape["row"]
    n_core = 2
    n_lo = 2
    n_hi = n_row // (n_core * n_lo)
    cut = Mesh(
        mesh.devices.reshape(n_seq, n_hi, n_lo, n_core), ("seq", "zhi", "zlo", "core")
    )
    row = ("zhi", "zlo", "core")
    every = ("seq",) + row
    acts = P(row, "seq", None)
    matrix = P(every, None)
    vector = P(every)
    return jax.shard_map(
        per_device,
        mesh=cut,
        in_specs=(acts, P(row, "seq")) + (matrix,) * 7 + (vector,) * 4 + (acts,),
        out_specs=(acts, acts) + (matrix,) * 7 + (vector,) * 4,
        check_vma=False,
    )
```
